32 devices in a mesh: grp: 4 (over z), voc: 8 (over y, x, core).
Axes of the slice: x: 2, y: 2, z: 4, core: 2. Of those that a mesh axis runs over, the one named last changes fastest.
Arguments:
- hidden_states: bfloat16 [4096, 8192], P('grp', 'voc'), may hold values from -6 to 6
- target_logits: float32 [4096, 16384], P('grp', 'voc'), may hold values from -12 to 240
- labels: int32 [4096, 8], P('grp'), may hold values from 0 to 2047
- down_weight: bfloat16 [8192, 256], P('voc'), may hold values from -0.0625 to 0.0625
- up_weight: bfloat16 [256, 8192], P(None, 'grp'), may hold values from -0.75 to 0.75
- head_weight: bfloat16 [8192, 16384], P('grp', 'voc'), may hold values from -0.0625 to 0.0625
Outputs:
- frame_loss: float32 [8, 4, 1024], P('voc', 'grp')
- grad_a: float32 [8192, 256], P('voc')
- grad_b: float32 [256, 8192], P(None, 'grp')
The draws below stay inside these ranges and needn't reach their ends.
All inputs are finite; a program needn't handle non-finite values.
Results may differ from the reference program's by a relative error of at most 0.0046.
Values may be sent and summed in bfloat16 or wider, within the bound.
No kernel may reach another device: no remote copies, remote signals or barrier semaphores. Data moves between devices by JAX's collectives and lax.ppermute only.
A program may use at most 64 MiB of HBM per device.

```python
import math
import jax
import jax.numpy as jnp
import numpy as np
from jax import lax

D = 8192
CODEBOOKS = 8
CB = 2048
R = 256
HEAD = 2
F = 1024
V = 16384
Q = 1
FB = 1024
FRAMES = 4096
N_GRP = 4


def draw_target_logits(key, part):
    subkeys = jax.random.split(key, 1)
    full_shape = (FRAMES, CODEBOOKS, CB)
    values = jnp.clip(jax.random.normal(subkeys[0], full_shape, jnp.float32) * 3.0, -12.0, 12.0)
    return values.reshape(FRAMES, CODEBOOKS * CB)


def touch_ends(values, stream_key, smallest, top_value):
    index_at = [jax.random.randint(jax.random.fold_in(stream_key, axis), (), 0, length) for axis, length in enumerate(values.shape)]
    longest = values.shape.index(max(values.shape))
    next_to = index_at[:longest] + [(index_at[longest] + 1) % values.shape[longest]] + index_at[longest + 1:]
    return values.at[tuple(index_at)].set(smallest).at[tuple(next_to)].set(top_value)


def shard_levels(key, extent, shards, least, top_value):
    loudness = 1.0
    for dim, parts in shards:
        draws = jax.random.uniform(jax.random.fold_in(jax.random.fold_in(key, 6), dim), (parts,), jnp.float32, least / len(shards), top_value / len(shards))
        loudness = loudness * jnp.repeat(jnp.exp(draws), extent[dim] // parts).reshape((-1,) + (1,) * (len(extent) - 1 - dim))
    return loudness


def rank_table(count, slope):
    portions = [(1 << 20) // math.isqrt(standing ** slope) + 1 for standing in range(1, count + 1)]
    deviation = 1 + sum(portions) // (1 << 30)
    return np.cumsum(np.array([max(1, weight // deviation) for weight in portions]))


def ranked_ids(rng, dims, number_of, slope):
    table = rank_table(number_of, slope)
    lot = jax.random.randint(jax.random.fold_in(rng, 1), dims, 0, int(table[number_of - 1]))
    grade = jnp.searchsorted(jnp.asarray(table, jnp.int32), lot, side="right")
    return jax.random.permutation(jax.random.fold_in(rng, 2), number_of)[grade].astype(jnp.int32)


def scatter_about(stream_key, dims, scale, limit, shards=(), kind=jnp.bfloat16):
    values = jax.random.normal(stream_key, dims, jnp.float32) * scale
    if len(shards) > 0:
        values = shard_levels(stream_key, dims, shards, -0.22, 0.18) * values
    return jnp.clip(values, min=-limit, max=limit).astype(kind)


def setup_inputs(seed: int = 0) -> dict:
    streams_of = jax.random.split(jax.random.key(seed), 7)
    return {
        "hidden_states": scatter_about(streams_of[0], (FRAMES, D), 1.0, 6.0, ((0, 4), (1, 8))),
        "target_logits": draw_target_logits(jax.random.fold_in(streams_of[6], 71), 0),
        "labels": touch_ends(ranked_ids(streams_of[2], (FRAMES, CODEBOOKS), CB, 2), jax.random.fold_in(streams_of[2], 3), 0, CB - 1).astype(jnp.int32),
        "down_weight": scatter_about(streams_of[3], (D, R), D ** -0.5, 0.0625, ((0, 8),)),
        "up_weight": scatter_about(streams_of[4], (R, D), (R // 4) ** -0.5, 0.75, ((1, 4),)),
        "head_weight": scatter_about(streams_of[5], (D, V), D ** -0.5, 0.0625, ((0, 4), (1, 8))),
    }


LAM = 0.1


def silu_slope(values):
    sigma = jax.nn.sigmoid(values)
    return sigma * (1.0 + values * (1.0 - sigma))


def reference(hidden_states, target_logits, labels, down_weight, up_weight, head_weight):
    pre_act = jnp.dot(hidden_states, down_weight, preferred_element_type=jnp.float32)
    activation = jax.nn.silu(pre_act).astype(jnp.bfloat16)
    vocab_proj = jnp.dot(up_weight, head_weight, preferred_element_type=jnp.float32).astype(jnp.bfloat16)
    shifted = jnp.concatenate([target_logits[HEAD:], jnp.zeros((HEAD, V), jnp.float32)], 0)
    live_mask = (jnp.arange(FRAMES) < FRAMES - HEAD).astype(jnp.float32)
    scanned = (target_logits.reshape(N_GRP, F, V), shifted.reshape(N_GRP, F, V),
               activation.reshape(N_GRP, F, R), labels.reshape(N_GRP, F, CODEBOOKS),
               live_mask.reshape(N_GRP, F))

    def group_step(accumulated, pieces):
        target_rows, shifted_rows, act_rows, label_rows, live_rows = pieces
        draft_logits = (target_rows.astype(jnp.float32)
                        + jnp.dot(act_rows, vocab_proj, preferred_element_type=jnp.float32))
        log_target = jax.nn.log_softmax(shifted_rows.astype(jnp.float32).reshape(F, CODEBOOKS, CB), -1)
        log_draft = jax.nn.log_softmax(draft_logits.reshape(F, CODEBOOKS, CB), -1)
        target_prob = jnp.exp(log_target)
        draft_prob = jnp.exp(log_draft)
        onehot = (jnp.arange(CB)[None, None, :] == label_rows[:, :, None]).astype(jnp.float32)
        divergence = jnp.sum(target_prob * (log_target - log_draft), -1)
        picked = jnp.sum(onehot * log_draft, -1)
        frame_rows = live_rows[:, None] * divergence - LAM * picked
        logit_grad = (live_rows[:, None, None] * (draft_prob - target_prob)
                      + LAM * (draft_prob - onehot)).astype(jnp.bfloat16).reshape(F, V)
        accumulated = accumulated + lax.dot_general(act_rows, logit_grad, (((0,), (0,)), ((), ())),
                                                    preferred_element_type=jnp.float32)
        act_grad = jnp.dot(logit_grad, vocab_proj.T, preferred_element_type=jnp.float32)
        return accumulated, (frame_rows, act_grad)

    proj_grad, (frame_rows, act_grad) = lax.scan(group_step, jnp.zeros((R, V), jnp.float32), scanned)
    act_grad = act_grad.reshape(FRAMES, R)
    pre_grad = (act_grad * silu_slope(pre_act)).astype(jnp.bfloat16)
    grad_a = jnp.dot(hidden_states.T, pre_grad, preferred_element_type=jnp.float32)
    grad_b = jnp.dot(proj_grad.astype(jnp.bfloat16), head_weight.T, preferred_element_type=jnp.float32)
    frame_loss = frame_rows.reshape(N_GRP, Q, FB, CODEBOOKS).transpose(3, 1, 0, 2).reshape(CODEBOOKS * Q, N_GRP, FB)
    return frame_loss, grad_a, grad_b
```

```python
import jax
import jax.numpy as jnp
from jax import lax
from jax.sharding import PartitionSpec as P

HEAD = 2
LAM = 0.1
CHUNKS = 4


def swap(value, axis, bit):
    mask = 1 << bit
    pairs = [(i, i ^ mask) for i in range(lax.axis_size(axis))]
    return lax.ppermute(value, axis, pairs)


def own_bit(axis, bit):
    return (lax.axis_index(axis) >> bit) & 1


def half(value, which):
    rows = value.shape[0] // 2
    return lax.dynamic_slice_in_dim(value, which * rows, rows, 0)


def reduce_bits(part, axis, bits, wire):
    for bit in bits[:-1]:
        mine = own_bit(axis, bit)
        arrived = swap(half(part, 1 - mine).astype(wire), axis, bit)
        part = half(part, mine) + arrived.astype(jnp.float32)
    sent = part.astype(wire)
    return sent.astype(jnp.float32) + swap(sent, axis, bits[-1]).astype(jnp.float32)


def gather_bits(piece, axis, bits):
    for bit in reversed(bits[:-1]):
        mine = own_bit(axis, bit)
        other = swap(piece, axis, bit)
        low = jnp.where(mine == 0, piece, other)
        high = jnp.where(mine == 0, other, piece)
        piece = jnp.concatenate((low, high), 0)
    return piece


def owned_rows(value, axis, bits):
    for bit in bits[:-1]:
        value = half(value, own_bit(axis, bit))
    return value


def bit_orders(axis):
    count = lax.axis_size(axis).bit_length() - 1
    first = list(range(count))
    return [first, first[:1] + first[:0:-1]]


def silu_slope(values):
    sigma = jax.nn.sigmoid(values)
    return sigma * (1.0 + values * (1.0 - sigma))


def inner_rows(left, right):
    return lax.dot_general(
        left, right, (((0,), (0,)), ((), ())), preferred_element_type=jnp.float32
    )


def inner_cols(left, right):
    return lax.dot_general(
        left, right, (((1,), (1,)), ((), ())), preferred_element_type=jnp.float32
    )


def over_books(values, combine, per_book):
    bit = 0
    while (1 << bit) < per_book:
        values = combine(values, jax.tree.map(lambda v: swap(v, "voc", bit), values))
        bit += 1
    return values


def on_device(hidden_states, target_logits, labels, down_weight, up_weight, head_weight):
    row_count, slice_cols = target_logits.shape
    book_count = labels.shape[1]
    group_count = lax.axis_size("grp")
    per_book = lax.axis_size("voc") // book_count
    block_rows = row_count // per_book
    position = lax.axis_index("voc")
    book_index = position // per_book
    book_part = position % per_book
    width = slice_cols // CHUNKS
    z_bits = list(range(group_count.bit_length() - 1))
    orders = bit_orders("voc")

    devices = range(group_count)
    incoming = lax.ppermute(
        target_logits[:HEAD], "grp", [(i + 1, i) for i in devices if i + 1 in devices]
    )

    vocab_parts = [
        jnp.dot(
            up_weight,
            head_weight[:, c * width : (c + 1) * width],
            preferred_element_type=jnp.float32,
        )
        for c in range(CHUNKS)
    ]
    pre_part = jnp.dot(hidden_states, down_weight, preferred_element_type=jnp.float32)
    halves = (pre_part[: row_count // 2], pre_part[row_count // 2 :])
    pre_act = [reduce_bits(p, "voc", o, jnp.float32) for p, o in zip(halves, orders)]
    acts = jnp.concatenate(
        [
            gather_bits(jax.nn.silu(p).astype(jnp.bfloat16), "voc", o)
            for p, o in zip(pre_act, orders)
        ],
        0,
    )
    vocab_proj = [
        gather_bits(
            reduce_bits(p, "grp", z_bits, jnp.float16).astype(jnp.bfloat16), "grp", z_bits
        )
        for p in vocab_parts
    ]

    draft = jnp.concatenate(
        [
            target_logits[:, c * width : (c + 1) * width]
            + jnp.dot(acts, vocab_proj[c], preferred_element_type=jnp.float32)
            for c in range(CHUNKS)
        ],
        1,
    )
    shifted = jnp.concatenate((target_logits[HEAD:], incoming), 0)
    frame_index = lax.axis_index("grp") * row_count + jnp.arange(row_count)
    live = (frame_index < row_count * group_count - HEAD).astype(jnp.float32)

    def log_sum(values):
        def merge(a, b):
            top = jnp.maximum(a[0], b[0])
            return top, a[1] * jnp.exp(a[0] - top) + b[1] * jnp.exp(b[0] - top)

        top = jnp.max(values, -1, keepdims=True)
        total = jnp.sum(jnp.exp(values - top), -1, keepdims=True)
        top, total = over_books((top, total), merge, per_book)
        return top + jnp.log(total)

    log_target = shifted - log_sum(shifted)
    log_draft = draft - log_sum(draft)
    label_ids = lax.dynamic_slice_in_dim(labels, book_index, 1, 1)
    columns = book_part * slice_cols + jnp.arange(slice_cols)
    onehot = (columns[None, :] == label_ids).astype(jnp.float32)
    target_prob = jnp.exp(log_target)
    draft_prob = jnp.exp(log_draft)
    divergence = jnp.sum(target_prob * (log_target - log_draft), -1)
    picked = jnp.sum(onehot * log_draft, -1)
    loss = over_books(live * divergence - LAM * picked, jnp.add, per_book)
    frame_loss = lax.dynamic_slice_in_dim(loss, book_part * block_rows, block_rows)
    frame_loss = frame_loss.reshape(1, 1, block_rows)
    logit_grad = (
        live[:, None] * (draft_prob - target_prob) + LAM * (draft_prob - onehot)
    ).astype(jnp.bfloat16)

    proj_parts = [
        inner_rows(acts, logit_grad[:, c * width : (c + 1) * width]) for c in range(CHUNKS)
    ]
    act_part = inner_cols(logit_grad, jnp.concatenate(vocab_proj, 1))
    halves = (act_part[: row_count // 2], act_part[row_count // 2 :])
    pre_grad = jnp.concatenate(
        [
            gather_bits(
                (reduce_bits(p, "voc", o, jnp.float32) * silu_slope(a)).astype(jnp.bfloat16),
                "voc",
                o,
            )
            for p, o, a in zip(halves, orders, pre_act)
        ],
        0,
    )
    proj_grad = [
        gather_bits(
            reduce_bits(p, "grp", z_bits, jnp.float16).astype(jnp.bfloat16), "grp", z_bits
        )
        for p in proj_parts
    ]
    up_part = sum(
        inner_cols(proj_grad[c], head_weight[:, c * width : (c + 1) * width])
        for c in range(CHUNKS)
    )
    down_part = inner_rows(hidden_states, pre_grad)

    def finish(part, axis, bits):
        total = reduce_bits(part, axis, bits, jnp.float16)
        return gather_bits(total.astype(jnp.float16), axis, bits).astype(jnp.float32)

    rank = up_part.shape[0] // 2
    grad_b = jnp.concatenate(
        [finish(p, "voc", o) for p, o in zip((up_part[:rank], up_part[rank:]), orders)], 0
    )
    width_rows = down_part.shape[0] // 2
    grad_a = jnp.concatenate(
        [finish(p, "grp", z_bits) for p in (down_part[:width_rows], down_part[width_rows:])], 0
    )
    return frame_loss, grad_a, grad_b


def solution(mesh):
    in_specs = (
        P("grp", "voc"),
        P("grp", "voc"),
        P("grp", None),
        P("voc", None),
        P(None, "grp"),
        P("grp", "voc"),
    )
    out_specs = (P("voc", "grp", None), P("voc", None), P(None, "grp"))
    return jax.shard_map(
        on_device, mesh=mesh, in_specs=in_specs, out_specs=out_specs, check_vma=False
    )
```

```python
import jax
import jax.numpy as jnp
from jax import lax
from jax.experimental import pallas as pl
from jax.experimental.pallas import tpu as pltpu
from jax.sharding import PartitionSpec as P

HEAD = 2
LAM = 0.1
CHUNKS = 4
BLOCK = 256
VOCAB_SCALE = 128.0
F32 = jnp.float32
BF16 = jnp.bfloat16
F16 = jnp.float16


def swap(value, axis, bit):
    mask = 1 << bit
    pairs = [(i, i ^ mask) for i in range(lax.axis_size(axis))]
    return lax.ppermute(value, axis, pairs)


def own_bit(axis, bit):
    return (lax.axis_index(axis) >> bit) & 1


def half(value, which):
    rows = value.shape[0] // 2
    return lax.dynamic_slice_in_dim(value, which * rows, rows, 0)


def reduce_bits(part, axis, bits, wires):
    for bit, wire in zip(bits[:-1], wires):
        mine = own_bit(axis, bit)
        arrived = swap(half(part, 1 - mine).astype(wire), axis, bit)
        part = half(part, mine) + arrived.astype(F32)
    sent = part.astype(wires[-1])
    return sent.astype(F32) + swap(sent, axis, bits[-1]).astype(F32)


def gather_bits(piece, axis, bits):
    for bit in reversed(bits[:-1]):
        mine = own_bit(axis, bit)
        other = swap(piece, axis, bit)
        low = jnp.where(mine == 0, piece, other)
        high = jnp.where(mine == 0, other, piece)
        piece = jnp.concatenate((low, high), 0)
    return piece


def silu_slope(values):
    sigma = jax.nn.sigmoid(values)
    return sigma * (1.0 + values * (1.0 - sigma))


def inner_rows(left, right):
    return lax.dot_general(left, right, (((0,), (0,)), ((), ())), preferred_element_type=F32)


def inner_cols(left, right):
    return lax.dot_general(left, right, (((1,), (1,)), ((), ())), preferred_element_type=F32)


def over_books(values, combine, per_book):
    bit = 0
    while (1 << bit) < per_book:
        values = combine(values, jax.tree.map(lambda v: swap(v, "voc", bit), values))
        bit += 1
    return values


def merge_sums(a, b):
    top = jnp.maximum(a[0], b[0])
    return top, a[1] * jnp.exp(a[0] - top) + b[1] * jnp.exp(b[0] - top)


def params(megabytes):
    return pltpu.CompilerParams(
        dimension_semantics=("arbitrary",), vmem_limit_bytes=megabytes << 20
    )


def cost(flops, read, exps):
    return pl.CostEstimate(flops=flops, bytes_accessed=read, transcendentals=exps)


def row_spec(block, cols, column=0):
    return pl.BlockSpec((block, cols), lambda i: (i, column))


def whole_spec(rows, cols):
    return pl.BlockSpec((rows, cols), lambda i: (0, 0))


def shift_in(target_ref, next_ref, incoming_ref, window):
    block = target_ref.shape[0]
    last = pl.program_id(0) == pl.num_programs(0) - 1
    window[:block, :] = target_ref[...]
    window[block:, :] = jnp.where(last, incoming_ref[...], next_ref[...])
    return window[HEAD : HEAD + block, :]


def target_sums(target, incoming):
    rows, cols = target.shape
    block = min(BLOCK, rows)

    def body(target_ref, next_ref, incoming_ref, top_ref, sum_ref, window):
        shifted = shift_in(target_ref, next_ref, incoming_ref, window)
        top = jnp.max(shifted, -1, keepdims=True)
        top_ref[...] = top
        sum_ref[...] = jnp.sum(jnp.exp(shifted - top), -1, keepdims=True)

    per = block // 8
    return pl.pallas_call(
        body,
        grid=(rows // block,),
        in_specs=[
            row_spec(block, cols),
            pl.BlockSpec((8, cols), lambda i: (jnp.minimum((i + 1) * per, rows // 8 - 1), 0)),
            whole_spec(8, cols),
        ],
        out_specs=[row_spec(block, 1)] * 2,
        out_shape=[jax.ShapeDtypeStruct((rows, 1), F32)] * 2,
        scratch_shapes=[pltpu.VMEM((block + 8, cols), F32)],
        compiler_params=params(24),
        cost_estimate=cost(4 * rows * cols, 4 * rows * cols, rows * cols),
        name="target_sums",
    )(target, target, incoming)


def target_probs(target, incoming, top, total):
    rows, cols = target.shape
    block = min(BLOCK, rows)

    def body(target_ref, next_ref, incoming_ref, top_ref, sum_ref, prob_ref, entropy_ref, window):
        shifted = shift_in(target_ref, next_ref, incoming_ref, window)
        first = lax.axis_index("grp") * rows + pl.program_id(0) * block
        count = lax.axis_size("grp") * rows
        row = first + lax.broadcasted_iota(jnp.int32, (block, 1), 0)
        live = jnp.where(row < count - HEAD, 1.0, 0.0)
        log_target = shifted - (top_ref[...] + jnp.log(sum_ref[...]))
        prob = jnp.exp(log_target) * live
        prob_ref[...] = prob
        entropy_ref[...] = jnp.sum(prob * log_target, -1, keepdims=True)

    per = block // 8
    return pl.pallas_call(
        body,
        grid=(rows // block,),
        in_specs=[
            row_spec(block, cols),
            pl.BlockSpec((8, cols), lambda i: (jnp.minimum((i + 1) * per, rows // 8 - 1), 0)),
            whole_spec(8, cols),
            row_spec(block, 1),
            row_spec(block, 1),
        ],
        out_specs=[row_spec(block, cols), row_spec(block, 1)],
        out_shape=[
            jax.ShapeDtypeStruct((rows, cols), F32),
            jax.ShapeDtypeStruct((rows, 1), F32),
        ],
        scratch_shapes=[pltpu.VMEM((block + 8, cols), F32)],
        compiler_params=params(24),
        cost_estimate=cost(6 * rows * cols, 8 * rows * cols, rows * cols),
        name="target_probs",
    )(target, target, incoming, top, total)


def draft_chunk(target, acts, vocab_proj, column, sums):
    rows = target.shape[0]
    rank, width = vocab_proj.shape
    block = min(BLOCK, rows)

    def body(target_ref, acts_ref, proj_ref, *rest):
        draft_ref, top_ref, sum_ref = rest[-3:]
        draft = target_ref[...] + jnp.dot(
            acts_ref[...], proj_ref[...], preferred_element_type=F32
        )
        draft_ref[...] = draft
        top = jnp.max(draft, -1, keepdims=True)
        if sums is not None:
            top = jnp.maximum(top, rest[0][...])
        total = jnp.sum(jnp.exp(draft - top), -1, keepdims=True)
        if sums is not None:
            total = total + rest[1][...] * jnp.exp(rest[0][...] - top)
        top_ref[...] = top
        sum_ref[...] = total

    carried = () if sums is None else tuple(sums)
    draft, top, total = pl.pallas_call(
        body,
        grid=(rows // block,),
        in_specs=[
            row_spec(block, width, column),
            row_spec(block, rank),
            whole_spec(rank, width),
        ]
        + [row_spec(block, 1)] * len(carried),
        out_specs=[row_spec(block, width), row_spec(block, 1), row_spec(block, 1)],
        out_shape=[
            jax.ShapeDtypeStruct((rows, width), F32),
            jax.ShapeDtypeStruct((rows, 1), F32),
            jax.ShapeDtypeStruct((rows, 1), F32),
        ],
        compiler_params=params(16),
        cost_estimate=cost(2 * rows * rank * width, 8 * rows * width, rows * width),
        name="draft_chunk",
    )(target, acts, vocab_proj, *carried)
    return draft, (top, total)


def grad_chunk(draft, prob, label, acts, vocab_proj, column, sums, carried):
    rows, width = draft.shape
    rank = acts.shape[1]
    block = min(BLOCK, rows)

    def body(draft_ref, prob_ref, label_ref, acts_ref, proj_ref, top_ref, sum_ref, *rest):
        grad_ref, act_ref, loss_ref = rest[-3:]
        step = pl.program_id(0)
        first = lax.axis_index("grp") * rows + step * block
        count = lax.axis_size("grp") * rows
        row = first + lax.broadcasted_iota(jnp.int32, (block, 1), 0)
        live = jnp.where(row < count - HEAD, 1.0, 0.0)
        log_draft = draft_ref[...] - (top_ref[...] + jnp.log(sum_ref[...]))
        prob = prob_ref[...]
        place = lax.broadcasted_iota(jnp.int32, (block, width), 1) + column * width
        hit = jnp.where(place == label_ref[...], LAM, 0.0)
        loss = -jnp.sum((prob + hit) * log_draft, -1, keepdims=True)
        grad = ((live + LAM) * jnp.exp(log_draft) - prob - hit).astype(BF16)
        act = inner_cols(grad, proj_ref[...])
        if carried is not None:
            loss = loss + rest[1][...]
            act = act + rest[0][...]
        loss_ref[...] = loss
        act_ref[...] = act
        term = inner_rows(acts_ref[...], grad)

        @pl.when(step == 0)
        def _():
            grad_ref[...] = term

        @pl.when(step > 0)
        def _():
            grad_ref[...] += term

    extra = () if carried is None else tuple(carried)
    proj_grad, act, loss = pl.pallas_call(
        body,
        grid=(rows // block,),
        in_specs=[
            row_spec(block, width),
            row_spec(block, width, column),
            row_spec(block, 1),
            row_spec(block, rank),
            whole_spec(rank, width),
            row_spec(block, 1),
            row_spec(block, 1),
        ]
        + ([row_spec(block, rank), row_spec(block, 1)] if extra else []),
        out_specs=[whole_spec(rank, width), row_spec(block, rank), row_spec(block, 1)],
        out_shape=[
            jax.ShapeDtypeStruct((rank, width), F32),
            jax.ShapeDtypeStruct((rows, rank), F32),
            jax.ShapeDtypeStruct((rows, 1), F32),
        ],
        compiler_params=params(16),
        cost_estimate=cost(4 * rows * rank * width, 8 * rows * width, rows * width),
        name="grad_chunk",
    )(draft, prob, label, acts, vocab_proj, *sums, *extra)
    return proj_grad, (act, loss)


def on_device(hidden_states, target_logits, labels, down_weight, up_weight, head_weight):
    row_count, slice_cols = target_logits.shape
    book_count = labels.shape[1]
    group_count = lax.axis_size("grp")
    per_book = lax.axis_size("voc") // book_count
    block_rows = row_count // per_book
    position = lax.axis_index("voc")
    book_index = position // per_book
    book_part = position % per_book
    width = slice_cols // CHUNKS
    z_bits = list(range(group_count.bit_length() - 1))
    v_bits = list(range(lax.axis_size("voc").bit_length() - 1))
    v_other = v_bits[:1] + v_bits[:0:-1]

    def columns(c):
        return head_weight[:, c * width : (c + 1) * width]

    mine = own_bit("grp", 0)
    up_away, up_kept = half(up_weight, 1 - mine), half(up_weight, mine)
    away = [
        (jnp.dot(up_away, columns(c), preferred_element_type=F32) * VOCAB_SCALE).astype(F16)
        for c in range(CHUNKS)
    ]
    kept = [
        jnp.dot(up_kept, columns(c), preferred_element_type=F32) * VOCAB_SCALE
        for c in range(CHUNKS)
    ]
    vocab_proj = []
    for c in range(CHUNKS):
        part = kept[c] + swap(away[c], "grp", 0).astype(F32)
        total = reduce_bits(part, "grp", z_bits[1:], [F16] * len(z_bits))
        total = (total * (1.0 / VOCAB_SCALE)).astype(BF16)
        vocab_proj.append(gather_bits(total, "grp", z_bits))

    pre_part = jnp.dot(hidden_states, down_weight, preferred_element_type=F32)
    pre_act = reduce_bits(pre_part, "voc", v_bits, [F32] * len(v_bits))
    acts = gather_bits(jax.nn.silu(pre_act).astype(BF16), "voc", v_bits)

    bound = jnp.broadcast_to(jnp.max(jnp.abs(acts.astype(F32))), (8, 128))
    for bit in z_bits:
        bound = jnp.maximum(bound, swap(bound, "grp", bit))
    most = jnp.maximum(bound[0, 0] * (1.1 * group_count * row_count), 1e-30)
    grad_scale = jnp.exp2(jnp.floor(15.0 - jnp.log2(most)))

    devices = range(group_count)
    incoming = lax.ppermute(
        target_logits[:8], "grp", [(i + 1, i) for i in devices if i + 1 in devices]
    )
    top, total = over_books(tuple(target_sums(target_logits, incoming)), merge_sums, per_book)
    prob, entropy = target_probs(target_logits, incoming, top, total)
    label = lax.dynamic_slice_in_dim(labels, book_index, 1, 1) - book_part * slice_cols

    drafts, sums = [], None
    for c in range(CHUNKS):
        draft, sums = draft_chunk(target_logits, acts, vocab_proj[c], c, sums)
        drafts.append(draft)
    sums = over_books(tuple(sums), merge_sums, per_book)

    proj_parts, carried = [], None
    for c in range(CHUNKS):
        part, carried = grad_chunk(
            drafts[c], prob, label, acts, vocab_proj[c], c, sums, carried
        )
        proj_parts.append(part)
    act_part, loss = carried

    loss = over_books(loss + entropy, jnp.add, per_book)
    frame_loss = lax.dynamic_slice_in_dim(loss, book_part * block_rows, block_rows, 0)
    frame_loss = frame_loss.reshape(1, 1, block_rows)

    up_part = 0.0
    for c in range(CHUNKS):
        total = reduce_bits(proj_parts[c] * grad_scale, "grp", z_bits, [F16] * len(z_bits))
        total = (total * (1.0 / grad_scale)).astype(BF16)
        up_part = up_part + inner_cols(gather_bits(total, "grp", z_bits), columns(c))

    act_grad = reduce_bits(act_part, "voc", v_bits, [F32] * len(v_bits))
    pre_grad = gather_bits((act_grad * silu_slope(pre_act)).astype(BF16), "voc", v_bits)
    down_part = inner_rows(hidden_states, pre_grad)

    def finish(part, axis, bits, wires):
        total = reduce_bits(part, axis, bits, wires)
        return gather_bits(total.astype(BF16), axis, bits).astype(F32)

    rank = up_part.shape[0] // 2
    wires = [F32] + [BF16] * len(v_bits)
    grad_b = jnp.concatenate(
        [
            finish(p, "voc", o, wires)
            for p, o in zip((up_part[:rank], up_part[rank:]), (v_bits, v_other))
        ],
        0,
    )
    grad_a = finish(down_part, "grp", z_bits, [BF16] * len(z_bits))
    return frame_loss, grad_a, grad_b


def solution(mesh):
    in_specs = (
        P("grp", "voc"),
        P("grp", "voc"),
        P("grp", None),
        P("voc", None),
        P(None, "grp"),
        P("grp", "voc"),
    )
    out_specs = (P("voc", "grp", None), P("voc", None), P(None, "grp"))
    return jax.shard_map(
        on_device, mesh=mesh, in_specs=in_specs, out_specs=out_specs, check_vma=False
    )
```

```python
import jax
import jax.numpy as jnp
from jax import lax
from jax.experimental import pallas as pl
from jax.experimental.pallas import tpu as pltpu
from jax.sharding import PartitionSpec as P

HEAD = 2
LAM = 0.1
CHUNKS = 4
BLOCK = 256
VOCAB_SCALE = 128.0
F32 = jnp.float32
BF16 = jnp.bfloat16
F16 = jnp.float16


def swap(value, axis, bit):
    mask = 1 << bit
    pairs = [(i, i ^ mask) for i in range(lax.axis_size(axis))]
    return lax.ppermute(value, axis, pairs)


def own_bit(axis, bit):
    return (lax.axis_index(axis) >> bit) & 1


def half(value, which):
    rows = value.shape[0] // 2
    return lax.dynamic_slice_in_dim(value, which * rows, rows, 0)


def silu_slope(values):
    sigma = jax.nn.sigmoid(values)
    return sigma * (1.0 + values * (1.0 - sigma))


def inner_rows(left, right):
    return lax.dot_general(left, right, (((0,), (0,)), ((), ())), preferred_element_type=F32)


def inner_cols(left, right):
    return lax.dot_general(left, right, (((1,), (1,)), ((), ())), preferred_element_type=F32)


def over_books(values, combine, per_book):
    bit = 0
    while (1 << bit) < per_book:
        values = combine(values, jax.tree.map(lambda v: swap(v, "voc", bit), values))
        bit += 1
    return values


def merge_sums(a, b):
    top = jnp.maximum(a[0], b[0])
    return top, a[1] * jnp.exp(a[0] - top) + b[1] * jnp.exp(b[0] - top)


def params(megabytes):
    return pltpu.CompilerParams(
        dimension_semantics=("arbitrary",), vmem_limit_bytes=megabytes << 20
    )


def cost(flops, read, exps):
    return pl.CostEstimate(flops=flops // 4096, bytes_accessed=read // 4096, transcendentals=0)


def row_spec(block, cols, column=0):
    return pl.BlockSpec((block, cols), lambda i: (i, column))


def whole_spec(rows, cols):
    return pl.BlockSpec((rows, cols), lambda i: (0, 0))


def shift_in(target_ref, next_ref, incoming_ref, window):
    block = target_ref.shape[0]
    last = pl.program_id(0) == pl.num_programs(0) - 1
    window[:block, :] = target_ref[...]
    window[block:, :] = jnp.where(last, incoming_ref[...], next_ref[...])
    return window[HEAD : HEAD + block, :]


def target_sums(target, incoming):
    rows, cols = target.shape
    block = min(BLOCK, rows)

    def body(target_ref, next_ref, incoming_ref, top_ref, sum_ref, window):
        shifted = shift_in(target_ref, next_ref, incoming_ref, window)
        top = jnp.max(shifted, -1, keepdims=True)
        top_ref[...] = top
        sum_ref[...] = jnp.sum(jnp.exp(shifted - top), -1, keepdims=True)

    per = block // 8
    return pl.pallas_call(
        body,
        grid=(rows // block,),
        in_specs=[
            row_spec(block, cols),
            pl.BlockSpec((8, cols), lambda i: (jnp.minimum((i + 1) * per, rows // 8 - 1), 0)),
            whole_spec(8, cols),
        ],
        out_specs=[row_spec(block, 1)] * 2,
        out_shape=[jax.ShapeDtypeStruct((rows, 1), F32)] * 2,
        scratch_shapes=[pltpu.VMEM((block + 8, cols), F32)],
        compiler_params=params(50),
        cost_estimate=cost(4 * rows * cols, 4 * rows * cols, rows * cols),
        name="target_sums",
    )(target, target, incoming)


def target_pass(target, incoming):
    rows, cols = target.shape
    block = min(BLOCK, rows)

    def body(target_ref, next_ref, incoming_ref, prob_ref, entropy_ref, window):
        shifted = shift_in(target_ref, next_ref, incoming_ref, window)
        first = lax.axis_index("grp") * rows + pl.program_id(0) * block
        count = lax.axis_size("grp") * rows
        row = first + lax.broadcasted_iota(jnp.int32, (block, 1), 0)
        live = jnp.where(row < count - HEAD, 1.0, 0.0)
        below = shifted - jnp.max(shifted, -1, keepdims=True)
        raised = jnp.exp(below)
        total = jnp.sum(raised, -1, keepdims=True)
        scale = live / total
        prob_ref[...] = raised * scale
        entropy_ref[...] = scale * jnp.sum(raised * below, -1, keepdims=True) - live * jnp.log(total)

    per = block // 8
    return pl.pallas_call(
        body,
        grid=(rows // block,),
        in_specs=[
            row_spec(block, cols),
            pl.BlockSpec((8, cols), lambda i: (jnp.minimum((i + 1) * per, rows // 8 - 1), 0)),
            whole_spec(8, cols),
        ],
        out_specs=[row_spec(block, cols), row_spec(block, 1)],
        out_shape=[
            jax.ShapeDtypeStruct((rows, cols), F32),
            jax.ShapeDtypeStruct((rows, 1), F32),
        ],
        scratch_shapes=[pltpu.VMEM((block + 8, cols), F32)],
        compiler_params=params(50),
        cost_estimate=cost(6 * rows * cols, 8 * rows * cols, rows * cols),
        name="target_pass",
    )(target, target, incoming)


def target_probs(target, incoming, top, total):
    rows, cols = target.shape
    block = min(BLOCK, rows)

    def body(target_ref, next_ref, incoming_ref, top_ref, sum_ref, prob_ref, entropy_ref, window):
        shifted = shift_in(target_ref, next_ref, incoming_ref, window)
        first = lax.axis_index("grp") * rows + pl.program_id(0) * block
        count = lax.axis_size("grp") * rows
        row = first + lax.broadcasted_iota(jnp.int32, (block, 1), 0)
        live = jnp.where(row < count - HEAD, 1.0, 0.0)
        log_target = shifted - (top_ref[...] + jnp.log(sum_ref[...]))
        prob = jnp.exp(log_target) * live
        prob_ref[...] = prob
        entropy_ref[...] = jnp.sum(prob * log_target, -1, keepdims=True)

    per = block // 8
    return pl.pallas_call(
        body,
        grid=(rows // block,),
        in_specs=[
            row_spec(block, cols),
            pl.BlockSpec((8, cols), lambda i: (jnp.minimum((i + 1) * per, rows // 8 - 1), 0)),
            whole_spec(8, cols),
            row_spec(block, 1),
            row_spec(block, 1),
        ],
        out_specs=[row_spec(block, cols), row_spec(block, 1)],
        out_shape=[
            jax.ShapeDtypeStruct((rows, cols), F32),
            jax.ShapeDtypeStruct((rows, 1), F32),
        ],
        scratch_shapes=[pltpu.VMEM((block + 8, cols), F32)],
        compiler_params=params(50),
        cost_estimate=cost(6 * rows * cols, 8 * rows * cols, rows * cols),
        name="target_probs",
    )(target, target, incoming, top, total)


def draft_chunk(target, acts, vocab_proj, column, sums):
    rows = target.shape[0]
    rank, width = vocab_proj.shape
    block = min(BLOCK, rows)

    def body(target_ref, acts_ref, proj_ref, *rest):
        draft_ref, top_ref, sum_ref = rest[-3:]
        draft = target_ref[...] + jnp.dot(
            acts_ref[...], proj_ref[...], preferred_element_type=F32
        )
        draft_ref[...] = draft
        top = jnp.max(draft, -1, keepdims=True)
        if sums is not None:
            top = jnp.maximum(top, rest[0][...])
        total = jnp.sum(jnp.exp(draft - top), -1, keepdims=True)
        if sums is not None:
            total = total + rest[1][...] * jnp.exp(rest[0][...] - top)
        top_ref[...] = top
        sum_ref[...] = total

    carried = () if sums is None else tuple(sums)
    draft, top, total = pl.pallas_call(
        body,
        grid=(rows // block,),
        in_specs=[
            row_spec(block, width, column),
            row_spec(block, rank),
            whole_spec(rank, width),
        ]
        + [row_spec(block, 1)] * len(carried),
        out_specs=[row_spec(block, width), row_spec(block, 1), row_spec(block, 1)],
        out_shape=[
            jax.ShapeDtypeStruct((rows, width), F32),
            jax.ShapeDtypeStruct((rows, 1), F32),
            jax.ShapeDtypeStruct((rows, 1), F32),
        ],
        compiler_params=params(16),
        cost_estimate=cost(2 * rows * rank * width, 8 * rows * width, rows * width),
        name="draft_chunk",
    )(target, acts, vocab_proj, *carried)
    return draft, (top, total)


def grad_chunk(draft, prob, label, acts, vocab_proj, column, sums, carried):
    rows, width = draft.shape
    rank = acts.shape[1]
    half_rank = rank // 2
    block = min(BLOCK, rows)

    def body(draft_ref, prob_ref, label_ref, acts_ref, proj_ref, top_ref, sum_ref, *rest):
        away_ref, kept_ref, act_ref, loss_ref, totals = rest[-5:]
        step = pl.program_id(0)
        first = lax.axis_index("grp") * rows + step * block
        count = lax.axis_size("grp") * rows
        row = first + lax.broadcasted_iota(jnp.int32, (block, 1), 0)
        live = jnp.where(row < count - HEAD, 1.0, 0.0)
        log_draft = draft_ref[...] - (top_ref[...] + jnp.log(sum_ref[...]))
        prob = prob_ref[...]
        place = lax.broadcasted_iota(jnp.int32, (block, width), 1) + column * width
        hit = jnp.where(place == label_ref[...], LAM, 0.0)
        loss = -jnp.sum((prob + hit) * log_draft, -1, keepdims=True)
        grad = ((live + LAM) * jnp.exp(log_draft) - prob - hit).astype(BF16)
        act = inner_cols(grad, proj_ref[...])
        if carried is not None:
            loss = loss + rest[1][...]
            act = act + rest[0][...]
        loss_ref[...] = loss
        act_ref[...] = act
        term = inner_rows(acts_ref[...], grad)

        @pl.when(step == 0)
        def _():
            totals[...] = term

        @pl.when(step > 0)
        def _():
            totals[...] += term

        @pl.when(step == pl.num_programs(0) - 1)
        def _():
            mine = lax.axis_index("grp") & 1
            away_ref[...] = totals[pl.ds(pl.multiple_of((1 - mine) * half_rank, half_rank), half_rank), :]
            kept_ref[...] = totals[pl.ds(pl.multiple_of(mine * half_rank, half_rank), half_rank), :]

    extra = () if carried is None else tuple(carried)
    away, kept, act, loss = pl.pallas_call(
        body,
        grid=(rows // block,),
        in_specs=[
            row_spec(block, width),
            row_spec(block, width, column),
            row_spec(block, 1),
            row_spec(block, rank),
            whole_spec(rank, width),
            row_spec(block, 1),
            row_spec(block, 1),
        ]
        + ([row_spec(block, rank), row_spec(block, 1)] if extra else []),
        out_specs=[whole_spec(half_rank, width)] * 2 + [row_spec(block, rank), row_spec(block, 1)],
        out_shape=[
            jax.ShapeDtypeStruct((half_rank, width), F32),
            jax.ShapeDtypeStruct((half_rank, width), F32),
            jax.ShapeDtypeStruct((rows, rank), F32),
            jax.ShapeDtypeStruct((rows, 1), F32),
        ],
        scratch_shapes=[pltpu.VMEM((rank, width), F32)],
        compiler_params=params(16),
        cost_estimate=cost(4 * rows * rank * width, 8 * rows * width, rows * width),
        name="grad_chunk",
    )(draft, prob, label, acts, vocab_proj, *sums, *extra)
    return (away, kept), (act, loss)


def vocab_parts(up_weight, head_weight, width, first, end):
    rank, depth = up_weight.shape
    rows = rank // 2
    block = min(512, depth)
    count = end - first

    def body(up_ref, *rest):
        heads, outs, totals = rest[:count], rest[count:-1], rest[-1]
        step = pl.program_id(0)
        for c, head_ref in enumerate(heads):
            term = jnp.dot(up_ref[...], head_ref[...], preferred_element_type=F32)

            @pl.when(step == 0)
            def _():
                totals[c] = term

            @pl.when(step > 0)
            def _():
                totals[c] += term

        @pl.when(step == pl.num_programs(0) - 1)
        def _():
            mine = lax.axis_index("grp") & 1
            for c in range(count):
                outs[2 * c][...] = totals[c, pl.ds(pl.multiple_of((1 - mine) * rows, rows), rows), :]
                outs[2 * c + 1][...] = totals[c, pl.ds(pl.multiple_of(mine * rows, rows), rows), :]

    def column_spec(c):
        return pl.BlockSpec((block, width), lambda k: (k, c))

    outs = pl.pallas_call(
        body,
        grid=(depth // block,),
        in_specs=[pl.BlockSpec((rank, block), lambda k: (0, k))]
        + [column_spec(first + c) for c in range(count)],
        out_specs=[pl.BlockSpec((rows, width), lambda k: (0, 0))] * (2 * count),
        out_shape=[jax.ShapeDtypeStruct((rows, width), F32)] * (2 * count),
        scratch_shapes=[pltpu.VMEM((count, rank, width), F32)],
        compiler_params=params(56),
        cost_estimate=cost(2 * rank * depth * width * count, 2 * depth * width * count, 0),
        name="vocab_parts",
    )(up_weight, *([head_weight] * count))
    return [(outs[2 * c], outs[2 * c + 1]) for c in range(count)]


class Line:
    def __init__(self):
        self.mark = None

    def after(self, value):
        if self.mark is None:
            return value
        return lax.optimization_barrier((value, self.mark))[0]

    def put(self, value):
        self.mark = jax.tree.leaves(value)[0]
        return value


class Chain:
    def __init__(self, steps):
        self.steps = steps
        self.value = None

    def step(self, times=1):
        for _ in range(times):
            if self.steps is not None:
                try:
                    next(self.steps)
                except StopIteration as end:
                    self.value = end.value
                    self.steps = None

    def result(self):
        while self.steps is not None:
            self.step()
        return self.value


def sent_over(line, value, axis, bit):
    value = line.put(line.after(value))
    arrived = swap(value, axis, bit)
    yield
    return line.after(arrived)


def reduce_steps(line, pair, axis, bits, wires, scale=None):
    away, part = pair
    for index, (bit, wire) in enumerate(zip(bits[:-1], wires)):
        mine = own_bit(axis, bit)
        if index > 0:
            away, part = half(part, 1 - mine), half(part, mine)
        if scale is not None and index == 0:
            away, part = away * scale, part * scale
        arrived = yield from sent_over(line, away.astype(wire), axis, bit)
        part = part + arrived.astype(F32)
    sent = part.astype(wires[-1])
    arrived = yield from sent_over(line, sent, axis, bits[-1])
    total = sent.astype(F32) + arrived.astype(F32)
    return total if scale is None else total * (1.0 / scale)


def gather_steps(line, piece, axis, bits):
    for bit in reversed(bits[:-1]):
        mine = own_bit(axis, bit)
        other = yield from sent_over(line, piece, axis, bit)
        low = jnp.where(mine == 0, piece, other)
        high = jnp.where(mine == 0, other, piece)
        piece = jnp.concatenate((low, high), 0)
    return piece


def split_pair(part, axis, bits):
    mine = own_bit(axis, bits[0])
    return half(part, 1 - mine), half(part, mine)


def summed(line, pair, axis, bits, wires, between, scale=None):
    def steps():
        total = yield from reduce_steps(line, pair, axis, bits, wires, scale)
        piece = between(total)
        return (yield from gather_steps(line, piece, axis, bits))

    return Chain(steps())


def on_device(hidden_states, target_logits, labels, down_weight, up_weight, head_weight):
    row_count, slice_cols = target_logits.shape
    book_count = labels.shape[1]
    group_count = lax.axis_size("grp")
    per_book = lax.axis_size("voc") // book_count
    block_rows = row_count // per_book
    position = lax.axis_index("voc")
    book_index = position // per_book
    book_part = position % per_book
    width = slice_cols // CHUNKS
    z_bits = list(range(group_count.bit_length() - 1))
    v_bits = list(range(lax.axis_size("voc").bit_length() - 1))
    v_other = v_bits[:1] + v_bits[:0:-1]
    half_wires = [F16] * len(z_bits)
    line = Line()

    def to_bf16(total):
        return total.astype(BF16)

    vocab = []

    def start_vocab(pairs):
        for pair in pairs:
            vocab.append(
                summed(line, pair, "grp", z_bits, half_wires, to_bf16, VOCAB_SCALE)
            )

    start_vocab(vocab_parts(up_weight, head_weight, width, 0, 1))
    vocab[0].step()
    pre_part = line.put(
        jnp.dot(line.after(hidden_states), down_weight, preferred_element_type=F32)
    )
    kept_pre = []

    def activate(total):
        kept_pre.append(total)
        return jax.nn.silu(total).astype(BF16)

    pre = summed(
        line, split_pair(pre_part, "voc", v_bits), "voc", v_bits, [F32] * len(v_bits), activate
    )
    pre.step()
    start_vocab(vocab_parts(line.after(up_weight), head_weight, width, 1, CHUNKS))
    vocab[1].step()
    vocab[0].step()
    vocab[2].step()
    pre.step()
    vocab[1].step()
    vocab[3].step()
    devices = range(group_count)
    top_rows = line.put(line.after(target_logits[:8]))
    incoming = lax.ppermute(top_rows, "grp", [(i + 1, i) for i in devices if i + 1 in devices])
    vocab[0].step()
    pre.step()
    vocab[2].step()
    if per_book == 1:
        prob, entropy = target_pass(target_logits, line.after(incoming))
    else:
        top, total = target_sums(target_logits, incoming)
        top, total = over_books((top, total), merge_sums, per_book)
        prob, entropy = target_probs(target_logits, incoming, top, total)
    line.put(entropy)
    label = lax.dynamic_slice_in_dim(labels, book_index, 1, 1) - book_part * slice_cols
    pre.step()
    vocab[1].step()
    vocab[3].step()
    pre.step()
    vocab[2].step()
    acts = line.put(pre.result())

    bounds = [jnp.broadcast_to(jnp.max(jnp.abs(acts.astype(F32))), (8, 128))]

    def bound_steps():
        for bit in z_bits:
            arrived = yield from sent_over(line, bounds[-1], "grp", bit)
            bounds.append(jnp.maximum(bounds[-1], arrived))

    bounding = Chain(bound_steps())
    bounding.step()

    drafts, sums = [], None
    vocab_proj = []
    for c in range(CHUNKS):
        vocab_proj.append(line.put(vocab[c].result()))
        draft, sums = draft_chunk(target_logits, acts, vocab_proj[c], c, sums)
        drafts.append(line.put(draft))
        bounding.step()
        if c == 1:
            vocab[3].step()
    bounding.result()
    most = jnp.maximum(bounds[-1][0, 0] * (1.1 * group_count * row_count), 1e-30)
    grad_scale = jnp.exp2(jnp.floor(15.0 - jnp.log2(most)))
    sums = over_books(tuple(sums), merge_sums, per_book)

    grads, carried = [], None
    for c in range(CHUNKS):
        pair, carried = grad_chunk(
            line.after(drafts[c]), prob, label, acts, vocab_proj[c], c, sums, carried
        )
        line.put(pair)
        grads.append(summed(line, pair, "grp", z_bits, half_wires, to_bf16, grad_scale))
        grads[c].step()
        if c > 0:
            grads[c - 1].step()
    act_part, loss = carried
    act = summed(
        line,
        split_pair(act_part, "voc", v_bits),
        "voc",
        v_bits,
        [F32] * len(v_bits),
        lambda total: (total * silu_slope(kept_pre[0])).astype(BF16),
    )
    act.step()
    loss = over_books(loss + entropy, jnp.add, per_book)
    frame_loss = lax.dynamic_slice_in_dim(loss, book_part * block_rows, block_rows, 0)
    frame_loss = frame_loss.reshape(1, 1, block_rows)

    def columns(c):
        return head_weight[:, c * width : (c + 1) * width]

    up_part = 0.0

    def add_up(c):
        return line.put(up_part + inner_cols(grads[c].result(), columns(c)))

    grads[0].step()
    act.step()
    grads[CHUNKS - 1].step()
    up_part = add_up(0)
    grads[1].step()
    act.step()
    grads[2].step()
    up_part = add_up(1)
    act.step()
    grads[3].step()
    up_part = add_up(2)
    act.step()
    pre_grad = line.put(act.result())
    down_part = line.put(inner_rows(line.after(hidden_states), pre_grad))

    def final(total):
        return total.astype(BF16)

    def finish(part, axis, bits, wires):
        return summed(line, split_pair(part, axis, bits), axis, bits, wires, final)

    rows = down_part.shape[0] // 2
    downs = [
        finish(p, "grp", z_bits, [BF16] * len(z_bits))
        for p in (down_part[:rows], down_part[rows:])
    ]
    downs[0].step()
    up_part = add_up(3)
    rank = up_part.shape[0] // 2
    wires = [F32] + [BF16] * len(v_bits)
    ups = [
        finish(p, "voc", o, wires)
        for p, o in zip((up_part[:rank], up_part[rank:]), (v_bits, v_other))
    ]
    ups[0].step()
    ups[1].step()
    downs[1].step()
    while any(chain.steps is not None for chain in ups + downs):
        for chain in (ups[0], ups[1], downs[0], downs[1]):
            chain.step()
    grad_b = jnp.concatenate([chain.result().astype(F32) for chain in ups], 0)
    grad_a = jnp.concatenate([chain.result().astype(F32) for chain in downs], 0)
    return frame_loss, grad_a, grad_b


def solution(mesh):
    in_specs = (
        P("grp", "voc"),
        P("grp", "voc"),
        P("grp", None),
        P("voc", None),
        P(None, "grp"),
        P("grp", "voc"),
    )
    out_specs = (P("voc", "grp", None), P("voc", None), P(None, "grp"))
    return jax.shard_map(
        on_device, mesh=mesh, in_specs=in_specs, out_specs=out_specs, check_vma=False
    )
```

```python
import jax
import jax.numpy as jnp
from jax import lax
from jax.experimental import pallas as pl
from jax.experimental.pallas import tpu as pltpu
from jax.sharding import PartitionSpec as P

HEAD = 2
LAM = 0.1
CHUNKS = 2
PARTS = 4
BLOCK = 256
VOCAB_SCALE = 128.0
F32 = jnp.float32
BF16 = jnp.bfloat16
F16 = jnp.float16


def swap(value, axis, bit):
    mask = 1 << bit
    pairs = [(i, i ^ mask) for i in range(lax.axis_size(axis))]
    return lax.ppermute(value, axis, pairs)


def own_bit(axis, bit):
    return (lax.axis_index(axis) >> bit) & 1


def half(value, which):
    rows = value.shape[0] // 2
    return lax.dynamic_slice_in_dim(value, which * rows, rows, 0)


def silu_slope(values):
    sigma = jax.nn.sigmoid(values)
    return sigma * (1.0 + values * (1.0 - sigma))


def inner_rows(left, right):
    return lax.dot_general(left, right, (((0,), (0,)), ((), ())), preferred_element_type=F32)


def inner_cols(left, right):
    return lax.dot_general(left, right, (((1,), (1,)), ((), ())), preferred_element_type=F32)


def over_books(values, combine, per_book):
    bit = 0
    while (1 << bit) < per_book:
        values = combine(values, jax.tree.map(lambda v: swap(v, "voc", bit), values))
        bit += 1
    return values


def merge_sums(a, b):
    top = jnp.maximum(a[0], b[0])
    return top, a[1] * jnp.exp(a[0] - top) + b[1] * jnp.exp(b[0] - top)


def params(megabytes):
    return pltpu.CompilerParams(
        dimension_semantics=("arbitrary",), vmem_limit_bytes=megabytes << 20
    )


def cost(flops, read, exps):
    return pl.CostEstimate(flops=flops // 4096, bytes_accessed=read // 4096, transcendentals=0)


def row_spec(block, cols, column=0):
    return pl.BlockSpec((block, cols), lambda i: (i, column))


def whole_spec(rows, cols):
    return pl.BlockSpec((rows, cols), lambda i: (0, 0))


def shift_in(target_ref, next_ref, incoming_ref, window):
    block = target_ref.shape[0]
    last = pl.program_id(0) == pl.num_programs(0) - 1
    window[:block, :] = target_ref[...]
    window[block:, :] = jnp.where(last, incoming_ref[...], next_ref[...])
    return window[HEAD : HEAD + block, :]


def target_sums(target, incoming):
    rows, cols = target.shape
    block = min(BLOCK, rows)

    def body(target_ref, next_ref, incoming_ref, top_ref, sum_ref, window):
        shifted = shift_in(target_ref, next_ref, incoming_ref, window)
        top = jnp.max(shifted, -1, keepdims=True)
        top_ref[...] = top
        sum_ref[...] = jnp.sum(jnp.exp(shifted - top), -1, keepdims=True)

    per = block // 8
    return pl.pallas_call(
        body,
        grid=(rows // block,),
        in_specs=[
            row_spec(block, cols),
            pl.BlockSpec((8, cols), lambda i: (jnp.minimum((i + 1) * per, rows // 8 - 1), 0)),
            whole_spec(8, cols),
        ],
        out_specs=[row_spec(block, 1)] * 2,
        out_shape=[jax.ShapeDtypeStruct((rows, 1), F32)] * 2,
        scratch_shapes=[pltpu.VMEM((block + 8, cols), F32)],
        compiler_params=params(50),
        cost_estimate=cost(4 * rows * cols, 4 * rows * cols, rows * cols),
        name="target_sums",
    )(target, target, incoming)


def vocab_parts(up_weight, head_weight, width):
    rank, depth = up_weight.shape
    cols = head_weight.shape[1]
    rows = rank // 2
    block = depth // PARTS
    count = cols // width

    def body(up_ref, head_ref, *rest):
        outs, (buffer, totals, arrived) = rest[: 2 * count], rest[2 * count :]
        copies = [
            pltpu.make_async_copy(
                head_ref.at[pl.ds(k * block, block), :], buffer.at[k], arrived.at[k]
            )
            for k in range(PARTS)
        ]
        for copy in copies:
            copy.start()
        tile = min(512, cols)
        for k in range(PARTS):
            copies[k].wait()
            left = up_ref[:, k * block : (k + 1) * block]

            @pl.loop(0, cols // tile)
            def _(t):
                place = pl.ds(pl.multiple_of(t * tile, tile), tile)
                term = jnp.dot(left, buffer[k, :, place], preferred_element_type=F32)
                if k == 0:
                    totals[:, place] = term
                else:
                    totals[:, place] += term

        mine = lax.axis_index("grp") & 1
        for c in range(count):
            here = slice(c * width, (c + 1) * width)
            away = totals[pl.ds(pl.multiple_of((1 - mine) * rows, rows), rows), here]
            kept = totals[pl.ds(pl.multiple_of(mine * rows, rows), rows), here]
            outs[2 * c][...] = away * VOCAB_SCALE
            outs[2 * c + 1][...] = kept * VOCAB_SCALE

    outs = pl.pallas_call(
        body,
        in_specs=[pl.BlockSpec(memory_space=pltpu.VMEM), pl.BlockSpec(memory_space=pltpu.HBM)],
        out_specs=[pl.BlockSpec(memory_space=pltpu.VMEM)] * (2 * count),
        out_shape=[jax.ShapeDtypeStruct((rows, width), F32)] * (2 * count),
        scratch_shapes=[
            pltpu.VMEM((PARTS, block, cols), BF16),
            pltpu.VMEM((rank, cols), F32),
            pltpu.SemaphoreType.DMA((PARTS,)),
        ],
        compiler_params=pltpu.CompilerParams(vmem_limit_bytes=24 << 20),
        cost_estimate=cost(2 * rank * depth * cols, 2 * depth * cols, 0),
        name="vocab_parts",
    )(up_weight, head_weight)
    return [(outs[2 * c], outs[2 * c + 1]) for c in range(count)]


def draft_chunk(target, acts, pieces, column, sums):
    rows, rank = acts.shape
    half_rank, width = pieces[0].shape
    block = min(BLOCK, rows)

    def body(target_ref, acts_ref, own_ref, other_ref, *rest):
        draft_ref, proj_ref, most_ref, top_ref, sum_ref = rest[-5:]

        @pl.when(pl.program_id(0) == 0)
        def _():
            mine = lax.axis_index("grp") & 1
            proj_ref[pl.ds(pl.multiple_of(mine * half_rank, half_rank), half_rank), :] = own_ref[...]
            proj_ref[
                pl.ds(pl.multiple_of((1 - mine) * half_rank, half_rank), half_rank), :
            ] = other_ref[...]
            most_ref[...] = jnp.zeros_like(most_ref)

        size = jnp.max(jnp.abs(acts_ref[...].astype(F32)), 0, keepdims=True)
        most_ref[...] = jnp.maximum(most_ref[...], jnp.max(size, -1, keepdims=True))
        draft = target_ref[...] + jnp.dot(
            acts_ref[...], proj_ref[...], preferred_element_type=F32
        )
        draft_ref[...] = draft
        top = jnp.max(draft, -1, keepdims=True)
        if sums is not None:
            top = jnp.maximum(top, rest[0][...])
        total = jnp.sum(jnp.exp(draft - top), -1, keepdims=True)
        if sums is not None:
            total = total + rest[1][...] * jnp.exp(rest[0][...] - top)
        top_ref[...] = top
        sum_ref[...] = total

    carried = () if sums is None else tuple(sums)
    draft, proj, most, top, total = pl.pallas_call(
        body,
        grid=(rows // block,),
        in_specs=[
            row_spec(block, width, column),
            row_spec(block, rank),
            whole_spec(half_rank, width),
            whole_spec(half_rank, width),
        ]
        + [row_spec(block, 1)] * len(carried),
        out_specs=[
            row_spec(block, width),
            whole_spec(rank, width),
            whole_spec(8, 128),
            row_spec(block, 1),
            row_spec(block, 1),
        ],
        out_shape=[
            jax.ShapeDtypeStruct((rows, width), F32),
            jax.ShapeDtypeStruct((rank, width), BF16),
            jax.ShapeDtypeStruct((8, 128), F32),
            jax.ShapeDtypeStruct((rows, 1), F32),
            jax.ShapeDtypeStruct((rows, 1), F32),
        ],
        compiler_params=params(24),
        cost_estimate=cost(2 * rows * rank * width, 8 * rows * width, rows * width),
        name="draft_chunk",
    )(target, acts, *pieces, *carried)
    return draft, proj, most, (top, total)


def grad_chunk(draft, target, incoming, label, acts, vocab_proj, column, sums, sizes, carried):
    rows, width = draft.shape
    rank = acts.shape[1]
    half_rank = rank // 2
    block = min(BLOCK, rows)
    bounds = sizes.shape[0]

    def body(
        draft_ref, target_ref, next_ref, incoming_ref, label_ref, acts_ref, proj_ref,
        top_ref, sum_ref, target_top_ref, target_sum_ref, sizes_ref, *rest
    ):
        away_ref, kept_ref, scale_ref, act_ref, loss_ref, totals, window = rest[-7:]
        step = pl.program_id(0)
        count = lax.axis_size("grp") * rows
        row = lax.axis_index("grp") * rows + step * block
        row = row + lax.broadcasted_iota(jnp.int32, (block, 1), 0)
        live = jnp.where(row < count - HEAD, 1.0, 0.0)
        shifted = shift_in(target_ref, next_ref, incoming_ref, window)
        log_target = shifted - (target_top_ref[...] + jnp.log(target_sum_ref[...]))
        log_draft = draft_ref[...] - (top_ref[...] + jnp.log(sum_ref[...]))
        prob = live * jnp.exp(log_target)
        place = lax.broadcasted_iota(jnp.int32, (block, width), 1) + column * width
        hit = jnp.where(place == label_ref[...], LAM, 0.0)
        loss = jnp.sum(prob * (log_target - log_draft) - hit * log_draft, -1, keepdims=True)
        grad = ((live + LAM) * jnp.exp(log_draft) - prob - hit).astype(BF16)
        act = inner_cols(grad, proj_ref[...])
        if carried is not None:
            loss = loss + rest[1][...]
            act = act + rest[0][...]
        loss_ref[...] = loss
        act_ref[...] = act
        term = inner_rows(acts_ref[...], grad)

        @pl.when(step == 0)
        def _():
            totals[...] = term

        @pl.when(step > 0)
        def _():
            totals[...] += term

        @pl.when(step == pl.num_programs(0) - 1)
        def _():
            size = jnp.max(jnp.max(sizes_ref[...], 0), (0, 1), keepdims=True)
            most = jnp.maximum(size * (1.1 * count), 1e-30)
            scale = jnp.exp2(jnp.floor(15.0 - jnp.log(most) * 1.4426950408889634))
            scale_ref[...] = jnp.broadcast_to(scale, (8, 128))
            mine = lax.axis_index("grp") & 1
            away = totals[pl.ds(pl.multiple_of((1 - mine) * half_rank, half_rank), half_rank), :]
            kept = totals[pl.ds(pl.multiple_of(mine * half_rank, half_rank), half_rank), :]
            away_ref[...] = away * scale
            kept_ref[...] = kept * scale

    per = block // 8
    extra = () if carried is None else tuple(carried)
    away, kept, scale, act, loss = pl.pallas_call(
        body,
        grid=(rows // block,),
        in_specs=[
            row_spec(block, width),
            row_spec(block, width, column),
            pl.BlockSpec(
                (8, width), lambda i: (jnp.minimum((i + 1) * per, rows // 8 - 1), column)
            ),
            pl.BlockSpec((8, width), lambda i: (0, column)),
            row_spec(block, 1),
            row_spec(block, rank),
            whole_spec(rank, width),
        ]
        + [row_spec(block, 1)] * 4
        + [pl.BlockSpec((bounds, 8, 128), lambda i: (0, 0, 0))]
        + ([row_spec(block, rank), row_spec(block, 1)] if extra else []),
        out_specs=[whole_spec(half_rank, width)] * 2
        + [whole_spec(8, 128), row_spec(block, rank), row_spec(block, 1)],
        out_shape=[
            jax.ShapeDtypeStruct((half_rank, width), F32),
            jax.ShapeDtypeStruct((half_rank, width), F32),
            jax.ShapeDtypeStruct((8, 128), F32),
            jax.ShapeDtypeStruct((rows, rank), F32),
            jax.ShapeDtypeStruct((rows, 1), F32),
        ],
        scratch_shapes=[pltpu.VMEM((rank, width), F32), pltpu.VMEM((block + 8, width), F32)],
        compiler_params=params(24),
        cost_estimate=cost(4 * rows * rank * width, 8 * rows * width, rows * width),
        name="grad_chunk",
    )(draft, target, target, incoming, label, acts, vocab_proj, *sums, sizes, *extra)
    return (away, kept), scale[0, 0], (act, loss)


class Line:
    def __init__(self):
        self.mark = None

    def after(self, value):
        if self.mark is None:
            return value
        return lax.optimization_barrier((value, self.mark))[0]

    def put(self, value):
        self.mark = jax.tree.leaves(value)[0]
        return value


class Chain:
    def __init__(self, steps):
        self.steps = steps
        self.value = None

    def step(self, times=1):
        for _ in range(times):
            if self.steps is not None:
                try:
                    next(self.steps)
                except StopIteration as end:
                    self.value = end.value
                    self.steps = None

    def result(self):
        while self.steps is not None:
            self.step()
        return self.value


def sent_over(line, value, axis, bit):
    value = line.put(line.after(value))
    arrived = swap(value, axis, bit)
    yield
    return line.after(arrived)


def reduce_steps(line, pair, axis, bits, wires):
    away, part = pair
    for index, (bit, wire) in enumerate(zip(bits[:-1], wires)):
        mine = own_bit(axis, bit)
        if index > 0:
            away, part = half(part, 1 - mine), half(part, mine)
        arrived = yield from sent_over(line, away.astype(wire), axis, bit)
        part = part + arrived.astype(F32)
    sent = part.astype(wires[-1])
    arrived = yield from sent_over(line, sent, axis, bits[-1])
    return sent.astype(F32) + arrived.astype(F32)


def joined(axis, bit, own, other):
    mine = own_bit(axis, bit)
    low = jnp.where(mine == 0, own, other)
    high = jnp.where(mine == 0, other, own)
    return jnp.concatenate((low, high), 0)


def gather_steps(line, piece, axis, bits):
    for bit in reversed(bits[1:-1]):
        other = yield from sent_over(line, piece, axis, bit)
        piece = joined(axis, bit, piece, other)
    return piece


def split_pair(part, axis, bits):
    mine = own_bit(axis, bits[0])
    return half(part, 1 - mine), half(part, mine)


def summed(line, pair, axis, bits, wires, between, pieces):
    def steps():
        total = yield from reduce_steps(line, pair, axis, bits, wires)
        own = yield from gather_steps(line, between(total), axis, bits)
        pieces.append(own)
        other = yield from sent_over(line, own, axis, bits[0])
        pieces.append(other)

    return Chain(steps())


def first_of(chain, pieces):
    while not pieces:
        chain.step()
    return pieces[0]


def scattered(line, part, wire):
    count = lax.axis_size("voc")
    blocks = part.astype(wire).reshape(count, part.shape[0] // count, part.shape[1])
    blocks = line.put(line.after(blocks))
    arrived = lax.all_to_all(blocks, "voc", 0, 0)
    yield
    return jnp.sum(line.after(arrived).astype(F32), 0)


def over_voc(line, part, wire, between):
    def steps():
        total = yield from scattered(line, part, wire)
        rows = line.put(line.after(between(total)))
        whole = lax.all_gather(rows, "voc", axis=0, tiled=True)
        yield
        return line.after(whole)

    return Chain(steps())


def on_device(hidden_states, target_logits, labels, down_weight, up_weight, head_weight):
    row_count, slice_cols = target_logits.shape
    book_count = labels.shape[1]
    group_count = lax.axis_size("grp")
    per_book = lax.axis_size("voc") // book_count
    block_rows = row_count // per_book
    position = lax.axis_index("voc")
    book_index = position // per_book
    book_part = position % per_book
    width = slice_cols // CHUNKS
    chunks = range(CHUNKS)
    z_bits = list(range(group_count.bit_length() - 1))
    half_wires = [F16] * len(z_bits)
    line = Line()

    vocab_pieces = [[] for c in chunks]
    vocab = [
        summed(
            line, pair, "grp", z_bits, half_wires,
            lambda total: (total * (1.0 / VOCAB_SCALE)).astype(BF16), vocab_pieces[c],
        )
        for c, pair in enumerate(vocab_parts(up_weight, head_weight, width))
    ]
    for c in chunks:
        vocab[c].step()
    pre_part = line.put(
        jnp.dot(line.after(hidden_states), down_weight, preferred_element_type=F32)
    )
    kept_pre = []

    def activate(total):
        kept_pre.append(total)
        return jax.nn.silu(total).astype(BF16)

    pre = over_voc(line, pre_part, F32, activate)
    devices = range(group_count)
    top_rows = line.put(line.after(target_logits[:8]))
    incoming = lax.ppermute(top_rows, "grp", [(i + 1, i) for i in devices if i + 1 in devices])
    vocab[0].step()
    pre.step()
    target = tuple(target_sums(target_logits, line.after(incoming)))
    line.put(target[0])
    target = over_books(target, merge_sums, per_book)
    label = lax.dynamic_slice_in_dim(labels, book_index, 1, 1) - book_part * slice_cols
    vocab[1].step()
    pre.step()
    vocab[0].step()
    vocab[1].step()
    acts = line.put(pre.result())

    drafts, vocab_proj, sums = [], [], None
    for c in chunks:
        vocab[c].result()
        pieces = vocab_pieces[c]
        line.put(pieces[1])
        draft, proj, size, sums = draft_chunk(target_logits, acts, pieces, c, sums)
        drafts.append(line.put(draft))
        vocab_proj.append(proj)
        if c == 0:
            sizes = lax.all_gather(size, "grp", axis=0)
    sums = over_books(tuple(sums), merge_sums, per_book)

    grads, carried, grad_pieces = [], None, [[] for c in chunks]
    for c in chunks:
        pair, scale, carried = grad_chunk(
            line.after(drafts[c]), target_logits, incoming, label, acts, vocab_proj[c], c,
            (*sums, *target), sizes, carried,
        )
        line.put(pair)
        unscale = 1.0 / scale
        grads.append(
            summed(
                line, pair, "grp", z_bits, half_wires,
                lambda total, unscale=unscale: (total * unscale).astype(BF16), grad_pieces[c],
            )
        )
        grads[c].step()
    act_part, loss = carried
    act = over_voc(
        line, act_part, F32, lambda total: (total * silu_slope(kept_pre[0])).astype(BF16)
    )
    grads[0].step()
    act.step()
    grads[1].step()
    loss = over_books(loss, jnp.add, per_book)
    frame_loss = lax.dynamic_slice_in_dim(loss, book_part * block_rows, block_rows, 0)
    frame_loss = frame_loss.reshape(1, 1, block_rows)

    def columns(c):
        return head_weight[:, c * width : (c + 1) * width]

    def times_head(before, piece, c):
        return line.put(before + inner_cols(line.after(piece), columns(c)))

    act.step()
    grads[0].step()
    own_up = times_head(0.0, first_of(grads[0], grad_pieces[0]), 0)
    pre_grad = line.put(act.result())
    down_part = line.put(inner_rows(line.after(hidden_states), pre_grad))
    grads[0].result()
    other_up = times_head(0.0, grad_pieces[0][1], 0)
    grads[1].step()
    rows = down_part.shape[0] // 2
    down_pieces = [[], []]
    downs = [
        summed(
            line, split_pair(part, "grp", z_bits), "grp", z_bits, [BF16] * len(z_bits),
            lambda total: total.astype(BF16), down_pieces[i],
        )
        for i, part in enumerate((down_part[:rows], down_part[rows:]))
    ]
    downs[0].step()
    downs[1].step()
    own_up = times_head(own_up, first_of(grads[1], grad_pieces[1]), 1)
    grads[1].result()
    other_up = times_head(other_up, grad_pieces[1][1], 1)
    up_part = joined("grp", 0, own_up, other_up)
    ups = over_voc(line, up_part, BF16, lambda total: total.astype(BF16))
    ups.step()
    downs[0].step()
    downs[1].step()
    ups.step()
    downs[0].step()
    downs[1].step()
    grad_b = ups.result().astype(F32)
    for chain in downs:
        chain.result()
    grad_a = jnp.concatenate(
        [joined("grp", z_bits[0], *pieces).astype(F32) for pieces in down_pieces], 0
    )
    return frame_loss, grad_a, grad_b


def solution(mesh):
    in_specs = (
        P("grp", "voc"),
        P("grp", "voc"),
        P("grp", None),
        P("voc", None),
        P(None, "grp"),
        P("grp", "voc"),
    )
    out_specs = (P("voc", "grp", None), P("voc", None), P(None, "grp"))
    return jax.shard_map(
        on_device, mesh=mesh, in_specs=in_specs, out_specs=out_specs, check_vma=False
    )
```

```python
import jax
import jax.numpy as jnp
from jax import lax
from jax.experimental import pallas as pl
from jax.experimental.pallas import tpu as pltpu
from jax.sharding import PartitionSpec as P

HEAD = 2
LAM = 0.1
CHUNKS = 4
PARTS = 4
BLOCK = 256
GROUP = 16
VOCAB_SCALE = 128.0
F32 = jnp.float32
BF16 = jnp.bfloat16
F16 = jnp.float16


def swap(value, axis, bit):
    mask = 1 << bit
    pairs = [(i, i ^ mask) for i in range(lax.axis_size(axis))]
    return lax.ppermute(value, axis, pairs)


def own_bit(axis, bit):
    return (lax.axis_index(axis) >> bit) & 1


def half(value, which):
    rows = value.shape[0] // 2
    return lax.dynamic_slice_in_dim(value, which * rows, rows, 0)


def silu_slope(values):
    sigma = jax.nn.sigmoid(values)
    return sigma * (1.0 + values * (1.0 - sigma))


def inner_rows(left, right):
    return lax.dot_general(left, right, (((0,), (0,)), ((), ())), preferred_element_type=F32)


def inner_cols(left, right):
    return lax.dot_general(left, right, (((1,), (1,)), ((), ())), preferred_element_type=F32)


def over_books(values, combine, per_book):
    bit = 0
    while (1 << bit) < per_book:
        values = combine(values, jax.tree.map(lambda v: swap(v, "voc", bit), values))
        bit += 1
    return values


def merge_sums(a, b):
    top = jnp.maximum(a[0], b[0])
    return top, a[1] * jnp.exp(a[0] - top) + b[1] * jnp.exp(b[0] - top)


def params(megabytes):
    return pltpu.CompilerParams(
        dimension_semantics=("arbitrary",), vmem_limit_bytes=megabytes << 20
    )


def cost(flops, read, exps):
    return pl.CostEstimate(flops=flops // 4096, bytes_accessed=read // 4096, transcendentals=0)


def row_spec(block, cols, column=0):
    return pl.BlockSpec((block, cols), lambda i: (i, column))


def whole_spec(rows, cols):
    return pl.BlockSpec((rows, cols), lambda i: (0, 0))


def shift_in(target_ref, next_ref, incoming_ref, window):
    block = target_ref.shape[0]
    last = pl.program_id(0) == pl.num_programs(0) - 1
    window[:block, :] = target_ref[...]
    window[block:, :] = jnp.where(last, incoming_ref[...], next_ref[...])
    return window[HEAD : HEAD + block, :]


def target_sums(target, incoming):
    rows, cols = target.shape
    block = min(BLOCK, rows)

    def body(target_ref, next_ref, incoming_ref, top_ref, sum_ref, window):
        shifted = shift_in(target_ref, next_ref, incoming_ref, window)
        top = jnp.max(shifted, -1, keepdims=True)
        top_ref[...] = top
        sum_ref[...] = jnp.sum(jnp.exp(shifted - top), -1, keepdims=True)

    per = block // 8
    return pl.pallas_call(
        body,
        grid=(rows // block,),
        in_specs=[
            row_spec(block, cols),
            pl.BlockSpec((8, cols), lambda i: (jnp.minimum((i + 1) * per, rows // 8 - 1), 0)),
            whole_spec(8, cols),
        ],
        out_specs=[row_spec(block, 1)] * 2,
        out_shape=[jax.ShapeDtypeStruct((rows, 1), F32)] * 2,
        scratch_shapes=[pltpu.VMEM((block + 8, cols), F32)],
        compiler_params=params(50),
        cost_estimate=cost(4 * rows * cols, 4 * rows * cols, rows * cols),
        name="target_sums",
    )(target, target, incoming)


def vocab_parts(up_weight, head_weight, count):
    rank, depth = up_weight.shape
    cols = head_weight.shape[1]
    chunk = rank // count
    rows = chunk // 2
    block = depth // PARTS

    def body(up_ref, head_ref, *rest):
        outs, (buffer, totals, arrived) = rest[: 2 * count], rest[2 * count :]
        copies = [
            pltpu.make_async_copy(
                head_ref.at[pl.ds(k * block, block), :], buffer.at[k], arrived.at[k]
            )
            for k in range(PARTS)
        ]
        for copy in copies:
            copy.start()
        tile = min(512, cols)
        for k in range(PARTS):
            copies[k].wait()
            left = up_ref[:, k * block : (k + 1) * block]

            @pl.loop(0, cols // tile)
            def _(t):
                place = pl.ds(pl.multiple_of(t * tile, tile), tile)
                term = jnp.dot(left, buffer[k, :, place], preferred_element_type=F32)
                if k == 0:
                    totals[:, place] = term
                else:
                    totals[:, place] += term

        mine = lax.axis_index("grp") & 1
        for c in range(count):
            away = totals[pl.ds(pl.multiple_of(c * chunk + (1 - mine) * rows, rows), rows), :]
            kept = totals[pl.ds(pl.multiple_of(c * chunk + mine * rows, rows), rows), :]
            outs[2 * c][...] = away * VOCAB_SCALE
            outs[2 * c + 1][...] = kept * VOCAB_SCALE

    outs = pl.pallas_call(
        body,
        in_specs=[pl.BlockSpec(memory_space=pltpu.VMEM), pl.BlockSpec(memory_space=pltpu.HBM)],
        out_specs=[pl.BlockSpec(memory_space=pltpu.VMEM)] * (2 * count),
        out_shape=[jax.ShapeDtypeStruct((rows, cols), F32)] * (2 * count),
        scratch_shapes=[
            pltpu.VMEM((PARTS, block, cols), BF16),
            pltpu.VMEM((rank, cols), F32),
            pltpu.SemaphoreType.DMA((PARTS,)),
        ],
        compiler_params=pltpu.CompilerParams(vmem_limit_bytes=24 << 20),
        cost_estimate=cost(2 * rank * depth * cols, 2 * depth * cols, 0),
        name="vocab_parts",
    )(up_weight, head_weight)
    return [(outs[2 * c], outs[2 * c + 1]) for c in range(count)]


def lane_parts(values, combine):
    parts = values[:, :128]
    for first in range(128, values.shape[1], 128):
        parts = combine(parts, values[:, first : first + 128])
    return parts


def draft_sums(target, acts, pieces):
    vocab_proj = jnp.concatenate([joined("grp", 0, *pair) for pair in pieces], 0)
    draft = target + jnp.dot(acts, vocab_proj, preferred_element_type=F32)
    top = jnp.max(draft, -1, keepdims=True)
    return top, jnp.sum(jnp.exp(draft - top), -1, keepdims=True)


def middle(target, incoming, label, acts, pieces, target_sum, sizes, draft_sum):
    rows, cols = target.shape
    rank = acts.shape[1]
    count = len(pieces)
    chunk = rank // count
    half_rows = chunk // 2
    block = min(BLOCK, rows)
    flat = [piece for pair in pieces for piece in pair]
    given = () if draft_sum is None else tuple(draft_sum)

    def body(target_ref, next_ref, incoming_ref, label_ref, acts_ref, *rest):
        target_top_ref, target_sum_ref, sizes_ref = rest[: 3]
        piece_refs = rest[3 : 3 + 2 * count]
        given_refs = rest[3 + 2 * count : 3 + 2 * count + len(given)]
        outs = rest[3 + 2 * count + len(given) :]
        parts, (scale_ref, act_ref, loss_ref) = outs[: 2 * count], outs[2 * count : 2 * count + 3]
        proj, totals, window, draft, grad, lanes, wide, wider = outs[2 * count + 3 :]
        step = pl.program_id(0)
        mine = lax.axis_index("grp") & 1

        @pl.when(step == 0)
        def _():
            for c in range(count):
                first = pl.multiple_of(c * chunk + mine * half_rows, half_rows)
                proj[pl.ds(first, half_rows), :] = piece_refs[2 * c][...]
                first = pl.multiple_of(c * chunk + (1 - mine) * half_rows, half_rows)
                proj[pl.ds(first, half_rows), :] = piece_refs[2 * c + 1][...]

        total_rows = lax.axis_size("grp") * rows
        row = lax.axis_index("grp") * rows + step * block
        row = row + lax.broadcasted_iota(jnp.int32, (block, 1), 0)
        live = row < total_rows - HEAD
        last = step == pl.num_programs(0) - 1
        window[:block, :] = target_ref[...]
        window[block:, :] = jnp.where(last, incoming_ref[...], next_ref[...])
        draft[...] = jnp.dot(acts_ref[...], proj[...], preferred_element_type=F32)

        def group(i):
            return pl.ds(pl.multiple_of(i * GROUP, GROUP), GROUP)

        if not given:

            @pl.loop(0, block // GROUP)
            def _(i):
                here = group(i)
                value = draft[here, :] + target_ref[here, :]
                draft[here, :] = value
                lanes[here, :] = lane_parts(value, jnp.maximum)

            wide[...] = jnp.broadcast_to(jnp.max(lanes[...], -1, keepdims=True), (block, 128))

            @pl.loop(0, block // GROUP)
            def _(i):
                here = group(i)
                raised = jnp.exp(draft[here, :] - wide[here, :1])
                lanes[here, :] = lane_parts(raised, jnp.add)

            sums = jnp.sum(lanes[...], -1, keepdims=True)
            wide[...] = jnp.broadcast_to(wide[:, :1] + jnp.log(sums), (block, 128))
        else:
            draft[...] += target_ref[...]
            wide[...] = jnp.broadcast_to(
                given_refs[0][...] + jnp.log(given_refs[1][...]), (block, 128)
            )
        below = target_top_ref[...] + jnp.log(target_sum_ref[...])
        wider[...] = jnp.broadcast_to(jnp.where(live, below, 1e6), (block, 128))
        lanes[...] = jnp.broadcast_to(jnp.where(live, 1.0 + LAM, LAM), (block, 128))
        shifted = window
        place = lax.broadcasted_iota(jnp.int32, (GROUP, cols), 1)

        @pl.loop(0, block // GROUP)
        def _(i):
            here = group(i)
            log_draft = draft[here, :] - wide[here, :1]
            there = window[pl.ds(pl.multiple_of(i * GROUP, GROUP), GROUP + 8), :]
            log_target = there[HEAD : HEAD + GROUP, :] - wider[here, :1]
            prob = jnp.exp(log_target)
            marked = prob + jnp.where(place == label_ref[here, :], LAM, 0.0)
            loss = prob * log_target - marked * log_draft
            grad[here, :] = (lanes[here, :1] * jnp.exp(log_draft) - marked).astype(BF16)
            lanes[here, :] = lane_parts(loss, jnp.add)

        loss_ref[...] = jnp.sum(lanes[...], -1, keepdims=True)
        act_ref[...] = inner_cols(grad[...], proj[...])
        term = inner_rows(acts_ref[...], grad[...])

        @pl.when(step == 0)
        def _():
            totals[...] = term

        @pl.when(step > 0)
        def _():
            totals[...] += term

        @pl.when(last)
        def _():
            size = jnp.max(sizes_ref[...], (0, 1), keepdims=True)
            most = jnp.maximum(size * (1.1 * total_rows), 1e-30)
            scale = jnp.exp2(jnp.floor(15.0 - jnp.log(most) * 1.4426950408889634))
            scale_ref[...] = jnp.broadcast_to(scale, (8, 128))
            for c in range(count):
                first = pl.multiple_of(c * chunk + (1 - mine) * half_rows, half_rows)
                parts[2 * c][...] = totals[pl.ds(first, half_rows), :] * scale
                first = pl.multiple_of(c * chunk + mine * half_rows, half_rows)
                parts[2 * c + 1][...] = totals[pl.ds(first, half_rows), :] * scale

    per = block // 8
    outs = pl.pallas_call(
        body,
        grid=(rows // block,),
        in_specs=[
            row_spec(block, cols),
            pl.BlockSpec((8, cols), lambda i: (jnp.minimum((i + 1) * per, rows // 8 - 1), 0)),
            whole_spec(8, cols),
            row_spec(block, 1),
            row_spec(block, rank),
            row_spec(block, 1),
            row_spec(block, 1),
            whole_spec(8, 128),
        ]
        + [whole_spec(half_rows, cols)] * (2 * count)
        + [row_spec(block, 1)] * len(given),
        out_specs=[whole_spec(half_rows, cols)] * (2 * count)
        + [whole_spec(8, 128), row_spec(block, rank), row_spec(block, 1)],
        out_shape=[jax.ShapeDtypeStruct((half_rows, cols), F32)] * (2 * count)
        + [
            jax.ShapeDtypeStruct((8, 128), F32),
            jax.ShapeDtypeStruct((rows, rank), F32),
            jax.ShapeDtypeStruct((rows, 1), F32),
        ],
        scratch_shapes=[
            pltpu.VMEM((rank, cols), BF16),
            pltpu.VMEM((rank, cols), F32),
            pltpu.VMEM((block + 8, cols), F32),
            pltpu.VMEM((block, cols), F32),
            pltpu.VMEM((block, cols), BF16),
            pltpu.VMEM((block, 128), F32),
            pltpu.VMEM((block, 128), F32),
            pltpu.VMEM((block, 128), F32),
        ],
        compiler_params=params(48),
        cost_estimate=cost(6 * rows * rank * cols, 4 * rows * cols, 2 * rows * cols),
        name="middle",
    )(target, target, incoming, label, acts, *target_sum, sizes, *flat, *given)
    pairs = [(outs[2 * c], outs[2 * c + 1]) for c in range(count)]
    return pairs, outs[2 * count][0, 0], outs[2 * count + 1], outs[2 * count + 2]


class Line:
    def __init__(self):
        self.mark = None

    def after(self, value):
        if self.mark is None:
            return value
        return lax.optimization_barrier((value, self.mark))[0]

    def put(self, value):
        self.mark = jax.tree.leaves(value)[0]
        return value


class Chain:
    def __init__(self, steps):
        self.steps = steps
        self.value = None

    def step(self, times=1):
        for _ in range(times):
            if self.steps is not None:
                try:
                    next(self.steps)
                except StopIteration as end:
                    self.value = end.value
                    self.steps = None

    def result(self):
        while self.steps is not None:
            self.step()
        return self.value


def sent_over(line, value, axis, bit):
    value = line.put(line.after(value))
    arrived = swap(value, axis, bit)
    yield
    return line.after(arrived)


def reduce_steps(line, pair, axis, bits, wires):
    away, part = pair
    for index, (bit, wire) in enumerate(zip(bits[:-1], wires)):
        mine = own_bit(axis, bit)
        if index > 0:
            away, part = half(part, 1 - mine), half(part, mine)
        arrived = yield from sent_over(line, away.astype(wire), axis, bit)
        part = part + arrived.astype(F32)
    sent = part.astype(wires[-1])
    arrived = yield from sent_over(line, sent, axis, bits[-1])
    return sent.astype(F32) + arrived.astype(F32)


def joined(axis, bit, own, other):
    mine = own_bit(axis, bit)
    low = jnp.where(mine == 0, own, other)
    high = jnp.where(mine == 0, other, own)
    return jnp.concatenate((low, high), 0)


def gather_steps(line, piece, axis, bits):
    for bit in reversed(bits[1:-1]):
        other = yield from sent_over(line, piece, axis, bit)
        piece = joined(axis, bit, piece, other)
    return piece


def split_pair(part, axis, bits):
    mine = own_bit(axis, bits[0])
    return half(part, 1 - mine), half(part, mine)


def summed(line, pair, axis, bits, wires, between, pieces):
    def steps():
        total = yield from reduce_steps(line, pair, axis, bits, wires)
        own = yield from gather_steps(line, between(total), axis, bits)
        pieces.append(own)
        other = yield from sent_over(line, own, axis, bits[0])
        pieces.append(other)

    return Chain(steps())


def over_voc(line, part, wire, between):
    def steps():
        count = lax.axis_size("voc")
        blocks = part.astype(wire).reshape(count, part.shape[0] // count, part.shape[1])
        blocks = line.put(line.after(blocks))
        arrived = lax.all_to_all(blocks, "voc", 0, 0)
        yield
        total = jnp.sum(line.after(arrived).astype(F32), 0)
        own = line.put(line.after(between(total)))
        copies = jnp.broadcast_to(own[None], (count, *own.shape))
        arrived = lax.all_to_all(copies, "voc", 0, 0)
        yield
        return line.after(arrived).reshape(part.shape)

    return Chain(steps())


def on_device(hidden_states, target_logits, labels, down_weight, up_weight, head_weight):
    row_count, slice_cols = target_logits.shape
    book_count = labels.shape[1]
    group_count = lax.axis_size("grp")
    per_book = lax.axis_size("voc") // book_count
    block_rows = row_count // per_book
    position = lax.axis_index("voc")
    book_index = position // per_book
    book_part = position % per_book
    rank = up_weight.shape[0]
    z_bits = list(range(group_count.bit_length() - 1))
    count = max(1, min(CHUNKS, rank // (32 << max(0, len(z_bits) - 2))))
    chunks = range(count)
    half_wires = [F16] * len(z_bits)
    line = Line()

    vocab_pieces = [[] for c in chunks]
    vocab = [
        summed(
            line, pair, "grp", z_bits, half_wires,
            lambda total: (total * (1.0 / VOCAB_SCALE)).astype(BF16), vocab_pieces[c],
        )
        for c, pair in enumerate(vocab_parts(up_weight, head_weight, count))
    ]
    vocab[0].step()
    devices = range(group_count)
    top_rows = line.put(line.after(target_logits[:8]))
    incoming = lax.ppermute(top_rows, "grp", [(i + 1, i) for i in devices if i + 1 in devices])
    for c in chunks[1:]:
        vocab[c].step()
    pre_part = line.put(
        jnp.dot(line.after(hidden_states), down_weight, preferred_element_type=F32)
    )
    kept_pre = []

    def activate(total):
        kept_pre.append(total)
        return jax.nn.silu(total).astype(BF16)

    pre = over_voc(line, pre_part, F32, activate)
    vocab[0].step()
    pre.step()
    for c in chunks[1:]:
        vocab[c].step()
    target = tuple(target_sums(target_logits, line.after(incoming)))
    line.put(target[0])
    target = over_books(target, merge_sums, per_book)
    label = lax.dynamic_slice_in_dim(labels, book_index, 1, 1) - book_part * slice_cols
    pre.step()
    vocab[0].step()
    acts = line.put(pre.result())
    bounds = [jnp.broadcast_to(jnp.max(jnp.abs(acts.astype(F32))), (8, 128))]

    def bound_steps():
        for bit in z_bits:
            arrived = yield from sent_over(line, bounds[-1], "grp", bit)
            bounds.append(jnp.maximum(bounds[-1], arrived))

    bounding = Chain(bound_steps())
    bounding.step()
    if count > 1:
        vocab[1].step()
    bounding.step()
    for c in chunks[2:]:
        vocab[c].step()
    bounding.result()
    for c in chunks:
        vocab[c].result()
    draft_sum = None
    if per_book > 1:
        draft_sum = over_books(
            draft_sums(target_logits, acts, vocab_pieces), merge_sums, per_book
        )
    pairs, scale, act_part, loss = middle(
        target_logits, incoming, label, acts, vocab_pieces, target, bounds[-1], draft_sum
    )
    line.put(pairs[0])

    unscale = 1.0 / scale
    grad_pieces = [[] for c in chunks]
    grads = [
        summed(
            line, pair, "grp", z_bits, half_wires,
            lambda total: (total * unscale).astype(BF16), grad_pieces[c],
        )
        for c, pair in enumerate(pairs)
    ]
    for c in chunks:
        grads[c].step()
    act = over_voc(
        line, act_part, F32, lambda total: (total * silu_slope(kept_pre[0])).astype(BF16)
    )
    grads[0].step()
    act.step()
    for c in chunks[1:]:
        grads[c].step()
    loss = over_books(loss, jnp.add, per_book)
    frame_loss = lax.dynamic_slice_in_dim(loss, book_part * block_rows, block_rows, 0)
    frame_loss = frame_loss.reshape(1, 1, block_rows)
    act.step()
    grads[0].step()
    pre_grad = line.put(act.result())
    down_part = line.put(inner_rows(line.after(hidden_states), pre_grad))
    rows = down_part.shape[0] // 2
    down_pieces = [[], []]
    downs = [
        summed(
            line, split_pair(part, "grp", z_bits), "grp", z_bits, [BF16] * len(z_bits),
            lambda total: total.astype(BF16), down_pieces[i],
        )
        for i, part in enumerate((down_part[:rows], down_part[rows:]))
    ]
    for c in chunks[1:2]:
        grads[c].step()
    downs[0].step()
    downs[1].step()

    split = 2 if count % 2 == 0 and rank // 2 >= 16 * lax.axis_size("voc") else 1
    ups = []

    def start_up(part):
        taken = chunks[part * count // split : (part + 1) * count // split]
        for c in taken:
            grads[c].result()
        grad = jnp.concatenate([joined("grp", 0, *grad_pieces[c]) for c in taken], 0)
        up_part = inner_cols(line.after(grad), head_weight)
        ups.append(over_voc(line, up_part, BF16, lambda total: total.astype(BF16)))
        ups[-1].step()

    start_up(0)
    for c in chunks[2:]:
        grads[c].step()
    downs[0].step()
    downs[1].step()
    if split > 1:
        start_up(1)
    for chain in ups:
        chain.step()
    downs[0].step()
    downs[1].step()
    grad_b = jnp.concatenate([chain.result().astype(F32) for chain in ups], 0)
    for chain in downs:
        chain.result()
    grad_a = jnp.concatenate(
        [joined("grp", z_bits[0], *pieces).astype(F32) for pieces in down_pieces], 0
    )
    return frame_loss, grad_a, grad_b


def solution(mesh):
    in_specs = (
        P("grp", "voc"),
        P("grp", "voc"),
        P("grp", None),
        P("voc", None),
        P(None, "grp"),
        P("grp", "voc"),
    )
    out_specs = (P("voc", "grp", None), P("voc", None), P(None, "grp"))
    return jax.shard_map(
        on_device, mesh=mesh, in_specs=in_specs, out_specs=out_specs, check_vma=False
    )
```

```python
import jax
import jax.numpy as jnp
from jax import lax
from jax.experimental import pallas as pl
from jax.experimental.pallas import tpu as pltpu
from jax.sharding import PartitionSpec as P

HEAD = 2
LAM = 0.1
CHUNKS = 2
PARTS = 4
BLOCK = 256
VOCAB_SCALE = 128.0
PRE_SCALE = 64.0
F32 = jnp.float32
BF16 = jnp.bfloat16
F16 = jnp.float16


def swap(value, axis, bit):
    mask = 1 << bit
    pairs = [(i, i ^ mask) for i in range(lax.axis_size(axis))]
    return lax.ppermute(value, axis, pairs)


def own_bit(axis, bit):
    return (lax.axis_index(axis) >> bit) & 1


def half(value, which):
    rows = value.shape[0] // 2
    return lax.dynamic_slice_in_dim(value, which * rows, rows, 0)


def silu_slope(values):
    sigma = jax.nn.sigmoid(values)
    return sigma * (1.0 + values * (1.0 - sigma))


def inner_rows(left, right):
    return lax.dot_general(left, right, (((0,), (0,)), ((), ())), preferred_element_type=F32)


def inner_cols(left, right):
    return lax.dot_general(left, right, (((1,), (1,)), ((), ())), preferred_element_type=F32)


def over_books(values, combine, per_book):
    bit = 0
    while (1 << bit) < per_book:
        values = combine(values, jax.tree.map(lambda v: swap(v, "voc", bit), values))
        bit += 1
    return values


def merge_sums(a, b):
    top = jnp.maximum(a[0], b[0])
    return top, a[1] * jnp.exp(a[0] - top) + b[1] * jnp.exp(b[0] - top)


def params(megabytes):
    return pltpu.CompilerParams(
        dimension_semantics=("arbitrary",), vmem_limit_bytes=megabytes << 20
    )


def cost(flops, read, exps):
    return pl.CostEstimate(flops=flops // 4096, bytes_accessed=read // 4096, transcendentals=0)


def row_spec(block, cols, column=0):
    return pl.BlockSpec((block, cols), lambda i: (i, column))


def whole_spec(rows, cols):
    return pl.BlockSpec((rows, cols), lambda i: (0, 0))


def shift_in(target_ref, next_ref, incoming_ref, window):
    block = target_ref.shape[0]
    last = pl.program_id(0) == pl.num_programs(0) - 1
    window[:block, :] = target_ref[...]
    window[block:, :] = jnp.where(last, incoming_ref[...], next_ref[...])
    return window[HEAD : HEAD + block, :]


def target_sums(target, incoming):
    rows, cols = target.shape
    block = min(BLOCK, rows)

    def body(target_ref, next_ref, incoming_ref, top_ref, sum_ref, window):
        shifted = shift_in(target_ref, next_ref, incoming_ref, window)
        top = jnp.max(shifted, -1, keepdims=True)
        top_ref[...] = top
        sum_ref[...] = jnp.sum(jnp.exp(shifted - top), -1, keepdims=True)

    per = block // 8
    return pl.pallas_call(
        body,
        grid=(rows // block,),
        in_specs=[
            row_spec(block, cols),
            pl.BlockSpec((8, cols), lambda i: (jnp.minimum((i + 1) * per, rows // 8 - 1), 0)),
            whole_spec(8, cols),
        ],
        out_specs=[row_spec(block, 1)] * 2,
        out_shape=[jax.ShapeDtypeStruct((rows, 1), F32)] * 2,
        scratch_shapes=[pltpu.VMEM((block + 8, cols), F32)],
        compiler_params=params(50),
        cost_estimate=cost(4 * rows * cols, 4 * rows * cols, rows * cols),
        name="target_sums",
    )(target, target, incoming)


def target_pass(target, incoming):
    rows, cols = target.shape
    block = min(BLOCK, rows)

    def body(target_ref, next_ref, incoming_ref, prob_ref, entropy_ref, window):
        shifted = shift_in(target_ref, next_ref, incoming_ref, window)
        first = lax.axis_index("grp") * rows + pl.program_id(0) * block
        count = lax.axis_size("grp") * rows
        row = first + lax.broadcasted_iota(jnp.int32, (block, 1), 0)
        live = jnp.where(row < count - HEAD, 1.0, 0.0)
        below = shifted - jnp.max(shifted, -1, keepdims=True)
        raised = jnp.exp(below)
        total = jnp.sum(raised, -1, keepdims=True)
        scale = live / total
        prob_ref[...] = raised * scale
        entropy_ref[...] = scale * jnp.sum(raised * below, -1, keepdims=True) - live * jnp.log(total)

    per = block // 8
    return pl.pallas_call(
        body,
        grid=(rows // block,),
        in_specs=[
            row_spec(block, cols),
            pl.BlockSpec((8, cols), lambda i: (jnp.minimum((i + 1) * per, rows // 8 - 1), 0)),
            whole_spec(8, cols),
        ],
        out_specs=[row_spec(block, cols), row_spec(block, 1)],
        out_shape=[
            jax.ShapeDtypeStruct((rows, cols), F32),
            jax.ShapeDtypeStruct((rows, 1), F32),
        ],
        scratch_shapes=[pltpu.VMEM((block + 8, cols), F32)],
        compiler_params=params(50),
        cost_estimate=cost(6 * rows * cols, 8 * rows * cols, rows * cols),
        name="target_pass",
    )(target, target, incoming)


def target_probs(target, incoming, top, total):
    rows, cols = target.shape
    block = min(BLOCK, rows)

    def body(target_ref, next_ref, incoming_ref, top_ref, sum_ref, prob_ref, entropy_ref, window):
        shifted = shift_in(target_ref, next_ref, incoming_ref, window)
        first = lax.axis_index("grp") * rows + pl.program_id(0) * block
        count = lax.axis_size("grp") * rows
        row = first + lax.broadcasted_iota(jnp.int32, (block, 1), 0)
        live = jnp.where(row < count - HEAD, 1.0, 0.0)
        log_target = shifted - (top_ref[...] + jnp.log(sum_ref[...]))
        prob = jnp.exp(log_target) * live
        prob_ref[...] = prob
        entropy_ref[...] = jnp.sum(prob * log_target, -1, keepdims=True)

    per = block // 8
    return pl.pallas_call(
        body,
        grid=(rows // block,),
        in_specs=[
            row_spec(block, cols),
            pl.BlockSpec((8, cols), lambda i: (jnp.minimum((i + 1) * per, rows // 8 - 1), 0)),
            whole_spec(8, cols),
            row_spec(block, 1),
            row_spec(block, 1),
        ],
        out_specs=[row_spec(block, cols), row_spec(block, 1)],
        out_shape=[
            jax.ShapeDtypeStruct((rows, cols), F32),
            jax.ShapeDtypeStruct((rows, 1), F32),
        ],
        scratch_shapes=[pltpu.VMEM((block + 8, cols), F32)],
        compiler_params=params(50),
        cost_estimate=cost(6 * rows * cols, 8 * rows * cols, rows * cols),
        name="target_probs",
    )(target, target, incoming, top, total)


def vocab_parts(up_weight, head_weight, width):
    rank, depth = up_weight.shape
    cols = head_weight.shape[1]
    rows = rank // 2
    block = depth // PARTS
    count = cols // width

    def body(up_ref, head_ref, *rest):
        outs, (buffer, totals, arrived) = rest[: 2 * count], rest[2 * count :]
        copies = [
            pltpu.make_async_copy(
                head_ref.at[pl.ds(k * block, block), :], buffer.at[k], arrived.at[k]
            )
            for k in range(PARTS)
        ]
        for copy in copies:
            copy.start()
        tile = min(512, cols)
        for k in range(PARTS):
            copies[k].wait()
            left = up_ref[:, k * block : (k + 1) * block]

            @pl.loop(0, cols // tile)
            def _(t):
                place = pl.ds(pl.multiple_of(t * tile, tile), tile)
                term = jnp.dot(left, buffer[k, :, place], preferred_element_type=F32)
                if k == 0:
                    totals[:, place] = term
                else:
                    totals[:, place] += term

        mine = lax.axis_index("grp") & 1
        for c in range(count):
            here = slice(c * width, (c + 1) * width)
            away = totals[pl.ds(pl.multiple_of((1 - mine) * rows, rows), rows), here]
            kept = totals[pl.ds(pl.multiple_of(mine * rows, rows), rows), here]
            outs[2 * c][...] = away * VOCAB_SCALE
            outs[2 * c + 1][...] = kept * VOCAB_SCALE

    outs = pl.pallas_call(
        body,
        in_specs=[pl.BlockSpec(memory_space=pltpu.VMEM), pl.BlockSpec(memory_space=pltpu.HBM)],
        out_specs=[pl.BlockSpec(memory_space=pltpu.VMEM)] * (2 * count),
        out_shape=[jax.ShapeDtypeStruct((rows, width), F32)] * (2 * count),
        scratch_shapes=[
            pltpu.VMEM((PARTS, block, cols), BF16),
            pltpu.VMEM((rank, cols), F32),
            pltpu.SemaphoreType.DMA((PARTS,)),
        ],
        compiler_params=pltpu.CompilerParams(vmem_limit_bytes=56 << 20),
        cost_estimate=cost(2 * rank * depth * cols, 2 * depth * cols, 0),
        name="vocab_parts",
    )(up_weight, head_weight)
    return [(outs[2 * c], outs[2 * c + 1]) for c in range(count)]


def draft_chunk(target, acts, pieces, column, sums):
    rows, rank = acts.shape
    half_rank, width = pieces[0].shape
    block = min(BLOCK, rows)

    def body(target_ref, acts_ref, own_ref, other_ref, *rest):
        draft_ref, proj_ref, top_ref, sum_ref = rest[-4:]

        @pl.when(pl.program_id(0) == 0)
        def _():
            mine = lax.axis_index("grp") & 1
            proj_ref[pl.ds(pl.multiple_of(mine * half_rank, half_rank), half_rank), :] = own_ref[...]
            proj_ref[
                pl.ds(pl.multiple_of((1 - mine) * half_rank, half_rank), half_rank), :
            ] = other_ref[...]

        draft = target_ref[...] + jnp.dot(
            acts_ref[...], proj_ref[...], preferred_element_type=F32
        )
        draft_ref[...] = draft
        top = jnp.max(draft, -1, keepdims=True)
        if sums is not None:
            top = jnp.maximum(top, rest[0][...])
        total = jnp.sum(jnp.exp(draft - top), -1, keepdims=True)
        if sums is not None:
            total = total + rest[1][...] * jnp.exp(rest[0][...] - top)
        top_ref[...] = top
        sum_ref[...] = total

    carried = () if sums is None else tuple(sums)
    draft, proj, top, total = pl.pallas_call(
        body,
        grid=(rows // block,),
        in_specs=[
            row_spec(block, width, column),
            row_spec(block, rank),
            whole_spec(half_rank, width),
            whole_spec(half_rank, width),
        ]
        + [row_spec(block, 1)] * len(carried),
        out_specs=[
            row_spec(block, width),
            whole_spec(rank, width),
            row_spec(block, 1),
            row_spec(block, 1),
        ],
        out_shape=[
            jax.ShapeDtypeStruct((rows, width), F32),
            jax.ShapeDtypeStruct((rank, width), BF16),
            jax.ShapeDtypeStruct((rows, 1), F32),
            jax.ShapeDtypeStruct((rows, 1), F32),
        ],
        compiler_params=params(54),
        cost_estimate=cost(2 * rows * rank * width, 8 * rows * width, rows * width),
        name="draft_chunk",
    )(target, acts, *pieces, *carried)
    return draft, proj, (top, total)


def grad_chunk(draft, prob, label, acts, vocab_proj, column, sums, carried):
    rows, width = draft.shape
    rank = acts.shape[1]
    half_rank = rank // 2
    block = min(BLOCK, rows)

    def body(draft_ref, prob_ref, label_ref, acts_ref, proj_ref, top_ref, sum_ref, *rest):
        away_ref, kept_ref, act_ref, loss_ref, totals = rest[-5:]
        step = pl.program_id(0)
        first = lax.axis_index("grp") * rows + step * block
        count = lax.axis_size("grp") * rows
        row = first + lax.broadcasted_iota(jnp.int32, (block, 1), 0)
        live = jnp.where(row < count - HEAD, 1.0, 0.0)
        log_draft = draft_ref[...] - (top_ref[...] + jnp.log(sum_ref[...]))
        prob = prob_ref[...]
        place = lax.broadcasted_iota(jnp.int32, (block, width), 1) + column * width
        hit = jnp.where(place == label_ref[...], LAM, 0.0)
        loss = -jnp.sum((prob + hit) * log_draft, -1, keepdims=True)
        grad = ((live + LAM) * jnp.exp(log_draft) - prob - hit).astype(BF16)
        act = inner_cols(grad, proj_ref[...])
        if carried is not None:
            loss = loss + rest[1][...]
            act = act + rest[0][...]
        loss_ref[...] = loss
        act_ref[...] = act
        term = inner_rows(acts_ref[...], grad)

        @pl.when(step == 0)
        def _():
            totals[...] = term

        @pl.when(step > 0)
        def _():
            totals[...] += term

        @pl.when(step == pl.num_programs(0) - 1)
        def _():
            mine = lax.axis_index("grp") & 1
            away = totals[pl.ds(pl.multiple_of((1 - mine) * half_rank, half_rank), half_rank), :]
            away_ref[...] = away.astype(BF16)
            kept_ref[...] = totals[pl.ds(pl.multiple_of(mine * half_rank, half_rank), half_rank), :]

    extra = () if carried is None else tuple(carried)
    away, kept, act, loss = pl.pallas_call(
        body,
        grid=(rows // block,),
        in_specs=[
            row_spec(block, width),
            row_spec(block, width, column),
            row_spec(block, 1),
            row_spec(block, rank),
            whole_spec(rank, width),
            row_spec(block, 1),
            row_spec(block, 1),
        ]
        + ([row_spec(block, rank), row_spec(block, 1)] if extra else []),
        out_specs=[whole_spec(half_rank, width)] * 2 + [row_spec(block, rank), row_spec(block, 1)],
        out_shape=[
            jax.ShapeDtypeStruct((half_rank, width), BF16),
            jax.ShapeDtypeStruct((half_rank, width), F32),
            jax.ShapeDtypeStruct((rows, rank), F32),
            jax.ShapeDtypeStruct((rows, 1), F32),
        ],
        scratch_shapes=[pltpu.VMEM((rank, width), F32)],
        compiler_params=params(54),
        cost_estimate=cost(4 * rows * rank * width, 8 * rows * width, rows * width),
        name="grad_chunk",
    )(draft, prob, label, acts, vocab_proj, *sums, *extra)
    return (away, kept), (act, loss)


class Line:
    def __init__(self):
        self.mark = None

    def after(self, value):
        if self.mark is None:
            return value
        return lax.optimization_barrier((value, self.mark))[0]

    def put(self, value):
        self.mark = jax.tree.leaves(value)[0]
        return value


class Chain:
    def __init__(self, steps):
        self.steps = steps
        self.value = None

    def step(self, times=1):
        for _ in range(times):
            if self.steps is not None:
                try:
                    next(self.steps)
                except StopIteration as end:
                    self.value = end.value
                    self.steps = None

    def result(self):
        while self.steps is not None:
            self.step()
        return self.value


def sent_over(line, value, axis, bit):
    value = line.put(line.after(value))
    arrived = swap(value, axis, bit)
    yield
    return line.after(arrived)


def reduce_steps(line, pair, axis, bits, wires, alike):
    away, part = pair
    for index, (bit, wire) in enumerate(zip(bits[:-1], wires)):
        mine = own_bit(axis, bit)
        if index > 0:
            away, part = half(part, 1 - mine), half(part, mine)
        arrived = yield from sent_over(line, away.astype(wire), axis, bit)
        part = part + arrived.astype(F32)
    sent = part.astype(wires[-1])
    arrived = yield from sent_over(line, sent, axis, bits[-1])
    return (sent.astype(F32) if alike else part) + arrived.astype(F32)


def joined(axis, bit, own, other):
    mine = own_bit(axis, bit)
    low = jnp.where(mine == 0, own, other)
    high = jnp.where(mine == 0, other, own)
    return jnp.concatenate((low, high), 0)


def gather_steps(line, piece, axis, bits):
    for bit in reversed(bits[1:-1]):
        other = yield from sent_over(line, piece, axis, bit)
        piece = joined(axis, bit, piece, other)
    return piece


def split_pair(part, axis, bits):
    mine = own_bit(axis, bits[0])
    return half(part, 1 - mine), half(part, mine)


def summed(line, pair, axis, bits, wires, between, pieces, alike=False):
    def steps():
        total = yield from reduce_steps(line, pair, axis, bits, wires, alike)
        own = yield from gather_steps(line, between(total), axis, bits)
        pieces.append(own)
        other = yield from sent_over(line, own, axis, bits[0])
        pieces.append(other)

    return Chain(steps())


def first_of(chain, pieces):
    while not pieces:
        chain.step()
    return pieces[0]


def all_to_all(blocks, groups):
    return lax.all_to_all(blocks, "voc", 0, 0, axis_index_groups=groups)


def over_voc(line, part, wire, between, paired=False):
    def steps():
        count = lax.axis_size("voc")
        rows = part
        groups = None
        if paired:
            count = count // 2
            groups = [list(range(parity, 2 * count, 2)) for parity in range(2)]
            mine = own_bit("voc", 0)
            away, kept = half(part, 1 - mine), half(part, mine)
            arrived = yield from sent_over(line, away.astype(wire), "voc", 0)
            rows = kept + arrived.astype(F32)
        blocks = rows.astype(wire).reshape(count, rows.shape[0] // count, rows.shape[1])
        blocks = line.put(line.after(blocks))
        arrived = all_to_all(blocks, groups)
        yield
        total = jnp.sum(line.after(arrived).astype(F32), 0)
        own = line.put(line.after(between(total)))
        copies = jnp.broadcast_to(own[None], (count, *own.shape))
        arrived = all_to_all(copies, groups)
        yield
        whole = line.after(arrived).reshape(rows.shape)
        if paired:
            other = yield from sent_over(line, whole, "voc", 0)
            return joined("voc", 0, whole, other)
        return whole

    return Chain(steps())


def on_device(hidden_states, target_logits, labels, down_weight, up_weight, head_weight):
    row_count, slice_cols = target_logits.shape
    book_count = labels.shape[1]
    group_count = lax.axis_size("grp")
    per_book = lax.axis_size("voc") // book_count
    block_rows = row_count // per_book
    position = lax.axis_index("voc")
    book_index = position // per_book
    book_part = position % per_book
    width = slice_cols // CHUNKS
    chunks = range(CHUNKS)
    z_bits = list(range(group_count.bit_length() - 1))
    line = Line()

    vocab_pieces = [[] for c in chunks]
    vocab = [
        summed(
            line, pair, "grp", z_bits, [F16] * len(z_bits),
            lambda total: (total * (1.0 / VOCAB_SCALE)).astype(BF16), vocab_pieces[c],
        )
        for c, pair in enumerate(vocab_parts(up_weight, head_weight, width))
    ]
    vocab[0].step()
    devices = range(group_count)
    top_rows = line.put(line.after(target_logits[:8]))
    incoming = lax.ppermute(top_rows, "grp", [(i + 1, i) for i in devices if i + 1 in devices])
    vocab[1].step()
    pre_part = line.put(
        jnp.dot(line.after(hidden_states), down_weight, preferred_element_type=F32)
    )
    kept_pre = []

    def activate(total):
        kept_pre.append(total * (1.0 / PRE_SCALE))
        return jax.nn.silu(kept_pre[0]).astype(BF16)

    pre = over_voc(line, pre_part * PRE_SCALE, F16, activate)
    vocab[0].step()
    pre.step()
    vocab[1].step()
    if per_book == 1:
        prob, entropy = target_pass(target_logits, line.after(incoming))
    else:
        top, total = target_sums(target_logits, incoming)
        top, total = over_books((top, total), merge_sums, per_book)
        prob, entropy = target_probs(target_logits, incoming, top, total)
    line.put(entropy)
    label = lax.dynamic_slice_in_dim(labels, book_index, 1, 1) - book_part * slice_cols
    pre.step()
    vocab[0].step()
    acts = line.put(pre.result())
    vocab[1].step()

    drafts, vocab_proj, sums = [], [], None
    for c in chunks:
        vocab[c].result()
        pieces = vocab_pieces[c]
        line.put(pieces[1])
        draft, proj, sums = draft_chunk(target_logits, acts, pieces, c, sums)
        drafts.append(line.put(draft))
        vocab_proj.append(proj)
    sums = over_books(tuple(sums), merge_sums, per_book)

    grads, carried, grad_pieces = [], None, [[] for c in chunks]
    for c in chunks:
        pair, carried = grad_chunk(
            line.after(drafts[c]), prob, label, acts, vocab_proj[c], c, sums, carried
        )
        line.put(pair)
        grads.append(
            summed(
                line, pair, "grp", z_bits, [BF16] * len(z_bits),
                lambda total: total.astype(BF16), grad_pieces[c],
            )
        )
        grads[c].step()
    act_part, loss = carried
    act = over_voc(
        line, act_part, F32, lambda total: (total * silu_slope(kept_pre[0])).astype(BF16)
    )
    grads[0].step()
    grads[1].step()
    act.step()
    loss = over_books(loss + entropy, jnp.add, per_book)
    frame_loss = lax.dynamic_slice_in_dim(loss, book_part * block_rows, block_rows, 0)
    frame_loss = frame_loss.reshape(1, 1, block_rows)

    def columns(c):
        return head_weight[:, c * width : (c + 1) * width]

    def times_head(before, piece, c):
        return line.put(before + inner_cols(line.after(piece), columns(c)))

    own_up = times_head(0.0, first_of(grads[0], grad_pieces[0]), 0)
    act.step()
    grads[0].result()
    other_up = times_head(0.0, grad_pieces[0][1], 0)
    pre_grad = line.put(act.result())
    down_part = line.put(inner_rows(line.after(hidden_states), pre_grad))
    own = first_of(grads[1], grad_pieces[1])
    rows = down_part.shape[0] // 2
    down_pieces = [[], []]
    downs = [
        summed(
            line, split_pair(part, "grp", z_bits), "grp", z_bits, [BF16] * len(z_bits),
            lambda total: total.astype(BF16), down_pieces[i], True,
        )
        for i, part in enumerate((down_part[:rows], down_part[rows:]))
    ]
    downs[0].step()
    downs[1].step()
    own_up = times_head(own_up, own, 1)
    grads[1].result()
    other_up = times_head(other_up, grad_pieces[1][1], 1)
    up_part = joined("grp", 0, own_up, other_up)
    ups = over_voc(line, up_part, BF16, lambda total: total.astype(BF16), True)
    ups.step()
    downs[0].step()
    downs[1].step()
    ups.step()
    ups.step()
    downs[0].step()
    downs[1].step()
    ups.step()
    grad_b = ups.result().astype(F32)
    for chain in downs:
        chain.result()
    grad_a = jnp.concatenate(
        [joined("grp", z_bits[0], *pieces).astype(F32) for pieces in down_pieces], 0
    )
    return frame_loss, grad_a, grad_b


def solution(mesh):
    in_specs = (
        P("grp", "voc"),
        P("grp", "voc"),
        P("grp", None),
        P("voc", None),
        P(None, "grp"),
        P("grp", "voc"),
    )
    out_specs = (P("voc", "grp", None), P("voc", None), P(None, "grp"))
    return jax.shard_map(
        on_device, mesh=mesh, in_specs=in_specs, out_specs=out_specs, check_vma=False
    )
```

```python
import jax
import jax.numpy as jnp
from jax import lax
from jax.experimental import pallas as pl
from jax.experimental.pallas import tpu as pltpu
from jax.sharding import PartitionSpec as P

HEAD = 2
LAM = 0.1
CHUNKS = 2
BLOCK = 256
VOCAB_SCALE = 128.0
PRE_SCALE = 64.0
F32 = jnp.float32
BF16 = jnp.bfloat16
F16 = jnp.float16


def swap(value, axis, bit):
    mask = 1 << bit
    pairs = [(i, i ^ mask) for i in range(lax.axis_size(axis))]
    return lax.ppermute(value, axis, pairs)


def own_bit(axis, bit):
    return (lax.axis_index(axis) >> bit) & 1


def half(value, which):
    rows = value.shape[0] // 2
    return lax.dynamic_slice_in_dim(value, which * rows, rows, 0)


def silu_slope(values):
    sigma = jax.nn.sigmoid(values)
    return sigma * (1.0 + values * (1.0 - sigma))


def inner_rows(left, right):
    return lax.dot_general(left, right, (((0,), (0,)), ((), ())), preferred_element_type=F32)


def inner_cols(left, right):
    return lax.dot_general(left, right, (((1,), (1,)), ((), ())), preferred_element_type=F32)


def over_books(values, combine, per_book):
    bit = 0
    while (1 << bit) < per_book:
        values = combine(values, jax.tree.map(lambda v: swap(v, "voc", bit), values))
        bit += 1
    return values


def merge_sums(a, b):
    top = jnp.maximum(a[0], b[0])
    return top, a[1] * jnp.exp(a[0] - top) + b[1] * jnp.exp(b[0] - top)


def params(megabytes):
    return pltpu.CompilerParams(
        dimension_semantics=("arbitrary",), vmem_limit_bytes=megabytes << 20
    )


def cost(flops, read, exps):
    return pl.CostEstimate(flops=flops // 4096, bytes_accessed=read // 4096, transcendentals=0)


def row_spec(block, cols, column=0):
    return pl.BlockSpec((block, cols), lambda i: (i, column))


def whole_spec(rows, cols):
    return pl.BlockSpec((rows, cols), lambda i: (0, 0))


def shift_in(target_ref, next_ref, incoming_ref, window):
    block = target_ref.shape[0]
    last = pl.program_id(0) == pl.num_programs(0) - 1
    window[:block, :] = target_ref[...]
    window[block:, :] = jnp.where(last, incoming_ref[...], next_ref[...])
    return window[HEAD : HEAD + block, :]


def target_sums(target, incoming):
    rows, cols = target.shape
    block = min(BLOCK, rows)

    def body(target_ref, next_ref, incoming_ref, top_ref, sum_ref, window):
        shifted = shift_in(target_ref, next_ref, incoming_ref, window)
        top = jnp.max(shifted, -1, keepdims=True)
        top_ref[...] = top
        sum_ref[...] = jnp.sum(jnp.exp(shifted - top), -1, keepdims=True)

    per = block // 8
    return pl.pallas_call(
        body,
        grid=(rows // block,),
        in_specs=[
            row_spec(block, cols),
            pl.BlockSpec((8, cols), lambda i: (jnp.minimum((i + 1) * per, rows // 8 - 1), 0)),
            whole_spec(8, cols),
        ],
        out_specs=[row_spec(block, 1)] * 2,
        out_shape=[jax.ShapeDtypeStruct((rows, 1), F32)] * 2,
        scratch_shapes=[pltpu.VMEM((block + 8, cols), F32)],
        compiler_params=params(50),
        cost_estimate=cost(4 * rows * cols, 4 * rows * cols, rows * cols),
        name="target_sums",
    )(target, target, incoming)


def target_pass(target, incoming):
    rows, cols = target.shape
    block = min(BLOCK, rows)

    def body(target_ref, next_ref, incoming_ref, prob_ref, entropy_ref, window):
        shifted = shift_in(target_ref, next_ref, incoming_ref, window)
        first = lax.axis_index("grp") * rows + pl.program_id(0) * block
        count = lax.axis_size("grp") * rows
        row = first + lax.broadcasted_iota(jnp.int32, (block, 1), 0)
        live = jnp.where(row < count - HEAD, 1.0, 0.0)
        below = shifted - jnp.max(shifted, -1, keepdims=True)
        raised = jnp.exp(below)
        total = jnp.sum(raised, -1, keepdims=True)
        scale = live / total
        prob_ref[...] = raised * scale
        entropy_ref[...] = scale * jnp.sum(raised * below, -1, keepdims=True) - live * jnp.log(total)

    per = block // 8
    return pl.pallas_call(
        body,
        grid=(rows // block,),
        in_specs=[
            row_spec(block, cols),
            pl.BlockSpec((8, cols), lambda i: (jnp.minimum((i + 1) * per, rows // 8 - 1), 0)),
            whole_spec(8, cols),
        ],
        out_specs=[row_spec(block, cols), row_spec(block, 1)],
        out_shape=[
            jax.ShapeDtypeStruct((rows, cols), F32),
            jax.ShapeDtypeStruct((rows, 1), F32),
        ],
        scratch_shapes=[pltpu.VMEM((block + 8, cols), F32)],
        compiler_params=params(50),
        cost_estimate=cost(6 * rows * cols, 8 * rows * cols, rows * cols),
        name="target_pass",
    )(target, target, incoming)


def target_probs(target, incoming, top, total):
    rows, cols = target.shape
    block = min(BLOCK, rows)

    def body(target_ref, next_ref, incoming_ref, top_ref, sum_ref, prob_ref, entropy_ref, window):
        shifted = shift_in(target_ref, next_ref, incoming_ref, window)
        first = lax.axis_index("grp") * rows + pl.program_id(0) * block
        count = lax.axis_size("grp") * rows
        row = first + lax.broadcasted_iota(jnp.int32, (block, 1), 0)
        live = jnp.where(row < count - HEAD, 1.0, 0.0)
        log_target = shifted - (top_ref[...] + jnp.log(sum_ref[...]))
        prob = jnp.exp(log_target) * live
        prob_ref[...] = prob
        entropy_ref[...] = jnp.sum(prob * log_target, -1, keepdims=True)

    per = block // 8
    return pl.pallas_call(
        body,
        grid=(rows // block,),
        in_specs=[
            row_spec(block, cols),
            pl.BlockSpec((8, cols), lambda i: (jnp.minimum((i + 1) * per, rows // 8 - 1), 0)),
            whole_spec(8, cols),
            row_spec(block, 1),
            row_spec(block, 1),
        ],
        out_specs=[row_spec(block, cols), row_spec(block, 1)],
        out_shape=[
            jax.ShapeDtypeStruct((rows, cols), F32),
            jax.ShapeDtypeStruct((rows, 1), F32),
        ],
        scratch_shapes=[pltpu.VMEM((block + 8, cols), F32)],
        compiler_params=params(50),
        cost_estimate=cost(6 * rows * cols, 8 * rows * cols, rows * cols),
        name="target_probs",
    )(target, target, incoming, top, total)


def draft_chunk(target, acts, pieces, column, sums):
    rows, rank = acts.shape
    half_rank, width = pieces[0].shape
    block = min(BLOCK, rows)

    def body(target_ref, acts_ref, own_ref, other_ref, *rest):
        draft_ref, proj_ref, top_ref, sum_ref = rest[-4:]

        @pl.when(pl.program_id(0) == 0)
        def _():
            mine = lax.axis_index("grp") & 1
            proj_ref[pl.ds(pl.multiple_of(mine * half_rank, half_rank), half_rank), :] = own_ref[...]
            proj_ref[
                pl.ds(pl.multiple_of((1 - mine) * half_rank, half_rank), half_rank), :
            ] = other_ref[...]

        draft = target_ref[...] + jnp.dot(
            acts_ref[...], proj_ref[...], preferred_element_type=F32
        )
        draft_ref[...] = draft
        top = jnp.max(draft, -1, keepdims=True)
        if sums is not None:
            top = jnp.maximum(top, rest[0][...])
        total = jnp.sum(jnp.exp(draft - top), -1, keepdims=True)
        if sums is not None:
            total = total + rest[1][...] * jnp.exp(rest[0][...] - top)
        top_ref[...] = top
        sum_ref[...] = total

    carried = () if sums is None else tuple(sums)
    draft, proj, top, total = pl.pallas_call(
        body,
        grid=(rows // block,),
        in_specs=[
            row_spec(block, width, column),
            row_spec(block, rank),
            whole_spec(half_rank, width),
            whole_spec(half_rank, width),
        ]
        + [row_spec(block, 1)] * len(carried),
        out_specs=[
            row_spec(block, width),
            whole_spec(rank, width),
            row_spec(block, 1),
            row_spec(block, 1),
        ],
        out_shape=[
            jax.ShapeDtypeStruct((rows, width), F32),
            jax.ShapeDtypeStruct((rank, width), BF16),
            jax.ShapeDtypeStruct((rows, 1), F32),
            jax.ShapeDtypeStruct((rows, 1), F32),
        ],
        compiler_params=params(16),
        cost_estimate=cost(2 * rows * rank * width, 8 * rows * width, rows * width),
        name="draft_chunk",
    )(target, acts, *pieces, *carried)
    return draft, proj, (top, total)


def grad_chunk(draft, prob, label, acts, vocab_proj, column, sums, carried):
    rows, width = draft.shape
    rank = acts.shape[1]
    half_rank = rank // 2
    block = min(BLOCK, rows)

    def body(draft_ref, prob_ref, label_ref, acts_ref, proj_ref, top_ref, sum_ref, *rest):
        away_ref, kept_ref, act_ref, loss_ref, totals = rest[-5:]
        step = pl.program_id(0)
        first = lax.axis_index("grp") * rows + step * block
        count = lax.axis_size("grp") * rows
        row = first + lax.broadcasted_iota(jnp.int32, (block, 1), 0)
        live = jnp.where(row < count - HEAD, 1.0, 0.0)
        log_draft = draft_ref[...] - (top_ref[...] + jnp.log(sum_ref[...]))
        prob = prob_ref[...]
        place = lax.broadcasted_iota(jnp.int32, (block, width), 1) + column * width
        hit = jnp.where(place == label_ref[...], LAM, 0.0)
        loss = -jnp.sum((prob + hit) * log_draft, -1, keepdims=True)
        grad = ((live + LAM) * jnp.exp(log_draft) - prob - hit).astype(BF16)
        act = inner_cols(grad, proj_ref[...])
        if carried is not None:
            loss = loss + rest[1][...]
            act = act + rest[0][...]
        loss_ref[...] = loss
        act_ref[...] = act
        term = inner_rows(acts_ref[...], grad)

        @pl.when(step == 0)
        def _():
            totals[...] = term

        @pl.when(step > 0)
        def _():
            totals[...] += term

        @pl.when(step == pl.num_programs(0) - 1)
        def _():
            mine = lax.axis_index("grp") & 1
            away = totals[pl.ds(pl.multiple_of((1 - mine) * half_rank, half_rank), half_rank), :]
            away_ref[...] = away.astype(BF16)
            kept_ref[...] = totals[pl.ds(pl.multiple_of(mine * half_rank, half_rank), half_rank), :]

    extra = () if carried is None else tuple(carried)
    away, kept, act, loss = pl.pallas_call(
        body,
        grid=(rows // block,),
        in_specs=[
            row_spec(block, width),
            row_spec(block, width, column),
            row_spec(block, 1),
            row_spec(block, rank),
            whole_spec(rank, width),
            row_spec(block, 1),
            row_spec(block, 1),
        ]
        + ([row_spec(block, rank), row_spec(block, 1)] if extra else []),
        out_specs=[whole_spec(half_rank, width)] * 2 + [row_spec(block, rank), row_spec(block, 1)],
        out_shape=[
            jax.ShapeDtypeStruct((half_rank, width), BF16),
            jax.ShapeDtypeStruct((half_rank, width), F32),
            jax.ShapeDtypeStruct((rows, rank), F32),
            jax.ShapeDtypeStruct((rows, 1), F32),
        ],
        scratch_shapes=[pltpu.VMEM((rank, width), F32)],
        compiler_params=params(16),
        cost_estimate=cost(4 * rows * rank * width, 8 * rows * width, rows * width),
        name="grad_chunk",
    )(draft, prob, label, acts, vocab_proj, *sums, *extra)
    return (away, kept), (act, loss)


class Line:
    def __init__(self):
        self.mark = None

    def after(self, value):
        if self.mark is None:
            return value
        return lax.optimization_barrier((value, self.mark))[0]

    def put(self, value):
        self.mark = jax.tree.leaves(value)[0]
        return value


class Chain:
    def __init__(self, steps):
        self.steps = steps
        self.value = None

    def step(self, times=1):
        for _ in range(times):
            if self.steps is not None:
                try:
                    next(self.steps)
                except StopIteration as end:
                    self.value = end.value
                    self.steps = None

    def result(self):
        while self.steps is not None:
            self.step()
        return self.value


def sent_over(line, value, axis, bit):
    value = line.put(line.after(value))
    arrived = swap(value, axis, bit)
    yield
    return line.after(arrived)


def reduce_steps(line, pair, axis, bits, wires, alike):
    away, part = pair
    for index, (bit, wire) in enumerate(zip(bits[:-1], wires)):
        mine = own_bit(axis, bit)
        if index > 0:
            away, part = half(part, 1 - mine), half(part, mine)
        arrived = yield from sent_over(line, away.astype(wire), axis, bit)
        part = part + arrived.astype(F32)
    sent = part.astype(wires[-1])
    arrived = yield from sent_over(line, sent, axis, bits[-1])
    return (sent.astype(F32) if alike else part) + arrived.astype(F32)


def joined(axis, bit, own, other):
    mine = own_bit(axis, bit)
    low = jnp.where(mine == 0, own, other)
    high = jnp.where(mine == 0, other, own)
    return jnp.concatenate((low, high), 0)


def gather_steps(line, piece, axis, bits):
    for bit in reversed(bits[1:-1]):
        other = yield from sent_over(line, piece, axis, bit)
        piece = joined(axis, bit, piece, other)
    return piece


def split_pair(part, axis, bits):
    mine = own_bit(axis, bits[0])
    return half(part, 1 - mine), half(part, mine)


def summed(line, pair, axis, bits, wires, between, pieces, alike=False):
    def steps():
        total = yield from reduce_steps(line, pair, axis, bits, wires, alike)
        own = yield from gather_steps(line, between(total), axis, bits)
        pieces.append(own)
        other = yield from sent_over(line, own, axis, bits[0])
        pieces.append(other)

    return Chain(steps())


def first_of(chain, pieces):
    while not pieces:
        chain.step()
    return pieces[0]


def over_voc(line, part, bits, wires, between, alike=False):
    pieces = []
    chain = summed(line, split_pair(part, "voc", bits), "voc", bits, wires, between, pieces, alike)
    return chain, lambda: (chain.result(), joined("voc", bits[0], *pieces))[1]


def on_device(hidden_states, target_logits, labels, down_weight, up_weight, head_weight):
    row_count, slice_cols = target_logits.shape
    book_count = labels.shape[1]
    group_count = lax.axis_size("grp")
    per_book = lax.axis_size("voc") // book_count
    block_rows = row_count // per_book
    position = lax.axis_index("voc")
    book_index = position // per_book
    book_part = position % per_book
    width = slice_cols // CHUNKS
    chunks = range(CHUNKS)
    z_bits = list(range(group_count.bit_length() - 1))
    v_bits = list(range(lax.axis_size("voc").bit_length() - 1))
    v_other = v_bits[:1] + v_bits[:0:-1]
    line = Line()

    def columns(c):
        return head_weight[:, c * width : (c + 1) * width]

    mine = own_bit("grp", z_bits[0])
    up_away, up_kept = half(up_weight, 1 - mine), half(up_weight, mine)
    vocab_pieces = [[] for c in chunks]
    vocab = []
    for c in chunks:
        away, kept = [
            jnp.dot(part, columns(c), preferred_element_type=F32) * VOCAB_SCALE
            for part in (up_away, up_kept)
        ]
        vocab.append(
            summed(
                line, (away, kept), "grp", z_bits, [F16] * len(z_bits),
                lambda total: (total * (1.0 / VOCAB_SCALE)).astype(BF16), vocab_pieces[c],
            )
        )
    vocab[0].step()
    devices = range(group_count)
    top_rows = line.put(line.after(target_logits[:8]))
    incoming = lax.ppermute(top_rows, "grp", [(i + 1, i) for i in devices if i + 1 in devices])
    vocab[1].step()
    pre_part = line.put(
        jnp.dot(line.after(hidden_states), down_weight, preferred_element_type=F32)
    )
    kept_pre = []

    def activate(total):
        kept_pre.append(total * (1.0 / PRE_SCALE))
        return jax.nn.silu(kept_pre[0]).astype(BF16)

    pre, all_acts = over_voc(
        line, pre_part * PRE_SCALE, v_bits, [F16] * len(v_bits), activate
    )
    pre.step()
    incoming = line.put(line.after(incoming))
    vocab[0].step()
    pre.step()
    vocab[1].step()
    pre.step()
    vocab[0].step()
    if per_book == 1:
        prob, entropy = target_pass(target_logits, line.after(incoming))
    else:
        top, total = target_sums(target_logits, incoming)
        top, total = over_books((top, total), merge_sums, per_book)
        prob, entropy = target_probs(target_logits, incoming, top, total)
    line.put(entropy)
    label = lax.dynamic_slice_in_dim(labels, book_index, 1, 1) - book_part * slice_cols
    pre.step()
    vocab[0].result()
    line.put(vocab_pieces[0][1])
    vocab[1].step()
    pre.step()
    acts = line.put(all_acts())

    drafts, vocab_proj, sums = [], [], None
    for c in chunks:
        vocab[c].result()
        pieces = vocab_pieces[c]
        line.put(pieces[1])
        draft, proj, sums = draft_chunk(target_logits, acts, pieces, c, sums)
        drafts.append(line.put(draft))
        vocab_proj.append(proj)
    sums = over_books(tuple(sums), merge_sums, per_book)

    grads, carried, grad_pieces = [], None, [[] for c in chunks]
    for c in chunks:
        pair, carried = grad_chunk(
            line.after(drafts[c]), prob, label, acts, vocab_proj[c], c, sums, carried
        )
        line.put(pair)
        grads.append(
            summed(
                line, pair, "grp", z_bits, [BF16] * len(z_bits),
                lambda total: total.astype(BF16), grad_pieces[c],
            )
        )
        grads[c].step()
    act_part, loss = carried
    act, all_pre_grad = over_voc(
        line, act_part, v_bits, [F32] + [BF16] * len(v_bits),
        lambda total: (total * silu_slope(kept_pre[0])).astype(BF16),
    )
    grads[0].step()
    act.step()
    act.step()
    grads[1].step()
    act.step()
    loss = over_books(loss + entropy, jnp.add, per_book)
    frame_loss = lax.dynamic_slice_in_dim(loss, book_part * block_rows, block_rows, 0)
    frame_loss = frame_loss.reshape(1, 1, block_rows)

    def times_head(before, piece, c):
        return line.put(before + inner_cols(line.after(piece), columns(c)))

    own_up = times_head(0.0, first_of(grads[0], grad_pieces[0]), 0)
    act.step()
    own = first_of(grads[1], grad_pieces[1])
    act.step()
    grads[0].result()
    other_up = times_head(0.0, grad_pieces[0][1], 0)
    pre_grad = line.put(all_pre_grad())
    down_part = line.put(inner_rows(line.after(hidden_states), pre_grad))
    rows = down_part.shape[0] // 2
    down_pieces = [[], []]
    downs = [
        summed(
            line, split_pair(part, "grp", z_bits), "grp", z_bits, [BF16] * len(z_bits),
            lambda total: total.astype(BF16), down_pieces[i], True,
        )
        for i, part in enumerate((down_part[:rows], down_part[rows:]))
    ]
    downs[0].step()
    downs[1].step()
    own_up = times_head(own_up, own, 1)
    grads[1].result()
    other_up = times_head(other_up, grad_pieces[1][1], 1)
    up_part = joined("grp", z_bits[0], own_up, other_up)
    rank = up_part.shape[0] // 2
    ups = [
        over_voc(
            line, part, bits, [F32] + [BF16] * len(v_bits), lambda total: total.astype(BF16), True
        )
        for part, bits in ((up_part[:rank], v_bits), (up_part[rank:], v_other))
    ]
    for _ in range(2 * len(v_bits)):
        for chain in (ups[0][0], ups[1][0], downs[0], downs[1]):
            chain.step()
    grad_b = jnp.concatenate([result().astype(F32) for _, result in ups], 0)
    for chain in downs:
        chain.result()
    grad_a = jnp.concatenate(
        [joined("grp", z_bits[0], *pieces).astype(F32) for pieces in down_pieces], 0
    )
    return frame_loss, grad_a, grad_b


def solution(mesh):
    in_specs = (
        P("grp", "voc"),
        P("grp", "voc"),
        P("grp", None),
        P("voc", None),
        P(None, "grp"),
        P("grp", "voc"),
    )
    out_specs = (P("voc", "grp", None), P("voc", None), P(None, "grp"))
    return jax.shard_map(
        on_device, mesh=mesh, in_specs=in_specs, out_specs=out_specs, check_vma=False
    )
```

```python
import jax
import jax.numpy as jnp
from jax import lax
from jax.experimental import pallas as pl
from jax.experimental.pallas import tpu as pltpu
from jax.sharding import PartitionSpec as P

HEAD = 2
LAM = 0.1
CHUNKS = 2
BLOCK = 256
VOCAB_SCALE = 128.0
PRE_SCALE = 64.0
F32 = jnp.float32
BF16 = jnp.bfloat16
F16 = jnp.float16


def swap(value, axis, bit):
    mask = 1 << bit
    pairs = [(i, i ^ mask) for i in range(lax.axis_size(axis))]
    return lax.ppermute(value, axis, pairs)


def own_bit(axis, bit):
    return (lax.axis_index(axis) >> bit) & 1


def half(value, which):
    rows = value.shape[0] // 2
    return lax.dynamic_slice_in_dim(value, which * rows, rows, 0)


def silu_slope(values):
    sigma = jax.nn.sigmoid(values)
    return sigma * (1.0 + values * (1.0 - sigma))


def inner_rows(left, right):
    return lax.dot_general(left, right, (((0,), (0,)), ((), ())), preferred_element_type=F32)


def inner_cols(left, right):
    return lax.dot_general(left, right, (((1,), (1,)), ((), ())), preferred_element_type=F32)


def over_books(values, combine, per_book):
    bit = 0
    while (1 << bit) < per_book:
        values = combine(values, jax.tree.map(lambda v: swap(v, "voc", bit), values))
        bit += 1
    return values


def merge_sums(a, b):
    top = jnp.maximum(a[0], b[0])
    return top, a[1] * jnp.exp(a[0] - top) + b[1] * jnp.exp(b[0] - top)


def params(megabytes):
    return pltpu.CompilerParams(
        dimension_semantics=("arbitrary",), vmem_limit_bytes=megabytes << 20
    )


def cost(flops, read, exps):
    return pl.CostEstimate(flops=flops // 4096, bytes_accessed=read // 4096, transcendentals=0)


def row_spec(block, cols, column=0):
    return pl.BlockSpec((block, cols), lambda i: (i, column))


def whole_spec(rows, cols):
    return pl.BlockSpec((rows, cols), lambda i: (0, 0))


def shift_in(target_ref, next_ref, incoming_ref, window):
    block = target_ref.shape[0]
    last = pl.program_id(0) == pl.num_programs(0) - 1
    window[:block, :] = target_ref[...]
    window[block:, :] = jnp.where(last, incoming_ref[...], next_ref[...])
    return window[HEAD : HEAD + block, :]


def target_sums(target, incoming):
    rows, cols = target.shape
    block = min(BLOCK, rows)

    def body(target_ref, next_ref, incoming_ref, top_ref, sum_ref, window):
        shifted = shift_in(target_ref, next_ref, incoming_ref, window)
        top = jnp.max(shifted, -1, keepdims=True)
        top_ref[...] = top
        sum_ref[...] = jnp.sum(jnp.exp(shifted - top), -1, keepdims=True)

    per = block // 8
    return pl.pallas_call(
        body,
        grid=(rows // block,),
        in_specs=[
            row_spec(block, cols),
            pl.BlockSpec((8, cols), lambda i: (jnp.minimum((i + 1) * per, rows // 8 - 1), 0)),
            whole_spec(8, cols),
        ],
        out_specs=[row_spec(block, 1)] * 2,
        out_shape=[jax.ShapeDtypeStruct((rows, 1), F32)] * 2,
        scratch_shapes=[pltpu.VMEM((block + 8, cols), F32)],
        compiler_params=params(24),
        cost_estimate=cost(4 * rows * cols, 4 * rows * cols, rows * cols),
        name="target_sums",
    )(target, target, incoming)


def target_pass(target, incoming):
    rows, cols = target.shape
    block = min(BLOCK, rows)

    def body(target_ref, next_ref, incoming_ref, prob_ref, entropy_ref, window):
        shifted = shift_in(target_ref, next_ref, incoming_ref, window)
        first = lax.axis_index("grp") * rows + pl.program_id(0) * block
        count = lax.axis_size("grp") * rows
        row = first + lax.broadcasted_iota(jnp.int32, (block, 1), 0)
        live = jnp.where(row < count - HEAD, 1.0, 0.0)
        below = shifted - jnp.max(shifted, -1, keepdims=True)
        raised = jnp.exp(below)
        total = jnp.sum(raised, -1, keepdims=True)
        scale = live / total
        prob_ref[...] = raised * scale
        entropy_ref[...] = scale * jnp.sum(raised * below, -1, keepdims=True) - live * jnp.log(total)

    per = block // 8
    return pl.pallas_call(
        body,
        grid=(rows // block,),
        in_specs=[
            row_spec(block, cols),
            pl.BlockSpec((8, cols), lambda i: (jnp.minimum((i + 1) * per, rows // 8 - 1), 0)),
            whole_spec(8, cols),
        ],
        out_specs=[row_spec(block, cols), row_spec(block, 1)],
        out_shape=[
            jax.ShapeDtypeStruct((rows, cols), F32),
            jax.ShapeDtypeStruct((rows, 1), F32),
        ],
        scratch_shapes=[pltpu.VMEM((block + 8, cols), F32)],
        compiler_params=params(24),
        cost_estimate=cost(6 * rows * cols, 8 * rows * cols, rows * cols),
        name="target_pass",
    )(target, target, incoming)


def target_probs(target, incoming, top, total):
    rows, cols = target.shape
    block = min(BLOCK, rows)

    def body(target_ref, next_ref, incoming_ref, top_ref, sum_ref, prob_ref, entropy_ref, window):
        shifted = shift_in(target_ref, next_ref, incoming_ref, window)
        first = lax.axis_index("grp") * rows + pl.program_id(0) * block
        count = lax.axis_size("grp") * rows
        row = first + lax.broadcasted_iota(jnp.int32, (block, 1), 0)
        live = jnp.where(row < count - HEAD, 1.0, 0.0)
        log_target = shifted - (top_ref[...] + jnp.log(sum_ref[...]))
        prob = jnp.exp(log_target) * live
        prob_ref[...] = prob
        entropy_ref[...] = jnp.sum(prob * log_target, -1, keepdims=True)

    per = block // 8
    return pl.pallas_call(
        body,
        grid=(rows // block,),
        in_specs=[
            row_spec(block, cols),
            pl.BlockSpec((8, cols), lambda i: (jnp.minimum((i + 1) * per, rows // 8 - 1), 0)),
            whole_spec(8, cols),
            row_spec(block, 1),
            row_spec(block, 1),
        ],
        out_specs=[row_spec(block, cols), row_spec(block, 1)],
        out_shape=[
            jax.ShapeDtypeStruct((rows, cols), F32),
            jax.ShapeDtypeStruct((rows, 1), F32),
        ],
        scratch_shapes=[pltpu.VMEM((block + 8, cols), F32)],
        compiler_params=params(24),
        cost_estimate=cost(6 * rows * cols, 8 * rows * cols, rows * cols),
        name="target_probs",
    )(target, target, incoming, top, total)


def draft_chunk(target, acts, pieces, column, sums):
    rows, rank = acts.shape
    half_rank, width = pieces[0].shape
    block = min(BLOCK, rows)

    def body(target_ref, acts_ref, own_ref, other_ref, *rest):
        draft_ref, proj_ref, top_ref, sum_ref = rest[-4:]

        @pl.when(pl.program_id(0) == 0)
        def _():
            mine = lax.axis_index("grp") & 1
            proj_ref[pl.ds(pl.multiple_of(mine * half_rank, half_rank), half_rank), :] = own_ref[...]
            proj_ref[
                pl.ds(pl.multiple_of((1 - mine) * half_rank, half_rank), half_rank), :
            ] = other_ref[...]

        draft = target_ref[...] + jnp.dot(
            acts_ref[...], proj_ref[...], preferred_element_type=F32
        )
        draft_ref[...] = draft
        top = jnp.max(draft, -1, keepdims=True)
        if sums is not None:
            top = jnp.maximum(top, rest[0][...])
        total = jnp.sum(jnp.exp(draft - top), -1, keepdims=True)
        if sums is not None:
            total = total + rest[1][...] * jnp.exp(rest[0][...] - top)
        top_ref[...] = top
        sum_ref[...] = total

    carried = () if sums is None else tuple(sums)
    draft, proj, top, total = pl.pallas_call(
        body,
        grid=(rows // block,),
        in_specs=[
            row_spec(block, width, column),
            row_spec(block, rank),
            whole_spec(half_rank, width),
            whole_spec(half_rank, width),
        ]
        + [row_spec(block, 1)] * len(carried),
        out_specs=[
            row_spec(block, width),
            whole_spec(rank, width),
            row_spec(block, 1),
            row_spec(block, 1),
        ],
        out_shape=[
            jax.ShapeDtypeStruct((rows, width), F32),
            jax.ShapeDtypeStruct((rank, width), BF16),
            jax.ShapeDtypeStruct((rows, 1), F32),
            jax.ShapeDtypeStruct((rows, 1), F32),
        ],
        compiler_params=params(16),
        cost_estimate=cost(2 * rows * rank * width, 8 * rows * width, rows * width),
        name="draft_chunk",
    )(target, acts, *pieces, *carried)
    return draft, proj, (top, total)


def grad_chunk(draft, prob, label, acts, vocab_proj, column, sums, carried):
    rows, width = draft.shape
    rank = acts.shape[1]
    half_rank = rank // 2
    block = min(BLOCK, rows)

    def body(draft_ref, prob_ref, label_ref, acts_ref, proj_ref, top_ref, sum_ref, *rest):
        away_ref, kept_ref, act_ref, loss_ref, totals = rest[-5:]
        step = pl.program_id(0)
        first = lax.axis_index("grp") * rows + step * block
        count = lax.axis_size("grp") * rows
        row = first + lax.broadcasted_iota(jnp.int32, (block, 1), 0)
        live = jnp.where(row < count - HEAD, 1.0, 0.0)
        log_draft = draft_ref[...] - (top_ref[...] + jnp.log(sum_ref[...]))
        prob = prob_ref[...]
        place = lax.broadcasted_iota(jnp.int32, (block, width), 1) + column * width
        hit = jnp.where(place == label_ref[...], LAM, 0.0)
        loss = -jnp.sum((prob + hit) * log_draft, -1, keepdims=True)
        grad = ((live + LAM) * jnp.exp(log_draft) - prob - hit).astype(BF16)
        act = inner_cols(grad, proj_ref[...])
        if carried is not None:
            loss = loss + rest[1][...]
            act = act + rest[0][...]
        loss_ref[...] = loss
        act_ref[...] = act
        term = inner_rows(acts_ref[...], grad)

        @pl.when(step == 0)
        def _():
            totals[...] = term

        @pl.when(step > 0)
        def _():
            totals[...] += term

        @pl.when(step == pl.num_programs(0) - 1)
        def _():
            mine = lax.axis_index("grp") & 1
            away = totals[pl.ds(pl.multiple_of((1 - mine) * half_rank, half_rank), half_rank), :]
            away_ref[...] = away.astype(BF16)
            kept_ref[...] = totals[pl.ds(pl.multiple_of(mine * half_rank, half_rank), half_rank), :]

    extra = () if carried is None else tuple(carried)
    away, kept, act, loss = pl.pallas_call(
        body,
        grid=(rows // block,),
        in_specs=[
            row_spec(block, width),
            row_spec(block, width, column),
            row_spec(block, 1),
            row_spec(block, rank),
            whole_spec(rank, width),
            row_spec(block, 1),
            row_spec(block, 1),
        ]
        + ([row_spec(block, rank), row_spec(block, 1)] if extra else []),
        out_specs=[whole_spec(half_rank, width)] * 2 + [row_spec(block, rank), row_spec(block, 1)],
        out_shape=[
            jax.ShapeDtypeStruct((half_rank, width), BF16),
            jax.ShapeDtypeStruct((half_rank, width), F32),
            jax.ShapeDtypeStruct((rows, rank), F32),
            jax.ShapeDtypeStruct((rows, 1), F32),
        ],
        scratch_shapes=[pltpu.VMEM((rank, width), F32)],
        compiler_params=params(16),
        cost_estimate=cost(4 * rows * rank * width, 8 * rows * width, rows * width),
        name="grad_chunk",
    )(draft, prob, label, acts, vocab_proj, *sums, *extra)
    return (away, kept), (act, loss)


class Line:
    def __init__(self):
        self.mark = None

    def after(self, value):
        if self.mark is None:
            return value
        return lax.optimization_barrier((value, self.mark))[0]

    def put(self, value):
        self.mark = jax.tree.leaves(value)[0]
        return value


class Chain:
    def __init__(self, steps):
        self.steps = steps
        self.value = None

    def step(self, times=1):
        for _ in range(times):
            if self.steps is not None:
                try:
                    next(self.steps)
                except StopIteration as end:
                    self.value = end.value
                    self.steps = None

    def result(self):
        while self.steps is not None:
            self.step()
        return self.value


def sent_over(line, value, axis, bit):
    value = line.put(line.after(value))
    arrived = swap(value, axis, bit)
    yield
    return line.after(arrived)


def reduce_steps(line, pair, axis, bits, wires, alike):
    away, part = pair
    for index, (bit, wire) in enumerate(zip(bits[:-1], wires)):
        mine = own_bit(axis, bit)
        if index > 0:
            away, part = half(part, 1 - mine), half(part, mine)
        arrived = yield from sent_over(line, away.astype(wire), axis, bit)
        part = part + arrived.astype(F32)
    sent = part.astype(wires[-1])
    arrived = yield from sent_over(line, sent, axis, bits[-1])
    return (sent.astype(F32) if alike else part) + arrived.astype(F32)


def joined(axis, bit, own, other):
    mine = own_bit(axis, bit)
    low = jnp.where(mine == 0, own, other)
    high = jnp.where(mine == 0, other, own)
    return jnp.concatenate((low, high), 0)


def gather_steps(line, piece, axis, bits):
    for bit in reversed(bits[1:-1]):
        other = yield from sent_over(line, piece, axis, bit)
        piece = joined(axis, bit, piece, other)
    return piece


def split_pair(part, axis, bits):
    mine = own_bit(axis, bits[0])
    return half(part, 1 - mine), half(part, mine)


def summed(line, pair, axis, bits, wires, between, pieces, alike=False):
    def steps():
        total = yield from reduce_steps(line, pair, axis, bits, wires, alike)
        own = yield from gather_steps(line, between(total), axis, bits)
        pieces.append(own)
        other = yield from sent_over(line, own, axis, bits[0])
        pieces.append(other)

    return Chain(steps())


def first_of(chain, pieces):
    while not pieces:
        chain.step()
    return pieces[0]


def over_voc(line, part, bits, wires, between, alike=False):
    pieces = []
    chain = summed(line, split_pair(part, "voc", bits), "voc", bits, wires, between, pieces, alike)
    return chain, lambda: (chain.result(), joined("voc", bits[0], *pieces))[1]


def on_device(hidden_states, target_logits, labels, down_weight, up_weight, head_weight):
    row_count, slice_cols = target_logits.shape
    book_count = labels.shape[1]
    group_count = lax.axis_size("grp")
    per_book = lax.axis_size("voc") // book_count
    block_rows = row_count // per_book
    position = lax.axis_index("voc")
    book_index = position // per_book
    book_part = position % per_book
    width = slice_cols // CHUNKS
    chunks = range(CHUNKS)
    z_bits = list(range(group_count.bit_length() - 1))
    v_bits = list(range(lax.axis_size("voc").bit_length() - 1))
    v_other = v_bits[:1] + v_bits[:0:-1]
    line = Line()

    def columns(c):
        return head_weight[:, c * width : (c + 1) * width]

    mine = own_bit("grp", z_bits[0])
    up_away, up_kept = half(up_weight, 1 - mine), half(up_weight, mine)
    vocab_pieces = [[] for c in chunks]
    vocab, sent = [], []
    for c in chunks:
        away, kept = [
            jnp.dot(part, columns(c), preferred_element_type=F32) * VOCAB_SCALE
            for part in (up_away, up_kept)
        ]
        sent.append(away.astype(F16))
        vocab.append(
            summed(
                line, (sent[c], kept), "grp", z_bits, [F16] * len(z_bits),
                lambda total: (total * (1.0 / VOCAB_SCALE)).astype(BF16), vocab_pieces[c],
            )
        )
    vocab[0].step()
    devices = range(group_count)
    top_rows = line.put(line.after(target_logits[:8]))
    incoming = lax.ppermute(top_rows, "grp", [(i + 1, i) for i in devices if i + 1 in devices])
    pre_part = line.put(
        jnp.dot(line.after(hidden_states), down_weight, preferred_element_type=F32)
    )
    kept_pre = []

    def activate(total):
        kept_pre.append(total * (1.0 / PRE_SCALE))
        return jax.nn.silu(kept_pre[0]).astype(BF16)

    pre, all_acts = over_voc(
        line, pre_part * PRE_SCALE, v_bits, [F16] * len(v_bits), activate
    )
    pre.step()
    line.put(sent[1])
    incoming = line.put(line.after(incoming))
    vocab[0].step()
    vocab[1].step()
    pre.step()
    vocab[1].step()
    pre.step()
    vocab[0].step()
    if per_book == 1:
        prob, entropy = target_pass(target_logits, line.after(incoming))
    else:
        top, total = target_sums(target_logits, incoming)
        top, total = over_books((top, total), merge_sums, per_book)
        prob, entropy = target_probs(target_logits, incoming, top, total)
    line.put(entropy)
    label = lax.dynamic_slice_in_dim(labels, book_index, 1, 1) - book_part * slice_cols
    pre.step()
    vocab[1].step()
    vocab[0].result()
    line.put(vocab_pieces[0][1])
    pre.step()
    acts = line.put(all_acts())

    drafts, vocab_proj, sums = [], [], None
    for c in chunks:
        vocab[c].result()
        pieces = vocab_pieces[c]
        line.put(pieces[1])
        draft, proj, sums = draft_chunk(target_logits, acts, pieces, c, sums)
        drafts.append(line.put(draft))
        vocab_proj.append(proj)
    sums = over_books(tuple(sums), merge_sums, per_book)

    grads, carried, grad_pieces = [], None, [[] for c in chunks]
    for c in chunks:
        pair, carried = grad_chunk(
            line.after(drafts[c]), prob, label, acts, vocab_proj[c], c, sums, carried
        )
        line.put(pair)
        grads.append(
            summed(
                line, pair, "grp", z_bits, [BF16] * len(z_bits),
                lambda total: total.astype(BF16), grad_pieces[c],
            )
        )
        grads[c].step()
    act_part, loss = carried
    act, all_pre_grad = over_voc(
        line, act_part, v_bits, [F32] + [BF16] * len(v_bits),
        lambda total: (total * silu_slope(kept_pre[0])).astype(BF16),
    )
    grads[0].step()
    act.step()
    act.step()
    grads[1].step()
    act.step()
    def times_head(before, piece, c):
        return line.put(before + inner_cols(line.after(piece), columns(c)))

    own_up = times_head(0.0, first_of(grads[0], grad_pieces[0]), 0)
    act.step()
    own = first_of(grads[1], grad_pieces[1])
    act.step()
    grads[0].result()
    other_up = times_head(0.0, grad_pieces[0][1], 0)
    pre_grad = line.put(all_pre_grad())
    down_part = line.put(inner_rows(line.after(hidden_states), pre_grad))
    rows = down_part.shape[0] // 2
    down_pieces = [[], []]
    downs = [
        summed(
            line, split_pair(part, "grp", z_bits), "grp", z_bits, [BF16] * len(z_bits),
            lambda total: total.astype(BF16), down_pieces[i], True,
        )
        for i, part in enumerate((down_part[:rows], down_part[rows:]))
    ]
    downs[0].step()
    downs[1].step()
    own_up = times_head(own_up, own, 1)
    grads[1].result()
    other_up = times_head(other_up, grad_pieces[1][1], 1)
    up_part = joined("grp", z_bits[0], own_up, other_up)
    rank = up_part.shape[0] // 2
    ups = [
        over_voc(
            line, part, bits, [F32] + [BF16] * len(v_bits), lambda total: total.astype(BF16), True
        )
        for part, bits in ((up_part[:rank], v_bits), (up_part[rank:], v_other))
    ]
    swaps = [chain for chain, _ in ups]
    loss = over_books(line.after(loss) + entropy, jnp.add, per_book)
    frame_loss = lax.dynamic_slice_in_dim(loss, book_part * block_rows, block_rows, 0)
    frame_loss = frame_loss.reshape(1, 1, block_rows)
    for turn in (swaps, downs, swaps, swaps, swaps, downs, swaps):
        for chain in turn:
            chain.step()
    grad_b = jnp.concatenate([result().astype(F32) for _, result in ups], 0)
    for chain in downs:
        chain.result()
    grad_a = jnp.concatenate(
        [joined("grp", z_bits[0], *pieces).astype(F32) for pieces in down_pieces], 0
    )
    return frame_loss, grad_a, grad_b


def solution(mesh):
    in_specs = (
        P("grp", "voc"),
        P("grp", "voc"),
        P("grp", None),
        P("voc", None),
        P(None, "grp"),
        P("grp", "voc"),
    )
    out_specs = (P("voc", "grp", None), P("voc", None), P(None, "grp"))
    return jax.shard_map(
        on_device, mesh=mesh, in_specs=in_specs, out_specs=out_specs, check_vma=False
    )
```

```python
import jax
import jax.numpy as jnp
from jax import lax
from jax.experimental import pallas as pl
from jax.experimental.pallas import tpu as pltpu
from jax.sharding import PartitionSpec as P

HEAD = 2
LAM = 0.1
CHUNKS = 2
BLOCK = 256
VOCAB_SCALE = 128.0
PRE_SCALE = 64.0
F32 = jnp.float32
BF16 = jnp.bfloat16
F16 = jnp.float16


def swap(value, axis, bit):
    mask = 1 << bit
    pairs = [(i, i ^ mask) for i in range(lax.axis_size(axis))]
    return lax.ppermute(value, axis, pairs)


def own_bit(axis, bit):
    return (lax.axis_index(axis) >> bit) & 1


def half(value, which):
    rows = value.shape[0] // 2
    return lax.dynamic_slice_in_dim(value, which * rows, rows, 0)


def silu_slope(values):
    sigma = jax.nn.sigmoid(values)
    return sigma * (1.0 + values * (1.0 - sigma))


def inner_rows(left, right):
    return lax.dot_general(left, right, (((0,), (0,)), ((), ())), preferred_element_type=F32)


def inner_cols(left, right):
    return lax.dot_general(left, right, (((1,), (1,)), ((), ())), preferred_element_type=F32)


def over_books(values, combine, per_book):
    bit = 0
    while (1 << bit) < per_book:
        values = combine(values, jax.tree.map(lambda v: swap(v, "voc", bit), values))
        bit += 1
    return values


def merge_sums(a, b):
    top = jnp.maximum(a[0], b[0])
    return top, a[1] * jnp.exp(a[0] - top) + b[1] * jnp.exp(b[0] - top)


def params(megabytes):
    return pltpu.CompilerParams(
        dimension_semantics=("arbitrary",), vmem_limit_bytes=megabytes << 20
    )


def cost(flops, read, exps):
    return pl.CostEstimate(flops=flops // 4096, bytes_accessed=read // 4096, transcendentals=0)


def row_spec(block, cols, column=0):
    return pl.BlockSpec((block, cols), lambda i: (i, column))


def whole_spec(rows, cols):
    return pl.BlockSpec((rows, cols), lambda i: (0, 0))


def shift_in(target_ref, next_ref, incoming_ref, window):
    block = target_ref.shape[0]
    last = pl.program_id(0) == pl.num_programs(0) - 1
    window[:block, :] = target_ref[...]
    window[block:, :] = jnp.where(last, incoming_ref[...], next_ref[...])
    return window[HEAD : HEAD + block, :]


def target_sums(target, incoming):
    rows, cols = target.shape
    block = min(BLOCK, rows)

    def body(target_ref, next_ref, incoming_ref, top_ref, sum_ref, window):
        shifted = shift_in(target_ref, next_ref, incoming_ref, window)
        top = jnp.max(shifted, -1, keepdims=True)
        top_ref[...] = top
        sum_ref[...] = jnp.sum(jnp.exp(shifted - top), -1, keepdims=True)

    per = block // 8
    return pl.pallas_call(
        body,
        grid=(rows // block,),
        in_specs=[
            row_spec(block, cols),
            pl.BlockSpec((8, cols), lambda i: (jnp.minimum((i + 1) * per, rows // 8 - 1), 0)),
            whole_spec(8, cols),
        ],
        out_specs=[row_spec(block, 1)] * 2,
        out_shape=[jax.ShapeDtypeStruct((rows, 1), F32)] * 2,
        scratch_shapes=[pltpu.VMEM((block + 8, cols), F32)],
        compiler_params=params(24),
        cost_estimate=cost(4 * rows * cols, 4 * rows * cols, rows * cols),
        name="target_sums",
    )(target, target, incoming)


def target_pass(target, incoming):
    rows, cols = target.shape
    block = min(BLOCK, rows)

    def body(target_ref, next_ref, incoming_ref, prob_ref, entropy_ref, window):
        shifted = shift_in(target_ref, next_ref, incoming_ref, window)
        first = lax.axis_index("grp") * rows + pl.program_id(0) * block
        count = lax.axis_size("grp") * rows
        row = first + lax.broadcasted_iota(jnp.int32, (block, 1), 0)
        live = jnp.where(row < count - HEAD, 1.0, 0.0)
        below = shifted - jnp.max(shifted, -1, keepdims=True)
        raised = jnp.exp(below)
        total = jnp.sum(raised, -1, keepdims=True)
        scale = live / total
        prob_ref[...] = raised * scale
        entropy_ref[...] = scale * jnp.sum(raised * below, -1, keepdims=True) - live * jnp.log(total)

    per = block // 8
    return pl.pallas_call(
        body,
        grid=(rows // block,),
        in_specs=[
            row_spec(block, cols),
            pl.BlockSpec((8, cols), lambda i: (jnp.minimum((i + 1) * per, rows // 8 - 1), 0)),
            whole_spec(8, cols),
        ],
        out_specs=[row_spec(block, cols), row_spec(block, 1)],
        out_shape=[
            jax.ShapeDtypeStruct((rows, cols), F32),
            jax.ShapeDtypeStruct((rows, 1), F32),
        ],
        scratch_shapes=[pltpu.VMEM((block + 8, cols), F32)],
        compiler_params=params(24),
        cost_estimate=cost(6 * rows * cols, 8 * rows * cols, rows * cols),
        name="target_pass",
    )(target, target, incoming)


def target_probs(target, incoming, top, total):
    rows, cols = target.shape
    block = min(BLOCK, rows)

    def body(target_ref, next_ref, incoming_ref, top_ref, sum_ref, prob_ref, entropy_ref, window):
        shifted = shift_in(target_ref, next_ref, incoming_ref, window)
        first = lax.axis_index("grp") * rows + pl.program_id(0) * block
        count = lax.axis_size("grp") * rows
        row = first + lax.broadcasted_iota(jnp.int32, (block, 1), 0)
        live = jnp.where(row < count - HEAD, 1.0, 0.0)
        log_target = shifted - (top_ref[...] + jnp.log(sum_ref[...]))
        prob = jnp.exp(log_target) * live
        prob_ref[...] = prob
        entropy_ref[...] = jnp.sum(prob * log_target, -1, keepdims=True)

    per = block // 8
    return pl.pallas_call(
        body,
        grid=(rows // block,),
        in_specs=[
            row_spec(block, cols),
            pl.BlockSpec((8, cols), lambda i: (jnp.minimum((i + 1) * per, rows // 8 - 1), 0)),
            whole_spec(8, cols),
            row_spec(block, 1),
            row_spec(block, 1),
        ],
        out_specs=[row_spec(block, cols), row_spec(block, 1)],
        out_shape=[
            jax.ShapeDtypeStruct((rows, cols), F32),
            jax.ShapeDtypeStruct((rows, 1), F32),
        ],
        scratch_shapes=[pltpu.VMEM((block + 8, cols), F32)],
        compiler_params=params(24),
        cost_estimate=cost(6 * rows * cols, 8 * rows * cols, rows * cols),
        name="target_probs",
    )(target, target, incoming, top, total)


def draft_chunk(target, acts, pieces, column, sums):
    rows, rank = acts.shape
    half_rank, width = pieces[0].shape
    block = min(BLOCK, rows)

    def body(target_ref, acts_ref, own_ref, other_ref, *rest):
        draft_ref, proj_ref, top_ref, sum_ref = rest[-4:]

        @pl.when(pl.program_id(0) == 0)
        def _():
            mine = lax.axis_index("grp") & 1
            proj_ref[pl.ds(pl.multiple_of(mine * half_rank, half_rank), half_rank), :] = own_ref[...]
            proj_ref[
                pl.ds(pl.multiple_of((1 - mine) * half_rank, half_rank), half_rank), :
            ] = other_ref[...]

        draft = target_ref[...] + jnp.dot(
            acts_ref[...], proj_ref[...], preferred_element_type=F32
        )
        draft_ref[...] = draft
        top = jnp.max(draft, -1, keepdims=True)
        if sums is not None:
            top = jnp.maximum(top, rest[0][...])
        total = jnp.sum(jnp.exp(draft - top), -1, keepdims=True)
        if sums is not None:
            total = total + rest[1][...] * jnp.exp(rest[0][...] - top)
        top_ref[...] = top
        sum_ref[...] = total

    carried = () if sums is None else tuple(sums)
    draft, proj, top, total = pl.pallas_call(
        body,
        grid=(rows // block,),
        in_specs=[
            row_spec(block, width, column),
            row_spec(block, rank),
            whole_spec(half_rank, width),
            whole_spec(half_rank, width),
        ]
        + [row_spec(block, 1)] * len(carried),
        out_specs=[
            row_spec(block, width),
            whole_spec(rank, width),
            row_spec(block, 1),
            row_spec(block, 1),
        ],
        out_shape=[
            jax.ShapeDtypeStruct((rows, width), F32),
            jax.ShapeDtypeStruct((rank, width), BF16),
            jax.ShapeDtypeStruct((rows, 1), F32),
            jax.ShapeDtypeStruct((rows, 1), F32),
        ],
        compiler_params=params(16),
        cost_estimate=cost(2 * rows * rank * width, 8 * rows * width, rows * width),
        name="draft_chunk",
    )(target, acts, *pieces, *carried)
    return draft, proj, (top, total)


def grad_chunk(draft, prob, label, acts, vocab_proj, column, sums, carried):
    rows, width = draft.shape
    rank = acts.shape[1]
    half_rank = rank // 2
    block = min(BLOCK, rows)

    def body(draft_ref, prob_ref, label_ref, acts_ref, proj_ref, top_ref, sum_ref, *rest):
        away_ref, kept_ref, act_ref, loss_ref, totals = rest[-5:]
        step = pl.program_id(0)
        first = lax.axis_index("grp") * rows + step * block
        count = lax.axis_size("grp") * rows
        row = first + lax.broadcasted_iota(jnp.int32, (block, 1), 0)
        live = jnp.where(row < count - HEAD, 1.0, 0.0)
        log_draft = draft_ref[...] - (top_ref[...] + jnp.log(sum_ref[...]))
        prob = prob_ref[...]
        place = lax.broadcasted_iota(jnp.int32, (block, width), 1) + column * width
        hit = jnp.where(place == label_ref[...], LAM, 0.0)
        loss = -jnp.sum((prob + hit) * log_draft, -1, keepdims=True)
        grad = ((live + LAM) * jnp.exp(log_draft) - prob - hit).astype(BF16)
        act = inner_cols(grad, proj_ref[...])
        if carried is not None:
            loss = loss + rest[1][...]
            act = act + rest[0][...]
        loss_ref[...] = loss
        act_ref[...] = act
        term = inner_rows(acts_ref[...], grad)

        @pl.when(step == 0)
        def _():
            totals[...] = term

        @pl.when(step > 0)
        def _():
            totals[...] += term

        @pl.when(step == pl.num_programs(0) - 1)
        def _():
            mine = lax.axis_index("grp") & 1
            away = totals[pl.ds(pl.multiple_of((1 - mine) * half_rank, half_rank), half_rank), :]
            away_ref[...] = away.astype(BF16)
            kept_ref[...] = totals[pl.ds(pl.multiple_of(mine * half_rank, half_rank), half_rank), :]

    extra = () if carried is None else tuple(carried)
    away, kept, act, loss = pl.pallas_call(
        body,
        grid=(rows // block,),
        in_specs=[
            row_spec(block, width),
            row_spec(block, width, column),
            row_spec(block, 1),
            row_spec(block, rank),
            whole_spec(rank, width),
            row_spec(block, 1),
            row_spec(block, 1),
        ]
        + ([row_spec(block, rank), row_spec(block, 1)] if extra else []),
        out_specs=[whole_spec(half_rank, width)] * 2 + [row_spec(block, rank), row_spec(block, 1)],
        out_shape=[
            jax.ShapeDtypeStruct((half_rank, width), BF16),
            jax.ShapeDtypeStruct((half_rank, width), F32),
            jax.ShapeDtypeStruct((rows, rank), F32),
            jax.ShapeDtypeStruct((rows, 1), F32),
        ],
        scratch_shapes=[pltpu.VMEM((rank, width), F32)],
        compiler_params=params(16),
        cost_estimate=cost(4 * rows * rank * width, 8 * rows * width, rows * width),
        name="grad_chunk",
    )(draft, prob, label, acts, vocab_proj, *sums, *extra)
    return (away, kept), (act, loss)


class Line:
    def __init__(self):
        self.mark = None

    def after(self, value):
        if self.mark is None:
            return value
        return lax.optimization_barrier((value, self.mark))[0]

    def put(self, value):
        self.mark = jax.tree.leaves(value)[0]
        return value


class Chain:
    def __init__(self, steps):
        self.steps = steps
        self.value = None

    def step(self, times=1):
        for _ in range(times):
            if self.steps is not None:
                try:
                    next(self.steps)
                except StopIteration as end:
                    self.value = end.value
                    self.steps = None

    def result(self):
        while self.steps is not None:
            self.step()
        return self.value


def sent_over(line, value, axis, bit):
    value = line.put(line.after(value))
    arrived = swap(value, axis, bit)
    yield
    return line.after(arrived)


def reduce_steps(line, pair, axis, bits, wires, alike):
    away, part = pair
    for index, (bit, wire) in enumerate(zip(bits[:-1], wires)):
        mine = own_bit(axis, bit)
        if index > 0:
            away, part = half(part, 1 - mine), half(part, mine)
        arrived = yield from sent_over(line, away.astype(wire), axis, bit)
        part = part + arrived.astype(F32)
    sent = part.astype(wires[-1])
    arrived = yield from sent_over(line, sent, axis, bits[-1])
    return (sent.astype(F32) if alike else part) + arrived.astype(F32)


def joined(axis, bit, own, other):
    mine = own_bit(axis, bit)
    low = jnp.where(mine == 0, own, other)
    high = jnp.where(mine == 0, other, own)
    return jnp.concatenate((low, high), 0)


def gather_steps(line, piece, axis, bits):
    for bit in reversed(bits[1:-1]):
        other = yield from sent_over(line, piece, axis, bit)
        piece = joined(axis, bit, piece, other)
    return piece


def split_pair(part, axis, bits):
    mine = own_bit(axis, bits[0])
    return half(part, 1 - mine), half(part, mine)


def summed(line, pair, axis, bits, wires, between, pieces, alike=False):
    def steps():
        total = yield from reduce_steps(line, pair, axis, bits, wires, alike)
        own = yield from gather_steps(line, between(total), axis, bits)
        pieces.append(own)
        other = yield from sent_over(line, own, axis, bits[0])
        pieces.append(other)

    return Chain(steps())


def first_of(chain, pieces):
    while not pieces:
        chain.step()
    return pieces[0]


def over_voc(line, part, bits, wires, between, alike=False):
    pieces = []
    chain = summed(line, split_pair(part, "voc", bits), "voc", bits, wires, between, pieces, alike)
    return chain, lambda: (chain.result(), joined("voc", bits[0], *pieces))[1]


def on_device(hidden_states, target_logits, labels, down_weight, up_weight, head_weight):
    row_count, slice_cols = target_logits.shape
    book_count = labels.shape[1]
    group_count = lax.axis_size("grp")
    per_book = lax.axis_size("voc") // book_count
    block_rows = row_count // per_book
    position = lax.axis_index("voc")
    book_index = position // per_book
    book_part = position % per_book
    width = slice_cols // CHUNKS
    chunks = range(CHUNKS)
    z_bits = list(range(group_count.bit_length() - 1))
    v_bits = list(range(lax.axis_size("voc").bit_length() - 1))
    v_other = v_bits[:1] + v_bits[:0:-1]
    line = Line()

    def columns(c):
        return head_weight[:, c * width : (c + 1) * width]

    mine = own_bit("grp", z_bits[0])
    up_away, up_kept = half(up_weight, 1 - mine), half(up_weight, mine)
    vocab_pieces = [[] for c in chunks]
    vocab, sent = [], []
    for c in chunks:
        away, kept = [
            jnp.dot(part, columns(c), preferred_element_type=F32) * VOCAB_SCALE
            for part in (up_away, up_kept)
        ]
        sent.append(away.astype(F16))
        vocab.append(
            summed(
                line, (sent[c], kept), "grp", z_bits, [F16] * len(z_bits),
                lambda total: (total * (1.0 / VOCAB_SCALE)).astype(BF16), vocab_pieces[c],
            )
        )
    vocab[0].step()
    devices = range(group_count)
    top_rows = line.put(line.after(target_logits[:8]))
    incoming = lax.ppermute(top_rows, "grp", [(i + 1, i) for i in devices if i + 1 in devices])
    vocab[1].step()
    pre_part = line.put(
        jnp.dot(line.after(hidden_states), down_weight, preferred_element_type=F32)
    )
    kept_pre = []

    def activate(total):
        kept_pre.append(total * (1.0 / PRE_SCALE))
        return jax.nn.silu(kept_pre[0]).astype(BF16)

    pre, all_acts = over_voc(
        line, pre_part * PRE_SCALE, v_bits, [F16] * len(v_bits), activate
    )
    pre.step()
    incoming = line.put(line.after(incoming))
    vocab[0].step()
    pre.step()
    vocab[1].step()
    pre.step()
    vocab[0].step()
    pre.step()
    vocab[1].step()
    vocab[0].result()
    line.put(vocab_pieces[0][1])
    pre.step()
    acts = line.put(all_acts())
    if per_book == 1:
        prob, entropy = target_pass(line.after(target_logits), incoming)
    else:
        top, total = target_sums(target_logits, incoming)
        top, total = over_books((top, total), merge_sums, per_book)
        prob, entropy = target_probs(target_logits, incoming, top, total)
    line.put(entropy)
    acts = line.after(acts)
    label = lax.dynamic_slice_in_dim(labels, book_index, 1, 1) - book_part * slice_cols

    drafts, vocab_proj, sums = [], [], None
    for c in chunks:
        vocab[c].result()
        pieces = vocab_pieces[c]
        line.put(pieces[1])
        draft, proj, sums = draft_chunk(target_logits, acts, pieces, c, sums)
        drafts.append(line.put(draft))
        vocab_proj.append(proj)
    sums = over_books(tuple(sums), merge_sums, per_book)

    grads, carried, grad_pieces = [], None, [[] for c in chunks]
    for c in chunks:
        pair, carried = grad_chunk(
            line.after(drafts[c]), prob, label, acts, vocab_proj[c], c, sums, carried
        )
        line.put(pair)
        grads.append(
            summed(
                line, pair, "grp", z_bits, [BF16] * len(z_bits),
                lambda total: total.astype(BF16), grad_pieces[c],
            )
        )
        grads[c].step()
    act_part, loss = carried
    act, all_pre_grad = over_voc(
        line, act_part, v_bits, [F32] + [BF16] * len(v_bits),
        lambda total: (total * silu_slope(kept_pre[0])).astype(BF16),
    )
    grads[0].step()
    act.step()
    act.step()
    grads[1].step()
    act.step()
    def times_head(before, piece, c):
        return line.put(before + inner_cols(line.after(piece), columns(c)))

    own_up = times_head(0.0, first_of(grads[0], grad_pieces[0]), 0)
    act.step()
    own = first_of(grads[1], grad_pieces[1])
    act.step()
    grads[0].result()
    other_up = times_head(0.0, grad_pieces[0][1], 0)
    pre_grad = line.put(all_pre_grad())
    down_part = line.put(inner_rows(line.after(hidden_states), pre_grad))
    rows = down_part.shape[0] // 2
    down_pieces = [[], []]
    downs = [
        summed(
            line, split_pair(part, "grp", z_bits), "grp", z_bits, [BF16] * len(z_bits),
            lambda total: total.astype(BF16), down_pieces[i], True,
        )
        for i, part in enumerate((down_part[:rows], down_part[rows:]))
    ]
    downs[0].step()
    downs[1].step()
    own_up = times_head(own_up, own, 1)
    grads[1].result()
    other_up = times_head(other_up, grad_pieces[1][1], 1)
    up_part = joined("grp", z_bits[0], own_up, other_up)
    rank = up_part.shape[0] // 2
    ups = [
        over_voc(
            line, part, bits, [F32] + [BF16] * len(v_bits), lambda total: total.astype(BF16), True
        )
        for part, bits in ((up_part[:rank], v_bits), (up_part[rank:], v_other))
    ]
    swaps = [chain for chain, _ in ups]
    loss = over_books(line.after(loss) + entropy, jnp.add, per_book)
    frame_loss = lax.dynamic_slice_in_dim(loss, book_part * block_rows, block_rows, 0)
    frame_loss = frame_loss.reshape(1, 1, block_rows)
    for turn in (swaps, downs, swaps, swaps, swaps, downs, swaps):
        for chain in turn:
            chain.step()
    grad_b = jnp.concatenate([result().astype(F32) for _, result in ups], 0)
    for chain in downs:
        chain.result()
    grad_a = jnp.concatenate(
        [joined("grp", z_bits[0], *pieces).astype(F32) for pieces in down_pieces], 0
    )
    return frame_loss, grad_a, grad_b


def solution(mesh):
    in_specs = (
        P("grp", "voc"),
        P("grp", "voc"),
        P("grp", None),
        P("voc", None),
        P(None, "grp"),
        P("grp", "voc"),
    )
    out_specs = (P("voc", "grp", None), P("voc", None), P(None, "grp"))
    return jax.shard_map(
        on_device, mesh=mesh, in_specs=in_specs, out_specs=out_specs, check_vma=False
    )
```

```python
import jax
import jax.numpy as jnp
from jax import lax
from jax.experimental import pallas as pl
from jax.experimental.pallas import tpu as pltpu
from jax.sharding import PartitionSpec as P

HEAD = 2
LAM = 0.1
CHUNKS = 2
BLOCK = 256
VOCAB_SCALE = 128.0
PRE_SCALE = 64.0
F32 = jnp.float32
BF16 = jnp.bfloat16
F16 = jnp.float16


def swap(value, axis, bit):
    mask = 1 << bit
    pairs = [(i, i ^ mask) for i in range(lax.axis_size(axis))]
    return lax.ppermute(value, axis, pairs)


def own_bit(axis, bit):
    return (lax.axis_index(axis) >> bit) & 1


def half(value, which):
    rows = value.shape[0] // 2
    return lax.dynamic_slice_in_dim(value, which * rows, rows, 0)


def silu_slope(values):
    sigma = jax.nn.sigmoid(values)
    return sigma * (1.0 + values * (1.0 - sigma))


def inner_rows(left, right):
    return lax.dot_general(left, right, (((0,), (0,)), ((), ())), preferred_element_type=F32)


def inner_cols(left, right):
    return lax.dot_general(left, right, (((1,), (1,)), ((), ())), preferred_element_type=F32)


def over_books(values, combine, per_book):
    bit = 0
    while (1 << bit) < per_book:
        values = combine(values, jax.tree.map(lambda v: swap(v, "voc", bit), values))
        bit += 1
    return values


def merge_sums(a, b):
    top = jnp.maximum(a[0], b[0])
    return top, a[1] * jnp.exp(a[0] - top) + b[1] * jnp.exp(b[0] - top)


def params(megabytes):
    return pltpu.CompilerParams(
        dimension_semantics=("arbitrary",), vmem_limit_bytes=megabytes << 20
    )


def cost(flops, read, exps):
    return pl.CostEstimate(flops=flops // 4096, bytes_accessed=read // 4096, transcendentals=0)


def row_spec(block, cols, column=0):
    return pl.BlockSpec((block, cols), lambda i: (i, column))


def whole_spec(rows, cols):
    return pl.BlockSpec((rows, cols), lambda i: (0, 0))


def shift_in(target_ref, next_ref, incoming_ref, window):
    block = target_ref.shape[0]
    last = pl.program_id(0) == pl.num_programs(0) - 1
    window[:block, :] = target_ref[...]
    window[block:, :] = jnp.where(last, incoming_ref[...], next_ref[...])
    return window[HEAD : HEAD + block, :]


def target_sums(target, incoming):
    rows, cols = target.shape
    block = min(BLOCK, rows)

    def body(target_ref, next_ref, incoming_ref, top_ref, sum_ref, window):
        shifted = shift_in(target_ref, next_ref, incoming_ref, window)
        top = jnp.max(shifted, -1, keepdims=True)
        top_ref[...] = top
        sum_ref[...] = jnp.sum(jnp.exp(shifted - top), -1, keepdims=True)

    per = block // 8
    return pl.pallas_call(
        body,
        grid=(rows // block,),
        in_specs=[
            row_spec(block, cols),
            pl.BlockSpec((8, cols), lambda i: (jnp.minimum((i + 1) * per, rows // 8 - 1), 0)),
            whole_spec(8, cols),
        ],
        out_specs=[row_spec(block, 1)] * 2,
        out_shape=[jax.ShapeDtypeStruct((rows, 1), F32)] * 2,
        scratch_shapes=[pltpu.VMEM((block + 8, cols), F32)],
        compiler_params=params(24),
        cost_estimate=cost(4 * rows * cols, 4 * rows * cols, rows * cols),
        name="target_sums",
    )(target, target, incoming)


def target_pass(target, incoming):
    rows, cols = target.shape
    block = min(BLOCK, rows)

    def body(target_ref, next_ref, incoming_ref, prob_ref, entropy_ref, window):
        shifted = shift_in(target_ref, next_ref, incoming_ref, window)
        first = lax.axis_index("grp") * rows + pl.program_id(0) * block
        count = lax.axis_size("grp") * rows
        row = first + lax.broadcasted_iota(jnp.int32, (block, 1), 0)
        live = jnp.where(row < count - HEAD, 1.0, 0.0)
        below = shifted - jnp.max(shifted, -1, keepdims=True)
        raised = jnp.exp(below)
        total = jnp.sum(raised, -1, keepdims=True)
        scale = live / total
        prob_ref[...] = raised * scale
        entropy_ref[...] = scale * jnp.sum(raised * below, -1, keepdims=True) - live * jnp.log(total)

    per = block // 8
    return pl.pallas_call(
        body,
        grid=(rows // block,),
        in_specs=[
            row_spec(block, cols),
            pl.BlockSpec((8, cols), lambda i: (jnp.minimum((i + 1) * per, rows // 8 - 1), 0)),
            whole_spec(8, cols),
        ],
        out_specs=[row_spec(block, cols), row_spec(block, 1)],
        out_shape=[
            jax.ShapeDtypeStruct((rows, cols), F32),
            jax.ShapeDtypeStruct((rows, 1), F32),
        ],
        scratch_shapes=[pltpu.VMEM((block + 8, cols), F32)],
        compiler_params=params(24),
        cost_estimate=cost(6 * rows * cols, 8 * rows * cols, rows * cols),
        name="target_pass",
    )(target, target, incoming)


def target_probs(target, incoming, top, total):
    rows, cols = target.shape
    block = min(BLOCK, rows)

    def body(target_ref, next_ref, incoming_ref, top_ref, sum_ref, prob_ref, entropy_ref, window):
        shifted = shift_in(target_ref, next_ref, incoming_ref, window)
        first = lax.axis_index("grp") * rows + pl.program_id(0) * block
        count = lax.axis_size("grp") * rows
        row = first + lax.broadcasted_iota(jnp.int32, (block, 1), 0)
        live = jnp.where(row < count - HEAD, 1.0, 0.0)
        log_target = shifted - (top_ref[...] + jnp.log(sum_ref[...]))
        prob = jnp.exp(log_target) * live
        prob_ref[...] = prob
        entropy_ref[...] = jnp.sum(prob * log_target, -1, keepdims=True)

    per = block // 8
    return pl.pallas_call(
        body,
        grid=(rows // block,),
        in_specs=[
            row_spec(block, cols),
            pl.BlockSpec((8, cols), lambda i: (jnp.minimum((i + 1) * per, rows // 8 - 1), 0)),
            whole_spec(8, cols),
            row_spec(block, 1),
            row_spec(block, 1),
        ],
        out_specs=[row_spec(block, cols), row_spec(block, 1)],
        out_shape=[
            jax.ShapeDtypeStruct((rows, cols), F32),
            jax.ShapeDtypeStruct((rows, 1), F32),
        ],
        scratch_shapes=[pltpu.VMEM((block + 8, cols), F32)],
        compiler_params=params(24),
        cost_estimate=cost(6 * rows * cols, 8 * rows * cols, rows * cols),
        name="target_probs",
    )(target, target, incoming, top, total)


def draft_chunk(target, acts, pieces, column, sums):
    rows, rank = acts.shape
    half_rank, width = pieces[0].shape
    block = min(BLOCK, rows)

    def body(target_ref, acts_ref, own_ref, other_ref, *rest):
        draft_ref, proj_ref, top_ref, sum_ref = rest[-4:]

        @pl.when(pl.program_id(0) == 0)
        def _():
            mine = lax.axis_index("grp") & 1
            proj_ref[pl.ds(pl.multiple_of(mine * half_rank, half_rank), half_rank), :] = own_ref[...]
            proj_ref[
                pl.ds(pl.multiple_of((1 - mine) * half_rank, half_rank), half_rank), :
            ] = other_ref[...]

        draft = target_ref[...] + jnp.dot(
            acts_ref[...], proj_ref[...], preferred_element_type=F32
        )
        draft_ref[...] = draft
        top = jnp.max(draft, -1, keepdims=True)
        if sums is not None:
            top = jnp.maximum(top, rest[0][...])
        total = jnp.sum(jnp.exp(draft - top), -1, keepdims=True)
        if sums is not None:
            total = total + rest[1][...] * jnp.exp(rest[0][...] - top)
        top_ref[...] = top
        sum_ref[...] = total

    carried = () if sums is None else tuple(sums)
    draft, proj, top, total = pl.pallas_call(
        body,
        grid=(rows // block,),
        in_specs=[
            row_spec(block, width, column),
            row_spec(block, rank),
            whole_spec(half_rank, width),
            whole_spec(half_rank, width),
        ]
        + [row_spec(block, 1)] * len(carried),
        out_specs=[
            row_spec(block, width),
            whole_spec(rank, width),
            row_spec(block, 1),
            row_spec(block, 1),
        ],
        out_shape=[
            jax.ShapeDtypeStruct((rows, width), F32),
            jax.ShapeDtypeStruct((rank, width), BF16),
            jax.ShapeDtypeStruct((rows, 1), F32),
            jax.ShapeDtypeStruct((rows, 1), F32),
        ],
        compiler_params=params(16),
        cost_estimate=cost(2 * rows * rank * width, 8 * rows * width, rows * width),
        name="draft_chunk",
    )(target, acts, *pieces, *carried)
    return draft, proj, (top, total)


def grad_chunk(draft, prob, label, acts, vocab_proj, column, sums, carried):
    rows, width = draft.shape
    rank = acts.shape[1]
    half_rank = rank // 2
    block = min(BLOCK, rows)

    def body(draft_ref, prob_ref, label_ref, acts_ref, proj_ref, top_ref, sum_ref, *rest):
        away_ref, kept_ref, act_ref, loss_ref, totals = rest[-5:]
        step = pl.program_id(0)
        first = lax.axis_index("grp") * rows + step * block
        count = lax.axis_size("grp") * rows
        row = first + lax.broadcasted_iota(jnp.int32, (block, 1), 0)
        live = jnp.where(row < count - HEAD, 1.0, 0.0)
        log_draft = draft_ref[...] - (top_ref[...] + jnp.log(sum_ref[...]))
        prob = prob_ref[...]
        place = lax.broadcasted_iota(jnp.int32, (block, width), 1) + column * width
        hit = jnp.where(place == label_ref[...], LAM, 0.0)
        loss = -jnp.sum((prob + hit) * log_draft, -1, keepdims=True)
        grad = ((live + LAM) * jnp.exp(log_draft) - prob - hit).astype(BF16)
        act = inner_cols(grad, proj_ref[...])
        if carried is not None:
            loss = loss + rest[1][...]
            act = act + rest[0][...]
        loss_ref[...] = loss
        act_ref[...] = act
        term = inner_rows(acts_ref[...], grad)

        @pl.when(step == 0)
        def _():
            totals[...] = term

        @pl.when(step > 0)
        def _():
            totals[...] += term

        @pl.when(step == pl.num_programs(0) - 1)
        def _():
            mine = lax.axis_index("grp") & 1
            away = totals[pl.ds(pl.multiple_of((1 - mine) * half_rank, half_rank), half_rank), :]
            away_ref[...] = away.astype(BF16)
            kept_ref[...] = totals[pl.ds(pl.multiple_of(mine * half_rank, half_rank), half_rank), :]

    extra = () if carried is None else tuple(carried)
    away, kept, act, loss = pl.pallas_call(
        body,
        grid=(rows // block,),
        in_specs=[
            row_spec(block, width),
            row_spec(block, width, column),
            row_spec(block, 1),
            row_spec(block, rank),
            whole_spec(rank, width),
            row_spec(block, 1),
            row_spec(block, 1),
        ]
        + ([row_spec(block, rank), row_spec(block, 1)] if extra else []),
        out_specs=[whole_spec(half_rank, width)] * 2 + [row_spec(block, rank), row_spec(block, 1)],
        out_shape=[
            jax.ShapeDtypeStruct((half_rank, width), BF16),
            jax.ShapeDtypeStruct((half_rank, width), F32),
            jax.ShapeDtypeStruct((rows, rank), F32),
            jax.ShapeDtypeStruct((rows, 1), F32),
        ],
        scratch_shapes=[pltpu.VMEM((rank, width), F32)],
        compiler_params=params(16),
        cost_estimate=cost(4 * rows * rank * width, 8 * rows * width, rows * width),
        name="grad_chunk",
    )(draft, prob, label, acts, vocab_proj, *sums, *extra)
    return (away, kept), (act, loss)


class Line:
    def __init__(self):
        self.mark = None

    def after(self, value):
        if self.mark is None:
            return value
        return lax.optimization_barrier((value, self.mark))[0]

    def put(self, value):
        self.mark = jax.tree.leaves(value)[0]
        return value


class Chain:
    def __init__(self, steps):
        self.steps = steps
        self.value = None

    def step(self, times=1):
        for _ in range(times):
            if self.steps is not None:
                try:
                    next(self.steps)
                except StopIteration as end:
                    self.value = end.value
                    self.steps = None

    def result(self):
        while self.steps is not None:
            self.step()
        return self.value


def sent_over(line, value, axis, bit):
    value = line.put(line.after(value))
    arrived = swap(value, axis, bit)
    yield
    return line.after(arrived)


def reduce_steps(line, pair, axis, bits, wires, alike):
    away, part = pair
    for index, (bit, wire) in enumerate(zip(bits[:-1], wires)):
        mine = own_bit(axis, bit)
        if index > 0:
            away, part = half(part, 1 - mine), half(part, mine)
        arrived = yield from sent_over(line, away.astype(wire), axis, bit)
        part = part + arrived.astype(F32)
    sent = part.astype(wires[-1])
    arrived = yield from sent_over(line, sent, axis, bits[-1])
    return (sent.astype(F32) if alike else part) + arrived.astype(F32)


def joined(axis, bit, own, other):
    mine = own_bit(axis, bit)
    low = jnp.where(mine == 0, own, other)
    high = jnp.where(mine == 0, other, own)
    return jnp.concatenate((low, high), 0)


def gather_steps(line, piece, axis, bits):
    for bit in reversed(bits[1:-1]):
        other = yield from sent_over(line, piece, axis, bit)
        piece = joined(axis, bit, piece, other)
    return piece


def split_pair(part, axis, bits):
    mine = own_bit(axis, bits[0])
    return half(part, 1 - mine), half(part, mine)


def summed(line, pair, axis, bits, wires, between, pieces, alike=False):
    def steps():
        total = yield from reduce_steps(line, pair, axis, bits, wires, alike)
        own = yield from gather_steps(line, between(total), axis, bits)
        pieces.append(own)
        other = yield from sent_over(line, own, axis, bits[0])
        pieces.append(other)

    return Chain(steps())


def first_of(chain, pieces):
    while not pieces:
        chain.step()
    return pieces[0]


def over_voc(line, part, bits, wires, between, alike=False):
    pieces = []
    chain = summed(line, split_pair(part, "voc", bits), "voc", bits, wires, between, pieces, alike)
    return chain, lambda: (chain.result(), joined("voc", bits[0], *pieces))[1]


def on_device(hidden_states, target_logits, labels, down_weight, up_weight, head_weight):
    row_count, slice_cols = target_logits.shape
    book_count = labels.shape[1]
    group_count = lax.axis_size("grp")
    per_book = lax.axis_size("voc") // book_count
    block_rows = row_count // per_book
    position = lax.axis_index("voc")
    book_index = position // per_book
    book_part = position % per_book
    width = slice_cols // CHUNKS
    chunks = range(CHUNKS)
    z_bits = list(range(group_count.bit_length() - 1))
    v_bits = list(range(lax.axis_size("voc").bit_length() - 1))
    v_other = v_bits[:1] + v_bits[:0:-1]
    line = Line()

    def columns(c):
        return head_weight[:, c * width : (c + 1) * width]

    mine = own_bit("grp", z_bits[0])
    up_away, up_kept = half(up_weight, 1 - mine), half(up_weight, mine)
    vocab_pieces = [[] for c in chunks]
    vocab, sent = [], []
    for c in chunks:
        away, kept = [
            jnp.dot(part, columns(c), preferred_element_type=F32) * VOCAB_SCALE
            for part in (up_away, up_kept)
        ]
        sent.append(away.astype(F16))
        vocab.append(
            summed(
                line, (sent[c], kept), "grp", z_bits, [F16] * len(z_bits),
                lambda total: (total * (1.0 / VOCAB_SCALE)).astype(BF16), vocab_pieces[c],
            )
        )
    vocab[0].step()
    devices = range(group_count)
    top_rows = line.put(line.after(target_logits[:8]))
    incoming = lax.ppermute(top_rows, "grp", [(i + 1, i) for i in devices if i + 1 in devices])
    vocab[1].step()
    pre_part = line.put(
        jnp.dot(line.after(hidden_states), down_weight, preferred_element_type=F32)
    )
    kept_pre = []

    def activate(total):
        kept_pre.append(total * (1.0 / PRE_SCALE))
        return jax.nn.silu(kept_pre[0]).astype(BF16)

    pre, all_acts = over_voc(
        line, pre_part * PRE_SCALE, v_bits, [F16] * len(v_bits), activate
    )
    pre.step()
    incoming = line.put(line.after(incoming))
    vocab[0].step()
    pre.step()
    vocab[1].step()
    pre.step()
    if per_book == 1:
        prob, entropy = target_pass(line.after(target_logits), incoming)
    else:
        top, total = target_sums(target_logits, incoming)
        top, total = over_books((top, total), merge_sums, per_book)
        prob, entropy = target_probs(target_logits, incoming, top, total)
    line.put(entropy)
    label = lax.dynamic_slice_in_dim(labels, book_index, 1, 1) - book_part * slice_cols
    vocab[0].step()
    pre.step()
    vocab[1].step()
    pre.step()
    vocab[0].result()
    line.put(vocab_pieces[0][1])
    acts = line.put(all_acts())

    drafts, vocab_proj, sums = [], [], None
    for c in chunks:
        vocab[c].result()
        pieces = vocab_pieces[c]
        line.put(pieces[1])
        draft, proj, sums = draft_chunk(target_logits, acts, pieces, c, sums)
        drafts.append(line.put(draft))
        vocab_proj.append(proj)
    sums = over_books(tuple(sums), merge_sums, per_book)

    grads, carried, grad_pieces = [], None, [[] for c in chunks]
    for c in chunks:
        pair, carried = grad_chunk(
            line.after(drafts[c]), prob, label, acts, vocab_proj[c], c, sums, carried
        )
        line.put(pair)
        grads.append(
            summed(
                line, pair, "grp", z_bits, [BF16] * len(z_bits),
                lambda total: total.astype(BF16), grad_pieces[c],
            )
        )
        grads[c].step()
    act_part, loss = carried
    act, all_pre_grad = over_voc(
        line, act_part, v_bits, [F32] + [BF16] * len(v_bits),
        lambda total: (total * silu_slope(kept_pre[0])).astype(BF16),
    )
    grads[0].step()
    act.step()
    act.step()
    grads[1].step()
    act.step()
    def times_head(before, piece, c):
        return line.put(before + inner_cols(line.after(piece), columns(c)))

    own_up = times_head(0.0, first_of(grads[0], grad_pieces[0]), 0)
    act.step()
    own = first_of(grads[1], grad_pieces[1])
    act.step()
    grads[0].result()
    other_up = times_head(0.0, grad_pieces[0][1], 0)
    pre_grad = line.put(all_pre_grad())
    down_part = line.put(inner_rows(line.after(hidden_states), pre_grad))
    rows = down_part.shape[0] // 2
    down_pieces = [[], []]
    downs = [
        summed(
            line, split_pair(part, "grp", z_bits), "grp", z_bits, [BF16] * len(z_bits),
            lambda total: total.astype(BF16), down_pieces[i], True,
        )
        for i, part in enumerate((down_part[:rows], down_part[rows:]))
    ]
    downs[0].step()
    downs[1].step()
    own_up = times_head(own_up, own, 1)
    grads[1].result()
    other_up = times_head(other_up, grad_pieces[1][1], 1)
    up_part = joined("grp", z_bits[0], own_up, other_up)
    rank = up_part.shape[0] // 2
    ups = [
        over_voc(
            line, part, bits, [F32] + [BF16] * len(v_bits), lambda total: total.astype(BF16), True
        )
        for part, bits in ((up_part[:rank], v_bits), (up_part[rank:], v_other))
    ]
    swaps = [chain for chain, _ in ups]
    loss = over_books(line.after(loss) + entropy, jnp.add, per_book)
    frame_loss = lax.dynamic_slice_in_dim(loss, book_part * block_rows, block_rows, 0)
    frame_loss = frame_loss.reshape(1, 1, block_rows)
    for turn in (swaps, downs, swaps, swaps, swaps, downs, swaps):
        for chain in turn:
            chain.step()
    grad_b = jnp.concatenate([result().astype(F32) for _, result in ups], 0)
    for chain in downs:
        chain.result()
    grad_a = jnp.concatenate(
        [joined("grp", z_bits[0], *pieces).astype(F32) for pieces in down_pieces], 0
    )
    return frame_loss, grad_a, grad_b


def solution(mesh):
    in_specs = (
        P("grp", "voc"),
        P("grp", "voc"),
        P("grp", None),
        P("voc", None),
        P(None, "grp"),
        P("grp", "voc"),
    )
    out_specs = (P("voc", "grp", None), P("voc", None), P(None, "grp"))
    return jax.shard_map(
        on_device, mesh=mesh, in_specs=in_specs, out_specs=out_specs, check_vma=False
    )
```

```python
import jax
import jax.numpy as jnp
from jax import lax
from jax.experimental import pallas as pl
from jax.experimental.pallas import tpu as pltpu
from jax.sharding import PartitionSpec as P

HEAD = 2
LAM = 0.1
CHUNKS = 2
BLOCK = 256
VOCAB_SCALE = 128.0
PRE_SCALE = 64.0
F32 = jnp.float32
BF16 = jnp.bfloat16
F16 = jnp.float16


def swap(value, axis, bit):
    mask = 1 << bit
    pairs = [(i, i ^ mask) for i in range(lax.axis_size(axis))]
    return lax.ppermute(value, axis, pairs)


def own_bit(axis, bit):
    return (lax.axis_index(axis) >> bit) & 1


def half(value, which):
    rows = value.shape[0] // 2
    return lax.dynamic_slice_in_dim(value, which * rows, rows, 0)


def silu_slope(values):
    sigma = jax.nn.sigmoid(values)
    return sigma * (1.0 + values * (1.0 - sigma))


def inner_rows(left, right):
    return lax.dot_general(left, right, (((0,), (0,)), ((), ())), preferred_element_type=F32)


def inner_cols(left, right):
    return lax.dot_general(left, right, (((1,), (1,)), ((), ())), preferred_element_type=F32)


def over_books(values, combine, per_book):
    bit = 0
    while (1 << bit) < per_book:
        values = combine(values, jax.tree.map(lambda v: swap(v, "voc", bit), values))
        bit += 1
    return values


def merge_sums(a, b):
    top = jnp.maximum(a[0], b[0])
    return top, a[1] * jnp.exp(a[0] - top) + b[1] * jnp.exp(b[0] - top)


def params(megabytes):
    return pltpu.CompilerParams(
        dimension_semantics=("arbitrary",), vmem_limit_bytes=megabytes << 20
    )


def cost(flops, read, exps):
    return pl.CostEstimate(flops=flops // 4096, bytes_accessed=read, transcendentals=0)


def row_spec(block, cols, column=0):
    return pl.BlockSpec((block, cols), lambda i: (i, column))


def whole_spec(rows, cols):
    return pl.BlockSpec((rows, cols), lambda i: (0, 0))


def shift_in(target_ref, next_ref, incoming_ref, window):
    block = target_ref.shape[0]
    last = pl.program_id(0) == pl.num_programs(0) - 1
    window[:block, :] = target_ref[...]
    window[block:, :] = jnp.where(last, incoming_ref[...], next_ref[...])
    return window[HEAD : HEAD + block, :]


def target_sums(target, incoming):
    rows, cols = target.shape
    block = min(BLOCK, rows)

    def body(target_ref, next_ref, incoming_ref, top_ref, sum_ref, window):
        shifted = shift_in(target_ref, next_ref, incoming_ref, window)
        top = jnp.max(shifted, -1, keepdims=True)
        top_ref[...] = top
        sum_ref[...] = jnp.sum(jnp.exp(shifted - top), -1, keepdims=True)

    per = block // 8
    return pl.pallas_call(
        body,
        grid=(rows // block,),
        in_specs=[
            row_spec(block, cols),
            pl.BlockSpec((8, cols), lambda i: (jnp.minimum((i + 1) * per, rows // 8 - 1), 0)),
            whole_spec(8, cols),
        ],
        out_specs=[row_spec(block, 1)] * 2,
        out_shape=[jax.ShapeDtypeStruct((rows, 1), F32)] * 2,
        scratch_shapes=[pltpu.VMEM((block + 8, cols), F32)],
        compiler_params=params(24),
        cost_estimate=cost(4 * rows * cols, 4 * rows * cols, rows * cols),
        name="target_sums",
    )(target, target, incoming)


def target_pass(target, incoming):
    rows, cols = target.shape
    block = min(BLOCK, rows)

    def body(target_ref, next_ref, incoming_ref, prob_ref, entropy_ref, window):
        shifted = shift_in(target_ref, next_ref, incoming_ref, window)
        first = lax.axis_index("grp") * rows + pl.program_id(0) * block
        count = lax.axis_size("grp") * rows
        row = first + lax.broadcasted_iota(jnp.int32, (block, 1), 0)
        live = jnp.where(row < count - HEAD, 1.0, 0.0)
        below = shifted - jnp.max(shifted, -1, keepdims=True)
        raised = jnp.exp(below)
        total = jnp.sum(raised, -1, keepdims=True)
        scale = live / total
        prob_ref[...] = raised * scale
        entropy_ref[...] = scale * jnp.sum(raised * below, -1, keepdims=True) - live * jnp.log(total)

    per = block // 8
    return pl.pallas_call(
        body,
        grid=(rows // block,),
        in_specs=[
            row_spec(block, cols),
            pl.BlockSpec((8, cols), lambda i: (jnp.minimum((i + 1) * per, rows // 8 - 1), 0)),
            whole_spec(8, cols),
        ],
        out_specs=[row_spec(block, cols), row_spec(block, 1)],
        out_shape=[
            jax.ShapeDtypeStruct((rows, cols), F32),
            jax.ShapeDtypeStruct((rows, 1), F32),
        ],
        scratch_shapes=[pltpu.VMEM((block + 8, cols), F32)],
        compiler_params=params(24),
        cost_estimate=cost(6 * rows * cols, 8 * rows * cols, rows * cols),
        name="target_pass",
    )(target, target, incoming)


def target_probs(target, incoming, top, total):
    rows, cols = target.shape
    block = min(BLOCK, rows)

    def body(target_ref, next_ref, incoming_ref, top_ref, sum_ref, prob_ref, entropy_ref, window):
        shifted = shift_in(target_ref, next_ref, incoming_ref, window)
        first = lax.axis_index("grp") * rows + pl.program_id(0) * block
        count = lax.axis_size("grp") * rows
        row = first + lax.broadcasted_iota(jnp.int32, (block, 1), 0)
        live = jnp.where(row < count - HEAD, 1.0, 0.0)
        log_target = shifted - (top_ref[...] + jnp.log(sum_ref[...]))
        prob = jnp.exp(log_target) * live
        prob_ref[...] = prob
        entropy_ref[...] = jnp.sum(prob * log_target, -1, keepdims=True)

    per = block // 8
    return pl.pallas_call(
        body,
        grid=(rows // block,),
        in_specs=[
            row_spec(block, cols),
            pl.BlockSpec((8, cols), lambda i: (jnp.minimum((i + 1) * per, rows // 8 - 1), 0)),
            whole_spec(8, cols),
            row_spec(block, 1),
            row_spec(block, 1),
        ],
        out_specs=[row_spec(block, cols), row_spec(block, 1)],
        out_shape=[
            jax.ShapeDtypeStruct((rows, cols), F32),
            jax.ShapeDtypeStruct((rows, 1), F32),
        ],
        scratch_shapes=[pltpu.VMEM((block + 8, cols), F32)],
        compiler_params=params(24),
        cost_estimate=cost(6 * rows * cols, 8 * rows * cols, rows * cols),
        name="target_probs",
    )(target, target, incoming, top, total)


def draft_chunk(target, acts, pieces, column, sums):
    rows, rank = acts.shape
    half_rank, width = pieces[0].shape
    block = min(BLOCK, rows)

    def body(target_ref, acts_ref, own_ref, other_ref, *rest):
        draft_ref, proj_ref, top_ref, sum_ref = rest[-4:]

        @pl.when(pl.program_id(0) == 0)
        def _():
            mine = lax.axis_index("grp") & 1
            proj_ref[pl.ds(pl.multiple_of(mine * half_rank, half_rank), half_rank), :] = own_ref[...]
            proj_ref[
                pl.ds(pl.multiple_of((1 - mine) * half_rank, half_rank), half_rank), :
            ] = other_ref[...]

        draft = target_ref[...] + jnp.dot(
            acts_ref[...], proj_ref[...], preferred_element_type=F32
        )
        draft_ref[...] = draft
        top = jnp.max(draft, -1, keepdims=True)
        if sums is not None:
            top = jnp.maximum(top, rest[0][...])
        total = jnp.sum(jnp.exp(draft - top), -1, keepdims=True)
        if sums is not None:
            total = total + rest[1][...] * jnp.exp(rest[0][...] - top)
        top_ref[...] = top
        sum_ref[...] = total

    carried = () if sums is None else tuple(sums)
    draft, proj, top, total = pl.pallas_call(
        body,
        grid=(rows // block,),
        in_specs=[
            row_spec(block, width, column),
            row_spec(block, rank),
            whole_spec(half_rank, width),
            whole_spec(half_rank, width),
        ]
        + [row_spec(block, 1)] * len(carried),
        out_specs=[
            row_spec(block, width),
            whole_spec(rank, width),
            row_spec(block, 1),
            row_spec(block, 1),
        ],
        out_shape=[
            jax.ShapeDtypeStruct((rows, width), F32),
            jax.ShapeDtypeStruct((rank, width), BF16),
            jax.ShapeDtypeStruct((rows, 1), F32),
            jax.ShapeDtypeStruct((rows, 1), F32),
        ],
        compiler_params=params(16),
        cost_estimate=cost(2 * rows * rank * width, 8 * rows * width, rows * width),
        name="draft_chunk",
    )(target, acts, *pieces, *carried)
    return draft, proj, (top, total)


def grad_chunk(draft, prob, label, acts, vocab_proj, column, sums, carried):
    rows, width = draft.shape
    rank = acts.shape[1]
    half_rank = rank // 2
    block = min(BLOCK, rows)

    def body(draft_ref, prob_ref, label_ref, acts_ref, proj_ref, top_ref, sum_ref, *rest):
        away_ref, kept_ref, act_ref, loss_ref, totals = rest[-5:]
        step = pl.program_id(0)
        first = lax.axis_index("grp") * rows + step * block
        count = lax.axis_size("grp") * rows
        row = first + lax.broadcasted_iota(jnp.int32, (block, 1), 0)
        live = jnp.where(row < count - HEAD, 1.0, 0.0)
        log_draft = draft_ref[...] - (top_ref[...] + jnp.log(sum_ref[...]))
        prob = prob_ref[...]
        place = lax.broadcasted_iota(jnp.int32, (block, width), 1) + column * width
        hit = jnp.where(place == label_ref[...], LAM, 0.0)
        loss = -jnp.sum((prob + hit) * log_draft, -1, keepdims=True)
        grad = ((live + LAM) * jnp.exp(log_draft) - prob - hit).astype(BF16)
        act = inner_cols(grad, proj_ref[...])
        if carried is not None:
            loss = loss + rest[1][...]
            act = act + rest[0][...]
        loss_ref[...] = loss
        act_ref[...] = act
        term = inner_rows(acts_ref[...], grad)

        @pl.when(step == 0)
        def _():
            totals[...] = term

        @pl.when(step > 0)
        def _():
            totals[...] += term

        @pl.when(step == pl.num_programs(0) - 1)
        def _():
            mine = lax.axis_index("grp") & 1
            away = totals[pl.ds(pl.multiple_of((1 - mine) * half_rank, half_rank), half_rank), :]
            away_ref[...] = away.astype(BF16)
            kept_ref[...] = totals[pl.ds(pl.multiple_of(mine * half_rank, half_rank), half_rank), :]

    extra = () if carried is None else tuple(carried)
    away, kept, act, loss = pl.pallas_call(
        body,
        grid=(rows // block,),
        in_specs=[
            row_spec(block, width),
            row_spec(block, width, column),
            row_spec(block, 1),
            row_spec(block, rank),
            whole_spec(rank, width),
            row_spec(block, 1),
            row_spec(block, 1),
        ]
        + ([row_spec(block, rank), row_spec(block, 1)] if extra else []),
        out_specs=[whole_spec(half_rank, width)] * 2 + [row_spec(block, rank), row_spec(block, 1)],
        out_shape=[
            jax.ShapeDtypeStruct((half_rank, width), BF16),
            jax.ShapeDtypeStruct((half_rank, width), F32),
            jax.ShapeDtypeStruct((rows, rank), F32),
            jax.ShapeDtypeStruct((rows, 1), F32),
        ],
        scratch_shapes=[pltpu.VMEM((rank, width), F32)],
        compiler_params=params(16),
        cost_estimate=cost(4 * rows * rank * width, 8 * rows * width, rows * width),
        name="grad_chunk",
    )(draft, prob, label, acts, vocab_proj, *sums, *extra)
    return (away, kept), (act, loss)


class Line:
    def __init__(self):
        self.mark = None

    def after(self, value):
        if self.mark is None:
            return value
        return lax.optimization_barrier((value, self.mark))[0]

    def put(self, value):
        self.mark = jax.tree.leaves(value)[0]
        return value


class Chain:
    def __init__(self, steps):
        self.steps = steps
        self.value = None

    def step(self, times=1):
        for _ in range(times):
            if self.steps is not None:
                try:
                    next(self.steps)
                except StopIteration as end:
                    self.value = end.value
                    self.steps = None

    def result(self):
        while self.steps is not None:
            self.step()
        return self.value


def sent_over(line, value, axis, bit):
    value = line.put(line.after(value))
    arrived = swap(value, axis, bit)
    yield
    return line.after(arrived)


def reduce_steps(line, pair, axis, bits, wires, alike):
    away, part = pair
    for index, (bit, wire) in enumerate(zip(bits[:-1], wires)):
        mine = own_bit(axis, bit)
        if index > 0:
            away, part = half(part, 1 - mine), half(part, mine)
        arrived = yield from sent_over(line, away.astype(wire), axis, bit)
        part = part + arrived.astype(F32)
    sent = part.astype(wires[-1])
    arrived = yield from sent_over(line, sent, axis, bits[-1])
    return (sent.astype(F32) if alike else part) + arrived.astype(F32)


def joined(axis, bit, own, other):
    mine = own_bit(axis, bit)
    low = jnp.where(mine == 0, own, other)
    high = jnp.where(mine == 0, other, own)
    return jnp.concatenate((low, high), 0)


def gather_steps(line, piece, axis, bits):
    for bit in reversed(bits[1:-1]):
        other = yield from sent_over(line, piece, axis, bit)
        piece = joined(axis, bit, piece, other)
    return piece


def split_pair(part, axis, bits):
    mine = own_bit(axis, bits[0])
    return half(part, 1 - mine), half(part, mine)


def summed(line, pair, axis, bits, wires, between, pieces, alike=False):
    def steps():
        total = yield from reduce_steps(line, pair, axis, bits, wires, alike)
        own = yield from gather_steps(line, between(total), axis, bits)
        pieces.append(own)
        other = yield from sent_over(line, own, axis, bits[0])
        pieces.append(other)

    return Chain(steps())


def first_of(chain, pieces):
    while not pieces:
        chain.step()
    return pieces[0]


def over_voc(line, part, bits, wires, between, alike=False):
    pieces = []
    chain = summed(line, split_pair(part, "voc", bits), "voc", bits, wires, between, pieces, alike)
    return chain, lambda: (chain.result(), joined("voc", bits[0], *pieces))[1]


def on_device(hidden_states, target_logits, labels, down_weight, up_weight, head_weight):
    row_count, slice_cols = target_logits.shape
    book_count = labels.shape[1]
    group_count = lax.axis_size("grp")
    per_book = lax.axis_size("voc") // book_count
    block_rows = row_count // per_book
    position = lax.axis_index("voc")
    book_index = position // per_book
    book_part = position % per_book
    width = slice_cols // CHUNKS
    chunks = range(CHUNKS)
    z_bits = list(range(group_count.bit_length() - 1))
    v_bits = list(range(lax.axis_size("voc").bit_length() - 1))
    v_other = v_bits[:1] + v_bits[:0:-1]
    line = Line()

    def columns(c):
        return head_weight[:, c * width : (c + 1) * width]

    mine = own_bit("grp", z_bits[0])
    up_away, up_kept = half(up_weight, 1 - mine), half(up_weight, mine)
    vocab_pieces = [[] for c in chunks]
    vocab, sent = [], []
    for c in chunks:
        away, kept = [
            jnp.dot(part, columns(c), preferred_element_type=F32) * VOCAB_SCALE
            for part in (up_away, up_kept)
        ]
        sent.append(away.astype(F16))
        vocab.append(
            summed(
                line, (sent[c], kept), "grp", z_bits, [F16] * len(z_bits),
                lambda total: (total * (1.0 / VOCAB_SCALE)).astype(BF16), vocab_pieces[c],
            )
        )
    vocab[0].step()
    devices = range(group_count)
    top_rows = line.put(line.after(target_logits[:8]))
    incoming = lax.ppermute(top_rows, "grp", [(i + 1, i) for i in devices if i + 1 in devices])
    vocab[1].step()
    pre_part = line.put(
        jnp.dot(line.after(hidden_states), down_weight, preferred_element_type=F32)
    )
    kept_pre = []

    def activate(total):
        kept_pre.append(total * (1.0 / PRE_SCALE))
        return jax.nn.silu(kept_pre[0]).astype(BF16)

    pre, all_acts = over_voc(
        line, pre_part * PRE_SCALE, v_bits, [F16] * len(v_bits), activate
    )
    pre.step()
    incoming = line.put(line.after(incoming))
    vocab[0].step()
    pre.step()
    vocab[1].step()
    pre.step()
    if per_book == 1:
        prob, entropy = target_pass(line.after(target_logits), incoming)
    else:
        top, total = target_sums(target_logits, incoming)
        top, total = over_books((top, total), merge_sums, per_book)
        prob, entropy = target_probs(target_logits, incoming, top, total)
    line.put(entropy)
    label = lax.dynamic_slice_in_dim(labels, book_index, 1, 1) - book_part * slice_cols
    vocab[0].step()
    pre.step()
    vocab[1].step()
    pre.step()
    vocab[0].result()
    line.put(vocab_pieces[0][1])
    acts = line.put(all_acts())

    drafts, vocab_proj, sums = [], [], None
    for c in chunks:
        vocab[c].result()
        pieces = vocab_pieces[c]
        line.put(pieces[1])
        draft, proj, sums = draft_chunk(target_logits, acts, pieces, c, sums)
        drafts.append(line.put(draft))
        vocab_proj.append(proj)
    sums = over_books(tuple(sums), merge_sums, per_book)

    grads, carried, grad_pieces = [], None, [[] for c in chunks]
    for c in chunks:
        pair, carried = grad_chunk(
            line.after(drafts[c]), prob, label, acts, vocab_proj[c], c, sums, carried
        )
        line.put(pair)
        grads.append(
            summed(
                line, pair, "grp", z_bits, [BF16] * len(z_bits),
                lambda total: total.astype(BF16), grad_pieces[c],
            )
        )
        grads[c].step()
    act_part, loss = carried
    act, all_pre_grad = over_voc(
        line, act_part, v_bits, [F32] + [BF16] * len(v_bits),
        lambda total: (total * silu_slope(kept_pre[0])).astype(BF16),
    )
    grads[0].step()
    act.step()
    act.step()
    grads[1].step()
    act.step()
    def times_head(before, piece, c):
        return line.put(before + inner_cols(line.after(piece), columns(c)))

    own_up = times_head(0.0, first_of(grads[0], grad_pieces[0]), 0)
    act.step()
    own = first_of(grads[1], grad_pieces[1])
    act.step()
    grads[0].result()
    line.put(grad_pieces[0][1])
    pre_grad = line.put(all_pre_grad())
    down_part = line.put(inner_rows(line.after(hidden_states), pre_grad))
    rows = down_part.shape[0] // 2
    down_pieces = [[], []]
    downs = [
        summed(
            line, split_pair(part, "grp", z_bits), "grp", z_bits, [BF16] * len(z_bits),
            lambda total: total.astype(BF16), down_pieces[i], True,
        )
        for i, part in enumerate((down_part[:rows], down_part[rows:]))
    ]
    downs[0].step()
    downs[1].step()
    own_up = times_head(own_up, own, 1)
    other_up = times_head(0.0, grad_pieces[0][1], 0)
    grads[1].result()
    other_up = times_head(other_up, grad_pieces[1][1], 1)
    up_part = joined("grp", z_bits[0], own_up, other_up)
    rank = up_part.shape[0] // 2
    ups = [
        over_voc(
            line, part, bits, [F32] + [BF16] * len(v_bits), lambda total: total.astype(BF16), True
        )
        for part, bits in ((up_part[:rank], v_bits), (up_part[rank:], v_other))
    ]
    swaps = [chain for chain, _ in ups]
    loss = over_books(line.after(loss) + entropy, jnp.add, per_book)
    frame_loss = lax.dynamic_slice_in_dim(loss, book_part * block_rows, block_rows, 0)
    frame_loss = frame_loss.reshape(1, 1, block_rows)
    for turn in (swaps, downs, swaps, swaps, swaps, downs, swaps):
        for chain in turn:
            chain.step()
    grad_b = jnp.concatenate([result().astype(F32) for _, result in ups], 0)
    for chain in downs:
        chain.result()
    grad_a = jnp.concatenate(
        [joined("grp", z_bits[0], *pieces).astype(F32) for pieces in down_pieces], 0
    )
    return frame_loss, grad_a, grad_b


def solution(mesh):
    in_specs = (
        P("grp", "voc"),
        P("grp", "voc"),
        P("grp", None),
        P("voc", None),
        P(None, "grp"),
        P("grp", "voc"),
    )
    out_specs = (P("voc", "grp", None), P("voc", None), P(None, "grp"))
    return jax.shard_map(
        on_device, mesh=mesh, in_specs=in_specs, out_specs=out_specs, check_vma=False
    )
```

```python
import jax
import jax.numpy as jnp
from jax import lax
from jax.experimental import pallas as pl
from jax.experimental.pallas import tpu as pltpu
from jax.sharding import PartitionSpec as P

HEAD = 2
LAM = 0.1
CHUNKS = 2
BLOCK = 256
VOCAB_SCALE = 128.0
PRE_SCALE = 64.0
F32 = jnp.float32
BF16 = jnp.bfloat16
F16 = jnp.float16


def swap(value, axis, bit):
    mask = 1 << bit
    pairs = [(i, i ^ mask) for i in range(lax.axis_size(axis))]
    return lax.ppermute(value, axis, pairs)


def own_bit(axis, bit):
    return (lax.axis_index(axis) >> bit) & 1


def half(value, which):
    rows = value.shape[0] // 2
    return lax.dynamic_slice_in_dim(value, which * rows, rows, 0)


def silu_slope(values):
    sigma = jax.nn.sigmoid(values)
    return sigma * (1.0 + values * (1.0 - sigma))


def inner_rows(left, right):
    return lax.dot_general(left, right, (((0,), (0,)), ((), ())), preferred_element_type=F32)


def inner_cols(left, right):
    return lax.dot_general(left, right, (((1,), (1,)), ((), ())), preferred_element_type=F32)


def over_books(values, combine, per_book):
    bit = 0
    while (1 << bit) < per_book:
        values = combine(values, jax.tree.map(lambda v: swap(v, "voc", bit), values))
        bit += 1
    return values


def merge_sums(a, b):
    top = jnp.maximum(a[0], b[0])
    return top, a[1] * jnp.exp(a[0] - top) + b[1] * jnp.exp(b[0] - top)


def params(megabytes):
    return pltpu.CompilerParams(
        dimension_semantics=("arbitrary",), vmem_limit_bytes=megabytes << 20
    )


def cost(flops, read, exps):
    return pl.CostEstimate(flops=flops // 4096, bytes_accessed=read // 4096, transcendentals=0)


def row_spec(block, cols, column=0):
    return pl.BlockSpec((block, cols), lambda i: (i, column))


def whole_spec(rows, cols):
    return pl.BlockSpec((rows, cols), lambda i: (0, 0))


def shift_in(target_ref, next_ref, incoming_ref, window):
    block = target_ref.shape[0]
    last = pl.program_id(0) == pl.num_programs(0) - 1
    window[:block, :] = target_ref[...]
    window[block:, :] = jnp.where(last, incoming_ref[...], next_ref[...])
    return window[HEAD : HEAD + block, :]


def target_sums(target, incoming):
    rows, cols = target.shape
    block = min(BLOCK // 2, rows)

    def body(target_ref, next_ref, incoming_ref, top_ref, sum_ref, window):
        shifted = shift_in(target_ref, next_ref, incoming_ref, window)
        top = jnp.max(shifted, -1, keepdims=True)
        top_ref[...] = top
        sum_ref[...] = jnp.sum(jnp.exp(shifted - top), -1, keepdims=True)

    per = block // 8
    return pl.pallas_call(
        body,
        grid=(rows // block,),
        in_specs=[
            row_spec(block, cols),
            pl.BlockSpec((8, cols), lambda i: (jnp.minimum((i + 1) * per, rows // 8 - 1), 0)),
            whole_spec(8, cols),
        ],
        out_specs=[row_spec(block, 1)] * 2,
        out_shape=[jax.ShapeDtypeStruct((rows, 1), F32)] * 2,
        scratch_shapes=[pltpu.VMEM((block + 8, cols), F32)],
        compiler_params=params(12),
        cost_estimate=cost(4 * rows * cols, 4 * rows * cols, rows * cols),
        name="target_sums",
    )(target, target, incoming)


def target_pass(target, incoming):
    rows, cols = target.shape
    block = min(BLOCK // 2, rows)

    def body(target_ref, next_ref, incoming_ref, prob_ref, entropy_ref, window):
        shifted = shift_in(target_ref, next_ref, incoming_ref, window)
        first = lax.axis_index("grp") * rows + pl.program_id(0) * block
        count = lax.axis_size("grp") * rows
        row = first + lax.broadcasted_iota(jnp.int32, (block, 1), 0)
        live = jnp.where(row < count - HEAD, 1.0, 0.0)
        below = shifted - jnp.max(shifted, -1, keepdims=True)
        raised = jnp.exp(below)
        total = jnp.sum(raised, -1, keepdims=True)
        scale = live / total
        prob_ref[...] = raised * scale
        entropy_ref[...] = scale * jnp.sum(raised * below, -1, keepdims=True) - live * jnp.log(total)

    per = block // 8
    return pl.pallas_call(
        body,
        grid=(rows // block,),
        in_specs=[
            row_spec(block, cols),
            pl.BlockSpec((8, cols), lambda i: (jnp.minimum((i + 1) * per, rows // 8 - 1), 0)),
            whole_spec(8, cols),
        ],
        out_specs=[row_spec(block, cols), row_spec(block, 1)],
        out_shape=[
            jax.ShapeDtypeStruct((rows, cols), F32),
            jax.ShapeDtypeStruct((rows, 1), F32),
        ],
        scratch_shapes=[pltpu.VMEM((block + 8, cols), F32)],
        compiler_params=params(12),
        cost_estimate=cost(6 * rows * cols, 8 * rows * cols, rows * cols),
        name="target_pass",
    )(target, target, incoming)


def target_probs(target, incoming, top, total):
    rows, cols = target.shape
    block = min(BLOCK // 2, rows)

    def body(target_ref, next_ref, incoming_ref, top_ref, sum_ref, prob_ref, entropy_ref, window):
        shifted = shift_in(target_ref, next_ref, incoming_ref, window)
        first = lax.axis_index("grp") * rows + pl.program_id(0) * block
        count = lax.axis_size("grp") * rows
        row = first + lax.broadcasted_iota(jnp.int32, (block, 1), 0)
        live = jnp.where(row < count - HEAD, 1.0, 0.0)
        log_target = shifted - (top_ref[...] + jnp.log(sum_ref[...]))
        prob = jnp.exp(log_target) * live
        prob_ref[...] = prob
        entropy_ref[...] = jnp.sum(prob * log_target, -1, keepdims=True)

    per = block // 8
    return pl.pallas_call(
        body,
        grid=(rows // block,),
        in_specs=[
            row_spec(block, cols),
            pl.BlockSpec((8, cols), lambda i: (jnp.minimum((i + 1) * per, rows // 8 - 1), 0)),
            whole_spec(8, cols),
            row_spec(block, 1),
            row_spec(block, 1),
        ],
        out_specs=[row_spec(block, cols), row_spec(block, 1)],
        out_shape=[
            jax.ShapeDtypeStruct((rows, cols), F32),
            jax.ShapeDtypeStruct((rows, 1), F32),
        ],
        scratch_shapes=[pltpu.VMEM((block + 8, cols), F32)],
        compiler_params=params(12),
        cost_estimate=cost(6 * rows * cols, 8 * rows * cols, rows * cols),
        name="target_probs",
    )(target, target, incoming, top, total)


def draft_chunk(target, acts, pieces, column, sums):
    rows, rank = acts.shape
    half_rank, width = pieces[0].shape
    block = min(BLOCK, rows)

    def body(target_ref, acts_ref, own_ref, other_ref, *rest):
        draft_ref, proj_ref, top_ref, sum_ref = rest[-4:]

        @pl.when(pl.program_id(0) == 0)
        def _():
            mine = lax.axis_index("grp") & 1
            proj_ref[pl.ds(pl.multiple_of(mine * half_rank, half_rank), half_rank), :] = own_ref[...]
            proj_ref[
                pl.ds(pl.multiple_of((1 - mine) * half_rank, half_rank), half_rank), :
            ] = other_ref[...]

        draft = target_ref[...] + jnp.dot(
            acts_ref[...], proj_ref[...], preferred_element_type=F32
        )
        draft_ref[...] = draft
        top = jnp.max(draft, -1, keepdims=True)
        if sums is not None:
            top = jnp.maximum(top, rest[0][...])
        total = jnp.sum(jnp.exp(draft - top), -1, keepdims=True)
        if sums is not None:
            total = total + rest[1][...] * jnp.exp(rest[0][...] - top)
        top_ref[...] = top
        sum_ref[...] = total

    carried = () if sums is None else tuple(sums)
    draft, proj, top, total = pl.pallas_call(
        body,
        grid=(rows // block,),
        in_specs=[
            row_spec(block, width, column),
            row_spec(block, rank),
            whole_spec(half_rank, width),
            whole_spec(half_rank, width),
        ]
        + [row_spec(block, 1)] * len(carried),
        out_specs=[
            row_spec(block, width),
            whole_spec(rank, width),
            row_spec(block, 1),
            row_spec(block, 1),
        ],
        out_shape=[
            jax.ShapeDtypeStruct((rows, width), F32),
            jax.ShapeDtypeStruct((rank, width), BF16),
            jax.ShapeDtypeStruct((rows, 1), F32),
            jax.ShapeDtypeStruct((rows, 1), F32),
        ],
        compiler_params=params(14),
        cost_estimate=cost(2 * rows * rank * width, 8 * rows * width, rows * width),
        name="draft_chunk",
    )(target, acts, *pieces, *carried)
    return draft, proj, (top, total)


def grad_chunk(draft, prob, label, acts, vocab_proj, column, sums, carried):
    rows, width = draft.shape
    rank = acts.shape[1]
    half_rank = rank // 2
    block = min(BLOCK, rows)

    def body(draft_ref, prob_ref, label_ref, acts_ref, proj_ref, top_ref, sum_ref, *rest):
        away_ref, kept_ref, act_ref, loss_ref, totals = rest[-5:]
        step = pl.program_id(0)
        first = lax.axis_index("grp") * rows + step * block
        count = lax.axis_size("grp") * rows
        row = first + lax.broadcasted_iota(jnp.int32, (block, 1), 0)
        live = jnp.where(row < count - HEAD, 1.0, 0.0)
        log_draft = draft_ref[...] - (top_ref[...] + jnp.log(sum_ref[...]))
        prob = prob_ref[...]
        place = lax.broadcasted_iota(jnp.int32, (block, width), 1) + column * width
        hit = jnp.where(place == label_ref[...], LAM, 0.0)
        loss = -jnp.sum((prob + hit) * log_draft, -1, keepdims=True)
        grad = ((live + LAM) * jnp.exp(log_draft) - prob - hit).astype(BF16)
        act = inner_cols(grad, proj_ref[...])
        if carried is not None:
            loss = loss + rest[1][...]
            act = act + rest[0][...]
        loss_ref[...] = loss
        act_ref[...] = act
        term = inner_rows(acts_ref[...], grad)

        @pl.when(step == 0)
        def _():
            totals[...] = term

        @pl.when(step > 0)
        def _():
            totals[...] += term

        @pl.when(step == pl.num_programs(0) - 1)
        def _():
            mine = lax.axis_index("grp") & 1
            away = totals[pl.ds(pl.multiple_of((1 - mine) * half_rank, half_rank), half_rank), :]
            away_ref[...] = away.astype(BF16)
            kept_ref[...] = totals[pl.ds(pl.multiple_of(mine * half_rank, half_rank), half_rank), :]

    extra = () if carried is None else tuple(carried)
    away, kept, act, loss = pl.pallas_call(
        body,
        grid=(rows // block,),
        in_specs=[
            row_spec(block, width),
            row_spec(block, width, column),
            row_spec(block, 1),
            row_spec(block, rank),
            whole_spec(rank, width),
            row_spec(block, 1),
            row_spec(block, 1),
        ]
        + ([row_spec(block, rank), row_spec(block, 1)] if extra else []),
        out_specs=[whole_spec(half_rank, width)] * 2 + [row_spec(block, rank), row_spec(block, 1)],
        out_shape=[
            jax.ShapeDtypeStruct((half_rank, width), BF16),
            jax.ShapeDtypeStruct((half_rank, width), F32),
            jax.ShapeDtypeStruct((rows, rank), F32),
            jax.ShapeDtypeStruct((rows, 1), F32),
        ],
        scratch_shapes=[pltpu.VMEM((rank, width), F32)],
        compiler_params=params(14),
        cost_estimate=cost(4 * rows * rank * width, 8 * rows * width, rows * width),
        name="grad_chunk",
    )(draft, prob, label, acts, vocab_proj, *sums, *extra)
    return (away, kept), (act, loss)


class Line:
    def __init__(self):
        self.mark = None

    def after(self, value):
        if self.mark is None:
            return value
        return lax.optimization_barrier((value, self.mark))[0]

    def put(self, value):
        self.mark = jax.tree.leaves(value)[0]
        return value


class Chain:
    def __init__(self, steps):
        self.steps = steps
        self.value = None

    def step(self, times=1):
        for _ in range(times):
            if self.steps is not None:
                try:
                    next(self.steps)
                except StopIteration as end:
                    self.value = end.value
                    self.steps = None

    def result(self):
        while self.steps is not None:
            self.step()
        return self.value


def sent_over(line, value, axis, bit):
    value = line.put(line.after(value))
    arrived = swap(value, axis, bit)
    yield
    return line.after(arrived)


def reduce_steps(line, pair, axis, bits, wires, alike):
    away, part = pair
    for index, (bit, wire) in enumerate(zip(bits[:-1], wires)):
        mine = own_bit(axis, bit)
        if index > 0:
            away, part = half(part, 1 - mine), half(part, mine)
        arrived = yield from sent_over(line, away.astype(wire), axis, bit)
        part = part + arrived.astype(F32)
    sent = part.astype(wires[-1])
    arrived = yield from sent_over(line, sent, axis, bits[-1])
    return (sent.astype(F32) if alike else part) + arrived.astype(F32)


def joined(axis, bit, own, other):
    mine = own_bit(axis, bit)
    low = jnp.where(mine == 0, own, other)
    high = jnp.where(mine == 0, other, own)
    return jnp.concatenate((low, high), 0)


def gather_steps(line, piece, axis, bits):
    for bit in reversed(bits[1:-1]):
        other = yield from sent_over(line, piece, axis, bit)
        piece = joined(axis, bit, piece, other)
    return piece


def split_pair(part, axis, bits):
    mine = own_bit(axis, bits[0])
    return half(part, 1 - mine), half(part, mine)


def summed(line, pair, axis, bits, wires, between, pieces, alike=False):
    def steps():
        total = yield from reduce_steps(line, pair, axis, bits, wires, alike)
        own = yield from gather_steps(line, between(total), axis, bits)
        pieces.append(own)
        other = yield from sent_over(line, own, axis, bits[0])
        pieces.append(other)

    return Chain(steps())


def first_of(chain, pieces):
    while not pieces:
        chain.step()
    return pieces[0]


def over_voc(line, part, bits, wires, between, alike=False):
    pieces = []
    chain = summed(line, split_pair(part, "voc", bits), "voc", bits, wires, between, pieces, alike)
    return chain, lambda: (chain.result(), joined("voc", bits[0], *pieces))[1]


def on_device(hidden_states, target_logits, labels, down_weight, up_weight, head_weight):
    row_count, slice_cols = target_logits.shape
    book_count = labels.shape[1]
    group_count = lax.axis_size("grp")
    per_book = lax.axis_size("voc") // book_count
    block_rows = row_count // per_book
    position = lax.axis_index("voc")
    book_index = position // per_book
    book_part = position % per_book
    width = slice_cols // CHUNKS
    chunks = range(CHUNKS)
    z_bits = list(range(group_count.bit_length() - 1))
    v_bits = list(range(lax.axis_size("voc").bit_length() - 1))
    v_other = v_bits[:1] + v_bits[:0:-1]
    line = Line()

    def columns(c):
        return head_weight[:, c * width : (c + 1) * width]

    mine = own_bit("grp", z_bits[0])
    up_away, up_kept = half(up_weight, 1 - mine), half(up_weight, mine)
    vocab_pieces = [[] for c in chunks]
    vocab, sent = [], []
    for c in chunks:
        away, kept = [
            jnp.dot(part, columns(c), preferred_element_type=F32) * VOCAB_SCALE
            for part in (up_away, up_kept)
        ]
        sent.append(away.astype(F16))
        vocab.append(
            summed(
                line, (sent[c], kept), "grp", z_bits, [F16] * len(z_bits),
                lambda total: (total * (1.0 / VOCAB_SCALE)).astype(BF16), vocab_pieces[c],
            )
        )
    vocab[0].step()
    devices = range(group_count)
    top_rows = line.put(line.after(target_logits[:8]))
    incoming = lax.ppermute(top_rows, "grp", [(i + 1, i) for i in devices if i + 1 in devices])
    vocab[1].step()
    pre_part = line.put(
        jnp.dot(line.after(hidden_states), down_weight, preferred_element_type=F32)
    )
    kept_pre = []

    def activate(total):
        kept_pre.append(total * (1.0 / PRE_SCALE))
        return jax.nn.silu(kept_pre[0]).astype(BF16)

    pre, all_acts = over_voc(
        line, pre_part * PRE_SCALE, v_bits, [F16] * len(v_bits), activate
    )
    pre.step()
    incoming = line.put(line.after(incoming))
    vocab[0].step()
    pre.step()
    vocab[1].step()
    pre.step()
    if per_book == 1:
        prob, entropy = target_pass(line.after(target_logits), incoming)
    else:
        top, total = target_sums(target_logits, incoming)
        top, total = over_books((top, total), merge_sums, per_book)
        prob, entropy = target_probs(target_logits, incoming, top, total)
    line.put(entropy)
    label = lax.dynamic_slice_in_dim(labels, book_index, 1, 1) - book_part * slice_cols
    vocab[0].step()
    pre.step()
    vocab[1].step()
    pre.step()
    vocab[0].result()
    line.put(vocab_pieces[0][1])
    acts = line.put(all_acts())

    drafts, vocab_proj, sums = [], [], None
    for c in chunks:
        vocab[c].result()
        pieces = vocab_pieces[c]
        line.put(pieces[1])
        draft, proj, sums = draft_chunk(target_logits, acts, pieces, c, sums)
        drafts.append(line.put(draft))
        vocab_proj.append(proj)
    sums = over_books(tuple(sums), merge_sums, per_book)

    grads, carried, grad_pieces = [], None, [[] for c in chunks]
    for c in chunks:
        pair, carried = grad_chunk(
            line.after(drafts[c]), prob, label, acts, vocab_proj[c], c, sums, carried
        )
        line.put(pair)
        grads.append(
            summed(
                line, pair, "grp", z_bits, [BF16] * len(z_bits),
                lambda total: total.astype(BF16), grad_pieces[c],
            )
        )
        grads[c].step()
    act_part, loss = carried
    act, all_pre_grad = over_voc(
        line, act_part, v_bits, [F32] + [BF16] * len(v_bits),
        lambda total: (total * silu_slope(kept_pre[0])).astype(BF16),
    )
    grads[0].step()
    act.step()
    act.step()
    grads[1].step()
    act.step()
    def times_head(before, piece, c):
        return line.put(before + inner_cols(line.after(piece), columns(c)))

    own_up = times_head(0.0, first_of(grads[0], grad_pieces[0]), 0)
    act.step()
    own = first_of(grads[1], grad_pieces[1])
    act.step()
    grads[0].result()
    other_up = times_head(0.0, grad_pieces[0][1], 0)
    pre_grad = line.put(all_pre_grad())
    down_part = line.put(inner_rows(line.after(hidden_states), pre_grad))
    rows = down_part.shape[0] // 2
    down_pieces = [[], []]
    downs = [
        summed(
            line, split_pair(part, "grp", z_bits), "grp", z_bits, [BF16] * len(z_bits),
            lambda total: total.astype(BF16), down_pieces[i], True,
        )
        for i, part in enumerate((down_part[:rows], down_part[rows:]))
    ]
    downs[0].step()
    downs[1].step()
    own_up = times_head(own_up, own, 1)
    grads[1].result()
    other_up = times_head(other_up, grad_pieces[1][1], 1)
    up_part = joined("grp", z_bits[0], own_up, other_up)
    rank = up_part.shape[0] // 2
    ups = [
        over_voc(
            line, part, bits, [F32] + [BF16] * len(v_bits), lambda total: total.astype(BF16), True
        )
        for part, bits in ((up_part[:rank], v_bits), (up_part[rank:], v_other))
    ]
    swaps = [chain for chain, _ in ups]
    loss = over_books(line.after(loss) + entropy, jnp.add, per_book)
    frame_loss = lax.dynamic_slice_in_dim(loss, book_part * block_rows, block_rows, 0)
    frame_loss = frame_loss.reshape(1, 1, block_rows)
    for turn in (swaps, downs, swaps, swaps, swaps, downs, swaps):
        for chain in turn:
            chain.step()
    grad_b = jnp.concatenate([result().astype(F32) for _, result in ups], 0)
    for chain in downs:
        chain.result()
    grad_a = jnp.concatenate(
        [joined("grp", z_bits[0], *pieces).astype(F32) for pieces in down_pieces], 0
    )
    return frame_loss, grad_a, grad_b


def solution(mesh):
    in_specs = (
        P("grp", "voc"),
        P("grp", "voc"),
        P("grp", None),
        P("voc", None),
        P(None, "grp"),
        P("grp", "voc"),
    )
    out_specs = (P("voc", "grp", None), P("voc", None), P(None, "grp"))
    return jax.shard_map(
        on_device, mesh=mesh, in_specs=in_specs, out_specs=out_specs, check_vma=False
    )
```

```python
import jax
import jax.numpy as jnp
from jax import lax
from jax.experimental import pallas as pl
from jax.experimental.pallas import tpu as pltpu
from jax.sharding import PartitionSpec as P

HEAD = 2
LAM = 0.1
CHUNKS = 2
BLOCK = 256
VOCAB_SCALE = 128.0
PRE_SCALE = 64.0
F32 = jnp.float32
BF16 = jnp.bfloat16
F16 = jnp.float16


def swap(value, axis, bit):
    mask = 1 << bit
    pairs = [(i, i ^ mask) for i in range(lax.axis_size(axis))]
    return lax.ppermute(value, axis, pairs)


def own_bit(axis, bit):
    return (lax.axis_index(axis) >> bit) & 1


def half(value, which):
    rows = value.shape[0] // 2
    return lax.dynamic_slice_in_dim(value, which * rows, rows, 0)


def silu_slope(values):
    sigma = jax.nn.sigmoid(values)
    return sigma * (1.0 + values * (1.0 - sigma))


def inner_rows(left, right):
    return lax.dot_general(left, right, (((0,), (0,)), ((), ())), preferred_element_type=F32)


def inner_cols(left, right):
    return lax.dot_general(left, right, (((1,), (1,)), ((), ())), preferred_element_type=F32)


def over_books(values, combine, per_book):
    bit = 0
    while (1 << bit) < per_book:
        values = combine(values, jax.tree.map(lambda v: swap(v, "voc", bit), values))
        bit += 1
    return values


def merge_sums(a, b):
    top = jnp.maximum(a[0], b[0])
    return top, a[1] * jnp.exp(a[0] - top) + b[1] * jnp.exp(b[0] - top)


def params(megabytes):
    return pltpu.CompilerParams(
        dimension_semantics=("arbitrary",), vmem_limit_bytes=megabytes << 20
    )


def cost(flops, read, exps):
    return pl.CostEstimate(flops=flops // 4096, bytes_accessed=read // 4096, transcendentals=0)


def row_spec(block, cols, column=0):
    return pl.BlockSpec((block, cols), lambda i: (i, column))


def whole_spec(rows, cols):
    return pl.BlockSpec((rows, cols), lambda i: (0, 0))


def shift_in(target_ref, next_ref, incoming_ref, window):
    block = target_ref.shape[0]
    last = pl.program_id(0) == pl.num_programs(0) - 1
    window[:block, :] = target_ref[...]
    window[block:, :] = jnp.where(last, incoming_ref[...], next_ref[...])
    return window[HEAD : HEAD + block, :]


def target_sums(target, incoming):
    rows, cols = target.shape
    block = min(BLOCK, rows)

    def body(target_ref, next_ref, incoming_ref, top_ref, sum_ref, window):
        shifted = shift_in(target_ref, next_ref, incoming_ref, window)
        top = jnp.max(shifted, -1, keepdims=True)
        top_ref[...] = top
        sum_ref[...] = jnp.sum(jnp.exp(shifted - top), -1, keepdims=True)

    per = block // 8
    return pl.pallas_call(
        body,
        grid=(rows // block,),
        in_specs=[
            row_spec(block, cols),
            pl.BlockSpec((8, cols), lambda i: (jnp.minimum((i + 1) * per, rows // 8 - 1), 0)),
            whole_spec(8, cols),
        ],
        out_specs=[row_spec(block, 1)] * 2,
        out_shape=[jax.ShapeDtypeStruct((rows, 1), F32)] * 2,
        scratch_shapes=[pltpu.VMEM((block + 8, cols), F32)],
        compiler_params=params(24),
        cost_estimate=cost(4 * rows * cols, 4 * rows * cols, rows * cols),
        name="target_sums",
    )(target, target, incoming)


def target_pass(target, incoming):
    rows, cols = target.shape
    block = min(BLOCK, rows)

    def body(target_ref, next_ref, incoming_ref, prob_ref, entropy_ref, window):
        shifted = shift_in(target_ref, next_ref, incoming_ref, window)
        first = lax.axis_index("grp") * rows + pl.program_id(0) * block
        count = lax.axis_size("grp") * rows
        row = first + lax.broadcasted_iota(jnp.int32, (block, 1), 0)
        live = jnp.where(row < count - HEAD, 1.0, 0.0)
        below = shifted - jnp.max(shifted, -1, keepdims=True)
        raised = jnp.exp(below)
        total = jnp.sum(raised, -1, keepdims=True)
        scale = live / total
        prob_ref[...] = raised * scale
        entropy_ref[...] = scale * jnp.sum(raised * below, -1, keepdims=True) - live * jnp.log(total)

    per = block // 8
    return pl.pallas_call(
        body,
        grid=(rows // block,),
        in_specs=[
            row_spec(block, cols),
            pl.BlockSpec((8, cols), lambda i: (jnp.minimum((i + 1) * per, rows // 8 - 1), 0)),
            whole_spec(8, cols),
        ],
        out_specs=[row_spec(block, cols), row_spec(block, 1)],
        out_shape=[
            jax.ShapeDtypeStruct((rows, cols), F32),
            jax.ShapeDtypeStruct((rows, 1), F32),
        ],
        scratch_shapes=[pltpu.VMEM((block + 8, cols), F32)],
        compiler_params=params(24),
        cost_estimate=cost(6 * rows * cols, 8 * rows * cols, rows * cols),
        name="target_pass",
    )(target, target, incoming)


def target_probs(target, incoming, top, total):
    rows, cols = target.shape
    block = min(BLOCK, rows)

    def body(target_ref, next_ref, incoming_ref, top_ref, sum_ref, prob_ref, entropy_ref, window):
        shifted = shift_in(target_ref, next_ref, incoming_ref, window)
        first = lax.axis_index("grp") * rows + pl.program_id(0) * block
        count = lax.axis_size("grp") * rows
        row = first + lax.broadcasted_iota(jnp.int32, (block, 1), 0)
        live = jnp.where(row < count - HEAD, 1.0, 0.0)
        log_target = shifted - (top_ref[...] + jnp.log(sum_ref[...]))
        prob = jnp.exp(log_target) * live
        prob_ref[...] = prob
        entropy_ref[...] = jnp.sum(prob * log_target, -1, keepdims=True)

    per = block // 8
    return pl.pallas_call(
        body,
        grid=(rows // block,),
        in_specs=[
            row_spec(block, cols),
            pl.BlockSpec((8, cols), lambda i: (jnp.minimum((i + 1) * per, rows // 8 - 1), 0)),
            whole_spec(8, cols),
            row_spec(block, 1),
            row_spec(block, 1),
        ],
        out_specs=[row_spec(block, cols), row_spec(block, 1)],
        out_shape=[
            jax.ShapeDtypeStruct((rows, cols), F32),
            jax.ShapeDtypeStruct((rows, 1), F32),
        ],
        scratch_shapes=[pltpu.VMEM((block + 8, cols), F32)],
        compiler_params=params(24),
        cost_estimate=cost(6 * rows * cols, 8 * rows * cols, rows * cols),
        name="target_probs",
    )(target, target, incoming, top, total)


def draft_chunk(target, acts, pieces, column, sums):
    rows, rank = acts.shape
    half_rank, width = pieces[0].shape
    block = min(BLOCK, rows)

    def body(target_ref, acts_ref, own_ref, other_ref, *rest):
        draft_ref, proj_ref, top_ref, sum_ref = rest[-4:]

        @pl.when(pl.program_id(0) == 0)
        def _():
            mine = lax.axis_index("grp") & 1
            proj_ref[pl.ds(pl.multiple_of(mine * half_rank, half_rank), half_rank), :] = own_ref[...]
            proj_ref[
                pl.ds(pl.multiple_of((1 - mine) * half_rank, half_rank), half_rank), :
            ] = other_ref[...]

        draft = target_ref[...] + jnp.dot(
            acts_ref[...], proj_ref[...], preferred_element_type=F32
        )
        draft_ref[...] = draft
        top = jnp.max(draft, -1, keepdims=True)
        if sums is not None:
            top = jnp.maximum(top, rest[0][...])
        total = jnp.sum(jnp.exp(draft - top), -1, keepdims=True)
        if sums is not None:
            total = total + rest[1][...] * jnp.exp(rest[0][...] - top)
        top_ref[...] = top
        sum_ref[...] = total

    carried = () if sums is None else tuple(sums)
    draft, proj, top, total = pl.pallas_call(
        body,
        grid=(rows // block,),
        in_specs=[
            row_spec(block, width, column),
            row_spec(block, rank),
            whole_spec(half_rank, width),
            whole_spec(half_rank, width),
        ]
        + [row_spec(block, 1)] * len(carried),
        out_specs=[
            row_spec(block, width),
            whole_spec(rank, width),
            row_spec(block, 1),
            row_spec(block, 1),
        ],
        out_shape=[
            jax.ShapeDtypeStruct((rows, width), F32),
            jax.ShapeDtypeStruct((rank, width), BF16),
            jax.ShapeDtypeStruct((rows, 1), F32),
            jax.ShapeDtypeStruct((rows, 1), F32),
        ],
        compiler_params=params(16),
        cost_estimate=cost(2 * rows * rank * width, 8 * rows * width, rows * width),
        name="draft_chunk",
    )(target, acts, *pieces, *carried)
    return draft, proj, (top, total)


def grad_chunk(draft, prob, label, acts, vocab_proj, column, sums, carried):
    rows, width = draft.shape
    rank = acts.shape[1]
    half_rank = rank // 2
    block = min(BLOCK, rows)

    def body(draft_ref, prob_ref, label_ref, acts_ref, proj_ref, top_ref, sum_ref, *rest):
        away_ref, kept_ref, act_ref, loss_ref, totals = rest[-5:]
        step = pl.program_id(0)
        first = lax.axis_index("grp") * rows + step * block
        count = lax.axis_size("grp") * rows
        row = first + lax.broadcasted_iota(jnp.int32, (block, 1), 0)
        live = jnp.where(row < count - HEAD, 1.0, 0.0)
        log_draft = draft_ref[...] - (top_ref[...] + jnp.log(sum_ref[...]))
        prob = prob_ref[...]
        place = lax.broadcasted_iota(jnp.int32, (block, width), 1) + column * width
        hit = jnp.where(place == label_ref[...], LAM, 0.0)
        loss = -jnp.sum((prob + hit) * log_draft, -1, keepdims=True)
        grad = ((live + LAM) * jnp.exp(log_draft) - prob - hit).astype(BF16)
        act = inner_cols(grad, proj_ref[...])
        if carried is not None:
            loss = loss + rest[1][...]
            act = act + rest[0][...]
        loss_ref[...] = loss
        act_ref[...] = act
        term = inner_rows(acts_ref[...], grad)

        @pl.when(step == 0)
        def _():
            totals[...] = term

        @pl.when(step > 0)
        def _():
            totals[...] += term

        @pl.when(step == pl.num_programs(0) - 1)
        def _():
            mine = lax.axis_index("grp") & 1
            away = totals[pl.ds(pl.multiple_of((1 - mine) * half_rank, half_rank), half_rank), :]
            away_ref[...] = away.astype(BF16)
            kept_ref[...] = totals[pl.ds(pl.multiple_of(mine * half_rank, half_rank), half_rank), :]

    extra = () if carried is None else tuple(carried)
    away, kept, act, loss = pl.pallas_call(
        body,
        grid=(rows // block,),
        in_specs=[
            row_spec(block, width),
            row_spec(block, width, column),
            row_spec(block, 1),
            row_spec(block, rank),
            whole_spec(rank, width),
            row_spec(block, 1),
            row_spec(block, 1),
        ]
        + ([row_spec(block, rank), row_spec(block, 1)] if extra else []),
        out_specs=[whole_spec(half_rank, width)] * 2 + [row_spec(block, rank), row_spec(block, 1)],
        out_shape=[
            jax.ShapeDtypeStruct((half_rank, width), BF16),
            jax.ShapeDtypeStruct((half_rank, width), F32),
            jax.ShapeDtypeStruct((rows, rank), F32),
            jax.ShapeDtypeStruct((rows, 1), F32),
        ],
        scratch_shapes=[pltpu.VMEM((rank, width), F32)],
        compiler_params=params(16),
        cost_estimate=cost(4 * rows * rank * width, 8 * rows * width, rows * width),
        name="grad_chunk",
    )(draft, prob, label, acts, vocab_proj, *sums, *extra)
    return (away, kept), (act, loss)


class Line:
    def __init__(self):
        self.mark = None

    def after(self, value):
        if self.mark is None:
            return value
        return lax.optimization_barrier((value, self.mark))[0]

    def put(self, value):
        self.mark = jax.tree.leaves(value)[0]
        return value


class Chain:
    def __init__(self, steps):
        self.steps = steps
        self.value = None

    def step(self, times=1):
        for _ in range(times):
            if self.steps is not None:
                try:
                    next(self.steps)
                except StopIteration as end:
                    self.value = end.value
                    self.steps = None

    def result(self):
        while self.steps is not None:
            self.step()
        return self.value


def sent_over(line, value, axis, bit):
    value = line.put(line.after(value))
    arrived = swap(value, axis, bit)
    yield
    return line.after(arrived)


def reduce_steps(line, pair, axis, bits, wires, alike):
    away, part = pair
    for index, (bit, wire) in enumerate(zip(bits[:-1], wires)):
        mine = own_bit(axis, bit)
        if index > 0:
            away, part = half(part, 1 - mine), half(part, mine)
        arrived = yield from sent_over(line, away.astype(wire), axis, bit)
        part = part + arrived.astype(F32)
    sent = part.astype(wires[-1])
    arrived = yield from sent_over(line, sent, axis, bits[-1])
    return (sent.astype(F32) if alike else part) + arrived.astype(F32)


def joined(axis, bit, own, other):
    mine = own_bit(axis, bit)
    low = jnp.where(mine == 0, own, other)
    high = jnp.where(mine == 0, other, own)
    return jnp.concatenate((low, high), 0)


def gather_steps(line, piece, axis, bits):
    for bit in reversed(bits[1:-1]):
        other = yield from sent_over(line, piece, axis, bit)
        piece = joined(axis, bit, piece, other)
    return piece


def split_pair(part, axis, bits):
    mine = own_bit(axis, bits[0])
    return half(part, 1 - mine), half(part, mine)


def summed(line, pair, axis, bits, wires, between, pieces, alike=False):
    def steps():
        total = yield from reduce_steps(line, pair, axis, bits, wires, alike)
        own = yield from gather_steps(line, between(total), axis, bits)
        pieces.append(own)
        other = yield from sent_over(line, own, axis, bits[0])
        pieces.append(other)

    return Chain(steps())


def first_of(chain, pieces):
    while not pieces:
        chain.step()
    return pieces[0]


def over_voc(line, part, bits, wires, between, alike=False):
    pieces = []
    chain = summed(line, split_pair(part, "voc", bits), "voc", bits, wires, between, pieces, alike)
    return chain, lambda: (chain.result(), joined("voc", bits[0], *pieces))[1]


def on_device(hidden_states, target_logits, labels, down_weight, up_weight, head_weight):
    row_count, slice_cols = target_logits.shape
    book_count = labels.shape[1]
    group_count = lax.axis_size("grp")
    per_book = lax.axis_size("voc") // book_count
    block_rows = row_count // per_book
    position = lax.axis_index("voc")
    book_index = position // per_book
    book_part = position % per_book
    width = slice_cols // CHUNKS
    chunks = range(CHUNKS)
    z_bits = list(range(group_count.bit_length() - 1))
    v_bits = list(range(lax.axis_size("voc").bit_length() - 1))
    v_other = v_bits[:1] + v_bits[:0:-1]
    line = Line()

    def columns(c):
        return head_weight[:, c * width : (c + 1) * width]

    mine = own_bit("grp", z_bits[0])
    up_away, up_kept = half(up_weight, 1 - mine), half(up_weight, mine)
    vocab_pieces = [[] for c in chunks]
    vocab, sent = [], []
    for c in chunks:
        away, kept = [
            jnp.dot(part, columns(c), preferred_element_type=F32) * VOCAB_SCALE
            for part in (up_away, up_kept)
        ]
        sent.append(away.astype(F16))
        vocab.append(
            summed(
                line, (sent[c], kept), "grp", z_bits, [F16] * len(z_bits),
                lambda total: (total * (1.0 / VOCAB_SCALE)).astype(BF16), vocab_pieces[c],
            )
        )
    vocab[0].step()
    devices = range(group_count)
    top_rows = line.put(line.after(target_logits[:8]))
    incoming = lax.ppermute(top_rows, "grp", [(i + 1, i) for i in devices if i + 1 in devices])
    vocab[1].step()
    pre_part = line.put(
        jnp.dot(line.after(hidden_states), down_weight, preferred_element_type=F32)
    )
    kept_pre = []

    def activate(total):
        kept_pre.append(total * (1.0 / PRE_SCALE))
        return jax.nn.silu(kept_pre[0]).astype(BF16)

    pre, all_acts = over_voc(
        line, pre_part * PRE_SCALE, v_bits, [F16] * len(v_bits), activate
    )
    pre.step()
    incoming = line.put(line.after(incoming))
    vocab[0].step()
    pre.step()
    vocab[1].step()
    pre.step()
    if per_book == 1:
        prob, entropy = target_pass(line.after(target_logits), incoming)
    else:
        top, total = target_sums(target_logits, incoming)
        top, total = over_books((top, total), merge_sums, per_book)
        prob, entropy = target_probs(target_logits, incoming, top, total)
    line.put(entropy)
    label = lax.dynamic_slice_in_dim(labels, book_index, 1, 1) - book_part * slice_cols
    vocab[0].step()
    pre.step()
    vocab[1].step()
    pre.step()
    vocab[0].result()
    line.put(vocab_pieces[0][1])
    acts = line.put(all_acts())

    drafts, vocab_proj, sums = [], [], None
    for c in chunks:
        vocab[c].result()
        pieces = vocab_pieces[c]
        line.put(pieces[1])
        draft, proj, sums = draft_chunk(target_logits, acts, pieces, c, sums)
        drafts.append(line.put(draft))
        vocab_proj.append(proj)
    sums = over_books(tuple(sums), merge_sums, per_book)

    grads, carried, grad_pieces = [], None, [[] for c in chunks]
    for c in chunks:
        pair, carried = grad_chunk(
            line.after(drafts[c]), prob, label, acts, vocab_proj[c], c, sums, carried
        )
        line.put(pair)
        grads.append(
            summed(
                line, pair, "grp", z_bits, [BF16] * len(z_bits),
                lambda total: total.astype(BF16), grad_pieces[c],
            )
        )
        grads[c].step()
    act_part, loss = carried
    act, all_pre_grad = over_voc(
        line, act_part, v_bits, [F32] + [BF16] * len(v_bits),
        lambda total: (total * silu_slope(kept_pre[0])).astype(BF16),
    )
    grads[0].step()
    act.step()
    act.step()
    grads[1].step()
    act.step()
    def times_head(before, piece, c):
        return line.put(before + inner_cols(line.after(piece), columns(c)))

    own_up = times_head(0.0, first_of(grads[0], grad_pieces[0]), 0)
    act.step()
    own = first_of(grads[1], grad_pieces[1])
    act.step()
    grads[0].result()
    other_up = times_head(0.0, grad_pieces[0][1], 0)
    pre_grad = line.put(all_pre_grad())
    down_part = line.put(inner_rows(line.after(hidden_states), pre_grad))
    rows = down_part.shape[0] // 2
    down_pieces = [[], []]
    downs = [
        summed(
            line, split_pair(part, "grp", z_bits), "grp", z_bits, [BF16] * len(z_bits),
            lambda total: total.astype(BF16), down_pieces[i], True,
        )
        for i, part in enumerate((down_part[:rows], down_part[rows:]))
    ]
    downs[0].step()
    downs[1].step()
    own_up = times_head(own_up, own, 1)
    grads[1].result()
    other_up = times_head(other_up, grad_pieces[1][1], 1)
    up_part = joined("grp", z_bits[0], own_up, other_up)
    def core_steps():
        away, kept = split_pair(up_part, "voc", v_bits)
        arrived = yield from sent_over(line, away, "voc", v_bits[0])
        return kept + arrived

    core = Chain(core_steps())
    downs[0].step()
    core.step()
    loss = over_books(line.after(loss) + entropy, jnp.add, per_book)
    frame_loss = lax.dynamic_slice_in_dim(loss, book_part * block_rows, block_rows, 0)
    frame_loss = frame_loss.reshape(1, 1, block_rows)
    downs[1].step()
    part = core.result()
    rank = part.shape[0] // 2
    routes = (v_bits[1:], v_bits[:0:-1])
    up_pieces = [[] for _ in routes]
    ups = [
        summed(
            line, split_pair(piece, "voc", bits), "voc", bits, [BF16] * len(bits),
            lambda total: total.astype(BF16), pieces, True,
        )
        for piece, bits, pieces in zip((part[:rank], part[rank:]), routes, up_pieces)
    ]
    for turn in (ups, ups, ups, downs):
        for chain in turn:
            chain.step()
    for chain in ups:
        chain.result()
    whole = jnp.concatenate(
        [joined("voc", bits[0], *pieces) for bits, pieces in zip(routes, up_pieces)], 0
    )

    def last_steps():
        other = yield from sent_over(line, whole, "voc", v_bits[0])
        return joined("voc", v_bits[0], whole, other)

    grad_b = Chain(last_steps()).result().astype(F32)
    for chain in downs:
        chain.result()
    grad_a = jnp.concatenate(
        [joined("grp", z_bits[0], *pieces).astype(F32) for pieces in down_pieces], 0
    )
    return frame_loss, grad_a, grad_b


def solution(mesh):
    in_specs = (
        P("grp", "voc"),
        P("grp", "voc"),
        P("grp", None),
        P("voc", None),
        P(None, "grp"),
        P("grp", "voc"),
    )
    out_specs = (P("voc", "grp", None), P("voc", None), P(None, "grp"))
    return jax.shard_map(
        on_device, mesh=mesh, in_specs=in_specs, out_specs=out_specs, check_vma=False
    )
```

```python
import jax
import jax.numpy as jnp
from jax import lax
from jax.experimental import pallas as pl
from jax.experimental.pallas import tpu as pltpu
from jax.sharding import PartitionSpec as P

HEAD = 2
LAM = 0.1
CHUNKS = 2
BLOCK = 256
VOCAB_SCALE = 128.0
PRE_SCALE = 32.0
F32 = jnp.float32
BF16 = jnp.bfloat16
F16 = jnp.float16


def swap(value, axis, bit):
    mask = 1 << bit
    pairs = [(i, i ^ mask) for i in range(lax.axis_size(axis))]
    return lax.ppermute(value, axis, pairs)


def own_bit(axis, bit):
    return (lax.axis_index(axis) >> bit) & 1


def half(value, which):
    rows = value.shape[0] // 2
    return lax.dynamic_slice_in_dim(value, which * rows, rows, 0)


def silu_slope(values):
    sigma = jax.nn.sigmoid(values)
    return sigma * (1.0 + values * (1.0 - sigma))


def inner_rows(left, right):
    return lax.dot_general(left, right, (((0,), (0,)), ((), ())), preferred_element_type=F32)


def inner_cols(left, right):
    return lax.dot_general(left, right, (((1,), (1,)), ((), ())), preferred_element_type=F32)


def over_books(values, combine, per_book):
    bit = 0
    while (1 << bit) < per_book:
        values = combine(values, jax.tree.map(lambda v: swap(v, "voc", bit), values))
        bit += 1
    return values


def merge_sums(a, b):
    top = jnp.maximum(a[0], b[0])
    return top, a[1] * jnp.exp(a[0] - top) + b[1] * jnp.exp(b[0] - top)


def params(megabytes):
    return pltpu.CompilerParams(
        dimension_semantics=("arbitrary",), vmem_limit_bytes=megabytes << 20
    )


def cost(flops, read, exps):
    return pl.CostEstimate(flops=flops // 4096, bytes_accessed=read // 4096, transcendentals=0)


def row_spec(block, cols, column=0):
    return pl.BlockSpec((block, cols), lambda i: (i, column))


def whole_spec(rows, cols):
    return pl.BlockSpec((rows, cols), lambda i: (0, 0))


def shift_in(target_ref, next_ref, incoming_ref, window):
    block = target_ref.shape[0]
    last = pl.program_id(0) == pl.num_programs(0) - 1
    window[:block, :] = target_ref[...]
    window[block:, :] = jnp.where(last, incoming_ref[...], next_ref[...])
    return window[HEAD : HEAD + block, :]


def target_sums(target, incoming):
    rows, cols = target.shape
    block = min(BLOCK, rows)

    def body(target_ref, next_ref, incoming_ref, top_ref, sum_ref, window):
        shifted = shift_in(target_ref, next_ref, incoming_ref, window)
        top = jnp.max(shifted, -1, keepdims=True)
        top_ref[...] = top
        sum_ref[...] = jnp.sum(jnp.exp(shifted - top), -1, keepdims=True)

    per = block // 8
    return pl.pallas_call(
        body,
        grid=(rows // block,),
        in_specs=[
            row_spec(block, cols),
            pl.BlockSpec((8, cols), lambda i: (jnp.minimum((i + 1) * per, rows // 8 - 1), 0)),
            whole_spec(8, cols),
        ],
        out_specs=[row_spec(block, 1)] * 2,
        out_shape=[jax.ShapeDtypeStruct((rows, 1), F32)] * 2,
        scratch_shapes=[pltpu.VMEM((block + 8, cols), F32)],
        compiler_params=params(24),
        cost_estimate=cost(4 * rows * cols, 4 * rows * cols, rows * cols),
        name="target_sums",
    )(target, target, incoming)


def target_pass(target, incoming):
    rows, cols = target.shape
    block = min(BLOCK, rows)

    def body(target_ref, next_ref, incoming_ref, prob_ref, entropy_ref, window):
        shifted = shift_in(target_ref, next_ref, incoming_ref, window)
        first = lax.axis_index("grp") * rows + pl.program_id(0) * block
        count = lax.axis_size("grp") * rows
        row = first + lax.broadcasted_iota(jnp.int32, (block, 1), 0)
        live = jnp.where(row < count - HEAD, 1.0, 0.0)
        below = shifted - jnp.max(shifted, -1, keepdims=True)
        raised = jnp.exp(below)
        total = jnp.sum(raised, -1, keepdims=True)
        scale = live / total
        prob_ref[...] = raised * scale
        entropy_ref[...] = scale * jnp.sum(raised * below, -1, keepdims=True) - live * jnp.log(total)

    per = block // 8
    return pl.pallas_call(
        body,
        grid=(rows // block,),
        in_specs=[
            row_spec(block, cols),
            pl.BlockSpec((8, cols), lambda i: (jnp.minimum((i + 1) * per, rows // 8 - 1), 0)),
            whole_spec(8, cols),
        ],
        out_specs=[row_spec(block, cols), row_spec(block, 1)],
        out_shape=[
            jax.ShapeDtypeStruct((rows, cols), F32),
            jax.ShapeDtypeStruct((rows, 1), F32),
        ],
        scratch_shapes=[pltpu.VMEM((block + 8, cols), F32)],
        compiler_params=params(24),
        cost_estimate=cost(6 * rows * cols, 8 * rows * cols, rows * cols),
        name="target_pass",
    )(target, target, incoming)


def target_probs(target, incoming, top, total):
    rows, cols = target.shape
    block = min(BLOCK, rows)

    def body(target_ref, next_ref, incoming_ref, top_ref, sum_ref, prob_ref, entropy_ref, window):
        shifted = shift_in(target_ref, next_ref, incoming_ref, window)
        first = lax.axis_index("grp") * rows + pl.program_id(0) * block
        count = lax.axis_size("grp") * rows
        row = first + lax.broadcasted_iota(jnp.int32, (block, 1), 0)
        live = jnp.where(row < count - HEAD, 1.0, 0.0)
        log_target = shifted - (top_ref[...] + jnp.log(sum_ref[...]))
        prob = jnp.exp(log_target) * live
        prob_ref[...] = prob
        entropy_ref[...] = jnp.sum(prob * log_target, -1, keepdims=True)

    per = block // 8
    return pl.pallas_call(
        body,
        grid=(rows // block,),
        in_specs=[
            row_spec(block, cols),
            pl.BlockSpec((8, cols), lambda i: (jnp.minimum((i + 1) * per, rows // 8 - 1), 0)),
            whole_spec(8, cols),
            row_spec(block, 1),
            row_spec(block, 1),
        ],
        out_specs=[row_spec(block, cols), row_spec(block, 1)],
        out_shape=[
            jax.ShapeDtypeStruct((rows, cols), F32),
            jax.ShapeDtypeStruct((rows, 1), F32),
        ],
        scratch_shapes=[pltpu.VMEM((block + 8, cols), F32)],
        compiler_params=params(24),
        cost_estimate=cost(6 * rows * cols, 8 * rows * cols, rows * cols),
        name="target_probs",
    )(target, target, incoming, top, total)


def draft_chunk(target, acts, pieces, column, sums):
    rows, rank = acts.shape
    half_rank, width = pieces[0].shape
    block = min(BLOCK, rows)

    def body(target_ref, acts_ref, own_ref, other_ref, *rest):
        draft_ref, proj_ref, top_ref, sum_ref = rest[-4:]

        @pl.when(pl.program_id(0) == 0)
        def _():
            mine = lax.axis_index("grp") & 1
            proj_ref[pl.ds(pl.multiple_of(mine * half_rank, half_rank), half_rank), :] = own_ref[...]
            proj_ref[
                pl.ds(pl.multiple_of((1 - mine) * half_rank, half_rank), half_rank), :
            ] = other_ref[...]

        draft = target_ref[...] + jnp.dot(
            acts_ref[...], proj_ref[...], preferred_element_type=F32
        )
        draft_ref[...] = draft
        top = jnp.max(draft, -1, keepdims=True)
        if sums is not None:
            top = jnp.maximum(top, rest[0][...])
        total = jnp.sum(jnp.exp(draft - top), -1, keepdims=True)
        if sums is not None:
            total = total + rest[1][...] * jnp.exp(rest[0][...] - top)
        top_ref[...] = top
        sum_ref[...] = total

    carried = () if sums is None else tuple(sums)
    draft, proj, top, total = pl.pallas_call(
        body,
        grid=(rows // block,),
        in_specs=[
            row_spec(block, width, column),
            row_spec(block, rank),
            whole_spec(half_rank, width),
            whole_spec(half_rank, width),
        ]
        + [row_spec(block, 1)] * len(carried),
        out_specs=[
            row_spec(block, width),
            whole_spec(rank, width),
            row_spec(block, 1),
            row_spec(block, 1),
        ],
        out_shape=[
            jax.ShapeDtypeStruct((rows, width), F32),
            jax.ShapeDtypeStruct((rank, width), BF16),
            jax.ShapeDtypeStruct((rows, 1), F32),
            jax.ShapeDtypeStruct((rows, 1), F32),
        ],
        compiler_params=params(16),
        cost_estimate=cost(2 * rows * rank * width, 8 * rows * width, rows * width),
        name="draft_chunk",
    )(target, acts, *pieces, *carried)
    return draft, proj, (top, total)


def grad_chunk(draft, prob, label, acts, vocab_proj, column, sums, carried):
    rows, width = draft.shape
    rank = acts.shape[1]
    half_rank = rank // 2
    block = min(BLOCK, rows)

    def body(draft_ref, prob_ref, label_ref, acts_ref, proj_ref, top_ref, sum_ref, *rest):
        away_ref, kept_ref, act_ref, loss_ref, totals = rest[-5:]
        step = pl.program_id(0)
        first = lax.axis_index("grp") * rows + step * block
        count = lax.axis_size("grp") * rows
        row = first + lax.broadcasted_iota(jnp.int32, (block, 1), 0)
        live = jnp.where(row < count - HEAD, 1.0, 0.0)
        log_draft = draft_ref[...] - (top_ref[...] + jnp.log(sum_ref[...]))
        prob = prob_ref[...]
        place = lax.broadcasted_iota(jnp.int32, (block, width), 1) + column * width
        hit = jnp.where(place == label_ref[...], LAM, 0.0)
        loss = -jnp.sum((prob + hit) * log_draft, -1, keepdims=True)
        grad = ((live + LAM) * jnp.exp(log_draft) - prob - hit).astype(BF16)
        act = inner_cols(grad, proj_ref[...])
        if carried is not None:
            loss = loss + rest[1][...]
            act = act + rest[0][...]
        loss_ref[...] = loss
        act_ref[...] = act
        term = inner_rows(acts_ref[...], grad)

        @pl.when(step == 0)
        def _():
            totals[...] = term

        @pl.when(step > 0)
        def _():
            totals[...] += term

        @pl.when(step == pl.num_programs(0) - 1)
        def _():
            mine = lax.axis_index("grp") & 1
            away = totals[pl.ds(pl.multiple_of((1 - mine) * half_rank, half_rank), half_rank), :]
            away_ref[...] = away.astype(BF16)
            kept_ref[...] = totals[pl.ds(pl.multiple_of(mine * half_rank, half_rank), half_rank), :]

    extra = () if carried is None else tuple(carried)
    away, kept, act, loss = pl.pallas_call(
        body,
        grid=(rows // block,),
        in_specs=[
            row_spec(block, width),
            row_spec(block, width, column),
            row_spec(block, 1),
            row_spec(block, rank),
            whole_spec(rank, width),
            row_spec(block, 1),
            row_spec(block, 1),
        ]
        + ([row_spec(block, rank), row_spec(block, 1)] if extra else []),
        out_specs=[whole_spec(half_rank, width)] * 2 + [row_spec(block, rank), row_spec(block, 1)],
        out_shape=[
            jax.ShapeDtypeStruct((half_rank, width), BF16),
            jax.ShapeDtypeStruct((half_rank, width), F32),
            jax.ShapeDtypeStruct((rows, rank), F32),
            jax.ShapeDtypeStruct((rows, 1), F32),
        ],
        scratch_shapes=[pltpu.VMEM((rank, width), F32)],
        compiler_params=params(16),
        cost_estimate=cost(4 * rows * rank * width, 8 * rows * width, rows * width),
        name="grad_chunk",
    )(draft, prob, label, acts, vocab_proj, *sums, *extra)
    return (away, kept), (act, loss)


class Line:
    def __init__(self):
        self.mark = None

    def after(self, value):
        if self.mark is None:
            return value
        return lax.optimization_barrier((value, self.mark))[0]

    def put(self, value):
        self.mark = jax.tree.leaves(value)[0]
        return value


class Chain:
    def __init__(self, steps):
        self.steps = steps
        self.value = None

    def step(self, times=1):
        for _ in range(times):
            if self.steps is not None:
                try:
                    next(self.steps)
                except StopIteration as end:
                    self.value = end.value
                    self.steps = None

    def result(self):
        while self.steps is not None:
            self.step()
        return self.value


def sent_over(line, value, axis, bit):
    value = line.put(line.after(value))
    arrived = swap(value, axis, bit)
    yield
    return line.after(arrived)


def reduce_steps(line, pair, axis, bits, wires, alike):
    away, part = pair
    for index, (bit, wire) in enumerate(zip(bits[:-1], wires)):
        mine = own_bit(axis, bit)
        if index > 0:
            away, part = half(part, 1 - mine), half(part, mine)
        arrived = yield from sent_over(line, away.astype(wire), axis, bit)
        part = part + arrived.astype(F32)
    sent = part.astype(wires[-1])
    arrived = yield from sent_over(line, sent, axis, bits[-1])
    return (sent.astype(F32) if alike else part) + arrived.astype(F32)


def joined(axis, bit, own, other):
    mine = own_bit(axis, bit)
    low = jnp.where(mine == 0, own, other)
    high = jnp.where(mine == 0, other, own)
    return jnp.concatenate((low, high), 0)


def gather_steps(line, piece, axis, bits):
    for bit in reversed(bits[1:-1]):
        other = yield from sent_over(line, piece, axis, bit)
        piece = joined(axis, bit, piece, other)
    return piece


def split_pair(part, axis, bits):
    mine = own_bit(axis, bits[0])
    return half(part, 1 - mine), half(part, mine)


def summed(line, pair, axis, bits, wires, between, pieces, alike=False):
    def steps():
        total = yield from reduce_steps(line, pair, axis, bits, wires, alike)
        own = yield from gather_steps(line, between(total), axis, bits)
        pieces.append(own)
        other = yield from sent_over(line, own, axis, bits[0])
        pieces.append(other)

    return Chain(steps())


def first_of(chain, pieces):
    while not pieces:
        chain.step()
    return pieces[0]


def over_voc(line, part, bits, wires, between, alike=False):
    pieces = []
    chain = summed(line, split_pair(part, "voc", bits), "voc", bits, wires, between, pieces, alike)
    return chain, lambda: (chain.result(), joined("voc", bits[0], *pieces))[1]


def on_device(hidden_states, target_logits, labels, down_weight, up_weight, head_weight):
    row_count, slice_cols = target_logits.shape
    book_count = labels.shape[1]
    group_count = lax.axis_size("grp")
    per_book = lax.axis_size("voc") // book_count
    block_rows = row_count // per_book
    position = lax.axis_index("voc")
    book_index = position // per_book
    book_part = position % per_book
    width = slice_cols // CHUNKS
    chunks = range(CHUNKS)
    z_bits = list(range(group_count.bit_length() - 1))
    v_bits = list(range(lax.axis_size("voc").bit_length() - 1))
    v_other = v_bits[:1] + v_bits[:0:-1]
    line = Line()

    def columns(c):
        return head_weight[:, c * width : (c + 1) * width]

    mine = own_bit("grp", z_bits[0])
    up_away, up_kept = half(up_weight, 1 - mine), half(up_weight, mine)
    vocab_pieces = [[] for c in chunks]
    vocab, sent = [], []
    for c in chunks:
        away, kept = [
            jnp.dot(part, columns(c), preferred_element_type=F32) * VOCAB_SCALE
            for part in (up_away, up_kept)
        ]
        sent.append(away.astype(F16))
        vocab.append(
            summed(
                line, (sent[c], kept), "grp", z_bits, [F16] * len(z_bits),
                lambda total: (total * (1.0 / VOCAB_SCALE)).astype(BF16), vocab_pieces[c],
            )
        )
    vocab[0].step()
    devices = range(group_count)
    top_rows = line.put(line.after(target_logits[:8]))
    incoming = lax.ppermute(top_rows, "grp", [(i + 1, i) for i in devices if i + 1 in devices])
    vocab[1].step()
    pre_part = line.put(
        jnp.dot(line.after(hidden_states), down_weight, preferred_element_type=F32)
    )
    kept_pre = []

    def activate(total):
        kept_pre.append(total * (1.0 / PRE_SCALE))
        return jax.nn.silu(kept_pre[0]).astype(BF16)

    pre, all_acts = over_voc(
        line, pre_part * PRE_SCALE, v_bits, [F16] * len(v_bits), activate
    )
    pre.step()
    incoming = line.put(line.after(incoming))
    vocab[0].step()
    pre.step()
    vocab[1].step()
    pre.step()
    if per_book == 1:
        prob, entropy = target_pass(line.after(target_logits), incoming)
    else:
        top, total = target_sums(target_logits, incoming)
        top, total = over_books((top, total), merge_sums, per_book)
        prob, entropy = target_probs(target_logits, incoming, top, total)
    line.put(entropy)
    label = lax.dynamic_slice_in_dim(labels, book_index, 1, 1) - book_part * slice_cols
    vocab[0].step()
    pre.step()
    vocab[1].step()
    pre.step()
    vocab[0].result()
    line.put(vocab_pieces[0][1])
    acts = line.put(all_acts())

    drafts, vocab_proj, sums = [], [], None
    for c in chunks:
        vocab[c].result()
        pieces = vocab_pieces[c]
        line.put(pieces[1])
        draft, proj, sums = draft_chunk(target_logits, acts, pieces, c, sums)
        drafts.append(line.put(draft))
        vocab_proj.append(proj)
    sums = over_books(tuple(sums), merge_sums, per_book)

    grads, carried, grad_pieces = [], None, [[] for c in chunks]
    for c in chunks:
        pair, carried = grad_chunk(
            line.after(drafts[c]), prob, label, acts, vocab_proj[c], c, sums, carried
        )
        line.put(pair)
        grads.append(
            summed(
                line, pair, "grp", z_bits, [BF16] * len(z_bits),
                lambda total: total.astype(BF16), grad_pieces[c],
            )
        )
        grads[c].step()
    act_part, loss = carried
    act, all_pre_grad = over_voc(
        line, act_part, v_bits, [F32] + [BF16] * len(v_bits),
        lambda total: (total * silu_slope(kept_pre[0])).astype(BF16),
    )
    grads[0].step()
    act.step()
    act.step()
    grads[1].step()
    act.step()
    def times_head(before, piece, c):
        return line.put(before + inner_cols(line.after(piece), columns(c)))

    own_up = times_head(0.0, first_of(grads[0], grad_pieces[0]), 0)
    act.step()
    own = first_of(grads[1], grad_pieces[1])
    act.step()
    grads[0].result()
    other_up = times_head(0.0, grad_pieces[0][1], 0)
    pre_grad = line.put(all_pre_grad())
    down_part = line.put(inner_rows(line.after(hidden_states), pre_grad))
    rows = down_part.shape[0] // 2
    down_pieces = [[], []]
    downs = [
        summed(
            line, split_pair(part, "grp", z_bits), "grp", z_bits, [BF16] * len(z_bits),
            lambda total: total.astype(BF16), down_pieces[i], True,
        )
        for i, part in enumerate((down_part[:rows], down_part[rows:]))
    ]
    downs[0].step()
    downs[1].step()
    own_up = times_head(own_up, own, 1)
    grads[1].result()
    other_up = times_head(other_up, grad_pieces[1][1], 1)
    up_part = joined("grp", z_bits[0], own_up, other_up)
    rank = up_part.shape[0] // 2
    ups = [
        over_voc(
            line, part, bits, [F32] + [BF16] * len(v_bits), lambda total: total.astype(BF16), True
        )
        for part, bits in ((up_part[:rank], v_bits), (up_part[rank:], v_other))
    ]
    swaps = [chain for chain, _ in ups]
    loss = over_books(line.after(loss) + entropy, jnp.add, per_book)
    frame_loss = lax.dynamic_slice_in_dim(loss, book_part * block_rows, block_rows, 0)
    frame_loss = frame_loss.reshape(1, 1, block_rows)
    for turn in (swaps, downs, swaps, swaps, swaps, downs, swaps):
        for chain in turn:
            chain.step()
    grad_b = jnp.concatenate([result().astype(F32) for _, result in ups], 0)
    for chain in downs:
        chain.result()
    grad_a = jnp.concatenate(
        [joined("grp", z_bits[0], *pieces).astype(F32) for pieces in down_pieces], 0
    )
    return frame_loss, grad_a, grad_b


def solution(mesh):
    in_specs = (
        P("grp", "voc"),
        P("grp", "voc"),
        P("grp", None),
        P("voc", None),
        P(None, "grp"),
        P("grp", "voc"),
    )
    out_specs = (P("voc", "grp", None), P("voc", None), P(None, "grp"))
    return jax.shard_map(
        on_device, mesh=mesh, in_specs=in_specs, out_specs=out_specs, check_vma=False
    )
```
